32 devices in a mesh: gx: 4 (over z), gy: 8 (over y, x, core).
Axes of the slice: x: 2, y: 2, z: 4, core: 2. Of those that a mesh axis runs over, the one named last changes fastest.
Arguments:
- flow_populations: float32 [19, 64, 64, 128], P(None, 'gx', 'gy'), may hold values from 0 to 1, as said below
- solute_populations: float32 [7, 64, 64, 128], P(None, 'gx', 'gy'), may hold values from 0 to 1, as said below
- voxel_kind: int32 [64, 64, 128], P('gx', 'gy'), may hold values from 0 to 3, as said below
Outputs:
- density: float32 [64, 64, 128], P('gx', 'gy')
- momentum: float32 [3, 64, 64, 128], P(None, 'gx', 'gy')
- concentration: float32 [64, 64, 128], P('gx', 'gy')
The draws below stay inside these ranges and needn't reach their ends.
Inputs may be any that keep to these rules, and one draw needn't show every extreme that they name: `flow_populations`: each flow population is its lattice weight w_i times a factor between 0.5 and 1.5. `solute_populations`: each solute population is its lattice weight v_k times a positive factor of at most 1.9. `voxel_kind`: the first z plane holds only inlet and solid voxels, the last z plane only outlet and solid voxels, every other plane only pore and solid voxels.
All inputs are finite; a program needn't handle non-finite values.
Results may differ from the reference program's by a relative error of at most 0.0001.
Values sent between devices are 32-bit elements; how exact they have to be, the bound alone decides.
No kernel may reach another device: no remote copies, remote signals or barrier semaphores. Data moves between devices by JAX's collectives and lax.ppermute only.
A program may use at most 64 MiB of HBM per device.

```python
import jax
import jax.numpy as jnp
from jax import lax

NZ = 128
STEPS = 3
NX = 64
NY = 64


def draw_flow_populations(key, part):
    weights = jnp.array([1.0 / 3.0] + [1.0 / 18.0] * 6 + [1.0 / 36.0] * 12, jnp.float32)
    factor = jax.random.uniform(key, (19, NX, NY, NZ), jnp.float32, 0.6, 1.4)
    return weights[:, None, None, None] * factor


def draw_solute_populations(key, part):
    weights = jnp.array([0.25] + [0.125] * 6, jnp.float32)
    level = jax.random.uniform(jax.random.fold_in(key, 1), (NX, NY, NZ), jnp.float32, 0.2, 1.2)
    factor = jax.random.uniform(jax.random.fold_in(key, 2), (7, NX, NY, NZ), jnp.float32, 0.7, 1.3)
    return weights[:, None, None, None] * level[None] * factor


def draw_voxel_kind(key, part):
    is_solid = jax.random.randint(key, (NX, NY, NZ), 0, 10) < 3
    depth = lax.broadcasted_iota(jnp.int32, (NX, NY, NZ), 2)
    border = jnp.where(depth == 0, 2, jnp.where(depth == NZ - 1, 3, 0))
    return jnp.where(is_solid, 1, border).astype(jnp.int32)


def setup_inputs(seed: int = 0) -> dict:
    streams_of = jax.random.split(jax.random.key(seed), 4)
    flow_populations = draw_flow_populations(jax.random.fold_in(streams_of[3], 71), 0)
    solute_populations = draw_solute_populations(jax.random.fold_in(streams_of[3], 71), 0)
    voxel_kind = draw_voxel_kind(jax.random.fold_in(streams_of[3], 71), 0)
    return {"flow_populations": flow_populations, "solute_populations": solute_populations, "voxel_kind": voxel_kind}


flow_velocity = [(0, 0, 0), (1, 0, 0), (-1, 0, 0), (0, 1, 0), (0, -1, 0), (0, 0, 1), (0, 0, -1),
                 (1, 1, 0), (-1, -1, 0), (1, -1, 0), (-1, 1, 0), (1, 0, 1), (-1, 0, -1),
                 (1, 0, -1), (-1, 0, 1), (0, 1, 1), (0, -1, -1), (0, 1, -1), (0, -1, 1)]
flow_weight = [1.0 / 3.0] + [1.0 / 18.0] * 6 + [1.0 / 36.0] * 12
solute_velocity = flow_velocity[:7]
solute_weight = [0.25] + [0.125] * 6
flow_plus = 1.25
flow_minus = 1.0 / 1.125
solute_plus = 1.0 / 1.75
solute_minus = 1.0 / 0.7
inlet_density = 1.05
outlet_density = 0.95
inlet_solute = 1.0


def opposite(component):
    if component == 0:
        return 0
    if component % 2 == 1:
        return component + 1
    return component - 1


def moments(flow):
    density = jnp.sum(flow, axis=0)
    components = []
    for axis_number in range(3):
        summed = jnp.zeros_like(density)
        for component, velocity in enumerate(flow_velocity):
            if velocity[axis_number] != 0:
                summed = summed + velocity[axis_number] * flow[component]
        components.append(summed)
    return density, components


def collide(flow, solute, voxel_kind):
    density, (mom_x, mom_y, mom_z) = moments(flow)
    concentration = jnp.sum(solute, axis=0)
    square = mom_x * mom_x + mom_y * mom_y + mom_z * mom_z
    is_fluid = voxel_kind == 0
    is_inlet = voxel_kind == 2
    is_outlet = voxel_kind == 3
    flow_out = []
    for component, velocity in enumerate(flow_velocity):
        weight = flow_weight[component]
        mirror = opposite(component)
        projection = velocity[0] * mom_x + velocity[1] * mom_y + velocity[2] * mom_z
        even_eq = weight * (density + 4.5 * projection * projection - 1.5 * square)
        odd_eq = weight * 3.0 * projection
        even_part = 0.5 * (flow[component] + flow[mirror])
        odd_part = 0.5 * (flow[component] - flow[mirror])
        relaxed = flow[component] - flow_plus * (even_part - even_eq) - flow_minus * (odd_part - odd_eq)
        result = jnp.where(is_fluid, relaxed, flow[mirror])
        result = jnp.where(is_inlet, weight * inlet_density, result)
        result = jnp.where(is_outlet, weight * outlet_density, result)
        flow_out.append(result)
    solute_out = []
    for component, velocity in enumerate(solute_velocity):
        weight = solute_weight[component]
        mirror = opposite(component)
        projection = velocity[0] * mom_x + velocity[1] * mom_y + velocity[2] * mom_z
        even_eq = weight * concentration
        odd_eq = weight * 4.0 * concentration * projection
        even_part = 0.5 * (solute[component] + solute[mirror])
        odd_part = 0.5 * (solute[component] - solute[mirror])
        relaxed = solute[component] - solute_plus * (even_part - even_eq) - solute_minus * (odd_part - odd_eq)
        result = jnp.where(is_fluid, relaxed, solute[mirror])
        result = jnp.where(is_inlet, weight * inlet_solute, result)
        result = jnp.where(is_outlet, jnp.zeros_like(result), result)
        solute_out.append(result)
    return jnp.stack(flow_out), jnp.stack(solute_out)


def depth_shift(section, along_z):
    if along_z == 1:
        return jnp.concatenate([jnp.zeros_like(section[:, :, :1]), section[:, :, :-1]], axis=2)
    if along_z == -1:
        return jnp.concatenate([section[:, :, 1:], jnp.zeros_like(section[:, :, :1])], axis=2)
    return section


def propagate(outgoing, velocities):
    planes = []
    for component, velocity in enumerate(velocities):
        section = jnp.roll(outgoing[component], (velocity[0], velocity[1]), axis=(0, 1))
        planes.append(depth_shift(section, velocity[2]))
    return jnp.stack(planes)


def reference(flow_populations, solute_populations, voxel_kind):
    flow = flow_populations
    solute = solute_populations
    for sweep in range(STEPS):
        flow_post, solute_post = collide(flow, solute, voxel_kind)
        flow = propagate(flow_post, flow_velocity)
        solute = propagate(solute_post, solute_velocity)
    density, components = moments(flow)
    return density, jnp.stack(components), jnp.sum(solute, axis=0)
```

```python
import functools
import math

import jax
import jax.numpy as jnp
from jax import lax
from jax.experimental import pallas as pl
from jax.experimental.pallas import tpu as pltpu
from jax.sharding import PartitionSpec as P

STEPS = 3
HALO = STEPS

flow_velocity = [
    (0, 0, 0),
    (1, 0, 0),
    (-1, 0, 0),
    (0, 1, 0),
    (0, -1, 0),
    (0, 0, 1),
    (0, 0, -1),
    (1, 1, 0),
    (-1, -1, 0),
    (1, -1, 0),
    (-1, 1, 0),
    (1, 0, 1),
    (-1, 0, -1),
    (1, 0, -1),
    (-1, 0, 1),
    (0, 1, 1),
    (0, -1, -1),
    (0, 1, -1),
    (0, -1, 1),
]
FLOW = len(flow_velocity)
all_velocity = flow_velocity + flow_velocity[:7]
COUNT = len(all_velocity)
KIND = COUNT
flow_plus = 1.25
flow_minus = 1.0 / 1.125
solute_plus = 1.0 / 1.75
solute_minus = 1.0 / 0.7
inlet_density = 1.05
outlet_density = 0.95
inlet_solute = 1.0


def mirrored(channel, sign_x, sign_y):
    if channel == KIND:
        return KIND
    cx, cy, cz = all_velocity[channel]
    wanted = (cx * sign_x, cy * sign_y, cz)
    if channel < FLOW:
        return flow_velocity.index(wanted)
    return FLOW + flow_velocity[:7].index(wanted)


face_x = [
    (c, d) for d in range(1, HALO + 1) for c in range(COUNT) if d - all_velocity[c][0] <= HALO - 1
] + [(KIND, d) for d in range(1, HALO)]
face_y = [
    (c, d) for d in range(1, HALO + 1) for c in range(COUNT) if d - all_velocity[c][1] <= HALO - 1
] + [(KIND, d) for d in range(1, HALO)]
corner = [
    (c, dx, dy)
    for dx in range(1, HALO + 1)
    for dy in range(1, HALO + 1)
    for c in range(COUNT)
    if dx - all_velocity[c][0] <= HALO - 1 and dy - all_velocity[c][1] <= HALO - 1
] + [(KIND, dx, dy) for dx in range(1, HALO) for dy in range(1, HALO)]
CORNER_ROWS = -(-len(corner) // 8) * 8


def collide(flow, solute, kind):
    pore = kind == 0.0
    solid = kind == 1.0
    inlet = kind == 2.0
    zero = jnp.zeros_like(kind)
    pairs = range(1, FLOW, 2)
    total = {i: flow[i] + flow[i + 1] for i in pairs}
    gap = {i: flow[i] - flow[i + 1] for i in pairs}
    density = (flow[0] + total[1] + total[3]) + (total[5] + total[7] + total[9])
    density = density + ((total[11] + total[13]) + (total[15] + total[17]))
    mom_x = (gap[1] + gap[7]) + (gap[9] + gap[11]) + gap[13]
    mom_y = (gap[3] + gap[7]) + (gap[15] - gap[9]) + gap[17]
    mom_z = (gap[5] + gap[11]) + (gap[15] - gap[13]) - gap[17]
    square = mom_x * mom_x + mom_y * mom_y + mom_z * mom_z
    wall = jnp.where(solid, 0.5, zero)
    even = jnp.where(pore, (1.0 - flow_plus) / 2.0, wall)
    odd = jnp.where(pore, (1.0 - flow_minus) / 2.0, -wall)
    border = jnp.where(inlet, inlet_density, jnp.where(solid, 0.0, outlet_density))
    base = jnp.where(pore, flow_plus * density - (1.5 * flow_plus) * square, border)
    base_18 = base * (1.0 / 18.0)
    base_36 = base * (1.0 / 36.0)
    scale = math.sqrt(4.5 * flow_plus / 36.0)
    held = jnp.where(pore, scale, zero)
    vel = (mom_x * held, mom_y * held, mom_z * held)
    along = 3.0 * flow_minus / (36.0 * scale)
    out = [None] * COUNT
    out[0] = (even + even) * flow[0] + base * (1.0 / 3.0)
    for i in pairs:
        cx, cy, cz = flow_velocity[i]
        parts = [(c, v) for c, v in zip((cx, cy, cz), vel) if c != 0]
        if len(parts) == 1:
            t = parts[0][1]
            a = even * total[i] + (base_18 + 2.0 * (t * t))
            b = odd * gap[i] + (2.0 * along) * t
        else:
            t = parts[0][1] + parts[1][1] if parts[1][0] > 0 else parts[0][1] - parts[1][1]
            a = even * total[i] + (base_36 + t * t)
            b = odd * gap[i] + along * t
        out[i] = a + b
        out[i + 1] = a - b
    total = {i: solute[i] + solute[i + 1] for i in (1, 3, 5)}
    gap = {i: solute[i] - solute[i + 1] for i in (1, 3, 5)}
    concentration = (solute[0] + total[1]) + (total[3] + total[5])
    even = jnp.where(pore, (1.0 - solute_plus) / 2.0, wall)
    odd = jnp.where(pore, (1.0 - solute_minus) / 2.0, -wall)
    border = jnp.where(inlet, inlet_solute, zero)
    base = jnp.where(pore, solute_plus * concentration, border) * 0.125
    drift = concentration * (0.5 * solute_minus / scale)
    out[FLOW] = (even + even) * solute[0] + (base + base)
    for i, t in zip((1, 3, 5), vel):
        a = even * total[i] + base
        b = odd * gap[i] + drift * t
        out[FLOW + i] = a + b
        out[FLOW + i + 1] = a - b
    return out


def depth_shift(section, along_z, lane):
    depth = section.shape[-1]
    if along_z == 1:
        return jnp.where(lane == 0, 0.0, pltpu.roll(section, 1, section.ndim - 1))
    if along_z == -1:
        return jnp.where(lane == depth - 1, 0.0, pltpu.roll(section, depth - 1, section.ndim - 1))
    return section


def store_outgoing(values, lane, store):
    for c in range(COUNT):
        store(c, depth_shift(values[c], all_velocity[c][2], lane))


def first_kernel(cells_x, cells_y, odd_ref, flow_ref, solute_ref, kind_ref, post_ref, kindf_ref,
                 xa_ref, xb_ref, ya_ref, yb_ref, cab_ref, cbb_ref):
    depth = kind_ref.shape[-1]
    lane = lax.broadcasted_iota(jnp.int32, (cells_y, depth), 1)

    def plane(x, carry):
        kind = kind_ref[x].astype(jnp.float32)
        rows = pl.ds(pl.multiple_of(x * cells_y, cells_y), cells_y)
        kindf_ref[rows, :] = kind
        values = collide(
            [flow_ref[c, x] for c in range(FLOW)],
            [solute_ref[c, x] for c in range(COUNT - FLOW)],
            kind,
        )

        def store(c, value):
            post_ref[c, rows, :] = value

        store_outgoing(values, lane, store)
        return carry

    lax.fori_loop(0, cells_x, plane, 0)

    def held(c, where):
        return kindf_ref[where, :] if c == KIND else post_ref[c, where, :]

    for odd_x in (0, 1):

        @pl.when(odd_ref[0] == odd_x)
        def _():
            for ref, sign in ((xa_ref, 1 - 2 * odd_x), (xb_ref, 2 * odd_x - 1)):
                for k, (c, d) in enumerate(face_x):
                    x = cells_x - d if sign > 0 else d - 1
                    ref[k] = held(mirrored(c, sign, 1), pl.ds(x * cells_y, cells_y))

    for odd_y in (0, 1):

        @pl.when(odd_ref[1] == odd_y)
        def _():
            for ref, sign in ((ya_ref, 1 - 2 * odd_y), (yb_ref, 2 * odd_y - 1)):
                for k, (c, d) in enumerate(face_y):
                    y = cells_y - d if sign > 0 else d - 1
                    ref[k] = held(mirrored(c, 1, sign), pl.ds(y, cells_x, stride=cells_y))

    for odd_x in (0, 1):
        for odd_y in (0, 1):

            @pl.when((odd_ref[0] == odd_x) & (odd_ref[1] == odd_y))
            def _():
                sign_y = 2 * odd_y - 1
                for ref, sign_x in ((cab_ref, 1 - 2 * odd_x), (cbb_ref, 2 * odd_x - 1)):
                    for k, (c, dx, dy) in enumerate(corner):
                        x = cells_x - dx if sign_x > 0 else dx - 1
                        y = cells_y - dy if sign_y > 0 else dy - 1
                        ref[pl.ds(k, 1), :] = held(
                            mirrored(c, sign_x, sign_y), pl.ds(x * cells_y + y, 1)
                        )


def forward_kernel(cells_y, odd_ref, xa_ref, xb_ref, out_ref):
    for odd_y in (0, 1):

        @pl.when(odd_ref[1] == odd_y)
        def _():
            sign_y = 1 - 2 * odd_y
            for side, ref in enumerate((xa_ref, xb_ref)):
                for k, (c, dx, dy) in enumerate(corner):
                    y = cells_y - dy if sign_y > 0 else dy - 1
                    out_ref[side, pl.ds(k, 1), :] = ref[
                        face_x.index((mirrored(c, 1, sign_y), dx)), pl.ds(y, 1), :
                    ]


def last_kernel(cells_x, cells_y, odd_ref, post_ref, kindf_ref, xa_ref, xb_ref, ya_ref, yb_ref,
                cab_ref, cbb_ref, cya_ref, density_ref, momentum_ref, concentration_ref,
                one_ref, two_ref, kinds_ref):
    depth = post_ref.shape[-1]
    pitch = cells_y + 2 * HALO

    def row(x, y):
        return (x + HALO) * pitch + y + HALO

    def put(c, where, value):
        if c == KIND:
            kinds_ref[where, :] = value
        else:
            one_ref[c, where, :] = value

    for x in range(cells_x):
        for c in range(COUNT):
            put(c, pl.ds(row(x, 0), cells_y), post_ref[c, pl.ds(x * cells_y, cells_y), :])
        put(KIND, pl.ds(row(x, 0), cells_y), kindf_ref[pl.ds(x * cells_y, cells_y), :])

    def beyond(cells, sign, d):
        return cells - 1 + d if sign > 0 else -d

    for odd_x in (0, 1):

        @pl.when(odd_ref[0] == odd_x)
        def _():
            for ref, sign in ((xa_ref, 1 - 2 * odd_x), (xb_ref, 2 * odd_x - 1)):
                for k, (c, d) in enumerate(face_x):
                    put(
                        mirrored(c, -sign, 1),
                        pl.ds(row(beyond(cells_x, sign, d), 0), cells_y),
                        ref[k],
                    )

    for odd_y in (0, 1):

        @pl.when(odd_ref[1] == odd_y)
        def _():
            for ref, sign in ((ya_ref, 1 - 2 * odd_y), (yb_ref, 2 * odd_y - 1)):
                for k, (c, d) in enumerate(face_y):
                    put(
                        mirrored(c, 1, -sign),
                        pl.ds(row(0, beyond(cells_y, sign, d)), cells_x, stride=pitch),
                        ref[k],
                    )

    for odd_x in (0, 1):
        for odd_y in (0, 1):

            @pl.when((odd_ref[0] == odd_x) & (odd_ref[1] == odd_y))
            def _():
                to_a, to_b = 1 - 2 * odd_x, 2 * odd_x - 1
                pair, far = 1 - 2 * odd_y, 2 * odd_y - 1
                for ref, sign_x, sign_y in (
                    (cab_ref, to_a, far),
                    (cbb_ref, to_b, far),
                    (cya_ref.at[0], to_a, pair),
                    (cya_ref.at[1], to_b, pair),
                ):
                    for k, (c, dx, dy) in enumerate(corner):
                        put(
                            mirrored(c, -sign_x, -sign_y),
                            pl.ds(row(beyond(cells_x, sign_x, dx), beyond(cells_y, sign_y, dy)), 1),
                            ref[pl.ds(k, 1), :],
                        )

    lane = lax.broadcasted_iota(jnp.int32, (8, depth), 1)

    def arriving(ref, c, start, size):
        cx, cy, _ = all_velocity[c]
        return ref[c, pl.ds(start - (cx * pitch + cy), size), :]

    def advance(source, target, width):
        first = row(-width, -width)
        chunks = -(-(row(cells_x - 1 + width, cells_y - 1 + width) + 1 - first) // 8)

        def chunk(k, carry):
            start = first + 8 * k
            values = [arriving(source, c, start, 8) for c in range(COUNT)]
            values = collide(values[:FLOW], values[FLOW:], kinds_ref[pl.ds(start, 8), :])

            def store(c, value):
                target[c, pl.ds(start, 8), :] = value

            store_outgoing(values, lane, store)
            return carry

        lax.fori_loop(0, chunks, chunk, 0)

    source, target = one_ref, two_ref
    for width in range(HALO - 1, 0, -1):
        advance(source, target, width)
        source, target = target, source

    def plane(x, carry):
        start = row(0, 0) + x * pitch
        values = [arriving(source, c, start, cells_y) for c in range(COUNT)]
        total = functools.reduce(jnp.add, values[:FLOW])
        density_ref[x] = total
        for axis in range(3):
            summed = None
            for c in range(FLOW):
                part = all_velocity[c][axis]
                if part == 0:
                    continue
                if summed is None:
                    summed = values[c] if part > 0 else -values[c]
                else:
                    summed = summed + values[c] if part > 0 else summed - values[c]
            momentum_ref[axis, x] = summed
        concentration_ref[x] = functools.reduce(jnp.add, values[FLOW:])
        return carry

    lax.fori_loop(0, cells_x, plane, 0)


def near(i, count):
    return i ^ 1


def across(i, count):
    return (i + 1) % count if i % 2 else (i - 1) % count


def swapped(block, count_x, count_y, move_x, move_y):
    pairs = []
    for i in range(count_x):
        for j in range(count_y):
            to_x = move_x(i, count_x) if move_x else i
            to_y = move_y(j, count_y) if move_y else j
            pairs.append((i * count_y + j, to_x * count_y + to_y))
    return lax.ppermute(block, ("gx", "gy"), pairs)


def solution(mesh):
    count_x, count_y = mesh.shape["gx"], mesh.shape["gy"]
    assert count_x % 2 == 0 and count_y % 2 == 0

    def local(flow, solute, kind):
        _, cells_x, cells_y, depth = flow.shape
        f32 = jnp.float32
        shape = lambda *dims: jax.ShapeDtypeStruct(dims, f32)
        smem = pl.BlockSpec(memory_space=pltpu.SMEM)
        vmem = pl.BlockSpec(memory_space=pltpu.VMEM)
        params = pltpu.CompilerParams(vmem_limit_bytes=40 * 1024 * 1024)
        odd = jnp.stack([lax.axis_index("gx") % 2, lax.axis_index("gy") % 2]).astype(jnp.int32)
        rows = cells_x * cells_y
        post, kindf, xa, xb, ya, yb, cab, cbb = pl.pallas_call(
            functools.partial(first_kernel, cells_x, cells_y),
            out_shape=[
                shape(COUNT, rows, depth),
                shape(rows, depth),
                shape(len(face_x), cells_y, depth),
                shape(len(face_x), cells_y, depth),
                shape(len(face_y), cells_x, depth),
                shape(len(face_y), cells_x, depth),
                shape(CORNER_ROWS, depth),
                shape(CORNER_ROWS, depth),
            ],
            in_specs=[smem, vmem, vmem, vmem],
            out_specs=[vmem] * 8,
            compiler_params=params,
        )(odd, flow, solute, kind)
        move = functools.partial(swapped, count_x=count_x, count_y=count_y)
        xb = move(xb, move_x=across, move_y=None)
        yb = move(yb, move_x=None, move_y=across)
        xa = move(xa, move_x=near, move_y=None)
        cbb = move(cbb, move_x=across, move_y=across)
        cab = move(cab, move_x=near, move_y=across)
        ya = move(ya, move_x=None, move_y=near)
        cya = pl.pallas_call(
            functools.partial(forward_kernel, cells_y),
            out_shape=shape(2, CORNER_ROWS, depth),
            in_specs=[smem, vmem, vmem],
            out_specs=vmem,
            compiler_params=params,
        )(odd, xa, xb)
        cya = move(cya, move_x=None, move_y=near)
        pitch = cells_y + 2 * HALO
        extended = -(-((cells_x + 2 * HALO) * pitch + 16) // 8) * 8
        return pl.pallas_call(
            functools.partial(last_kernel, cells_x, cells_y),
            out_shape=[
                shape(cells_x, cells_y, depth),
                shape(3, cells_x, cells_y, depth),
                shape(cells_x, cells_y, depth),
            ],
            in_specs=[smem] + [vmem] * 9,
            out_specs=[vmem] * 3,
            scratch_shapes=[
                pltpu.VMEM((COUNT, extended, depth), f32),
                pltpu.VMEM((COUNT, extended, depth), f32),
                pltpu.VMEM((extended, depth), f32),
            ],
            compiler_params=params,
        )(odd, post, kindf, xa, xb, ya, yb, cab, cbb, cya)

    placed = (P(None, "gx", "gy", None), P(None, "gx", "gy", None), P("gx", "gy", None))
    return jax.shard_map(
        lambda *args: tuple(local(*args)),
        mesh=mesh,
        in_specs=placed,
        out_specs=(P("gx", "gy", None), P(None, "gx", "gy", None), P("gx", "gy", None)),
        check_vma=False,
    )
```

```python
import functools
import math

import jax
import jax.numpy as jnp
from jax import lax
from jax.experimental import pallas as pl
from jax.experimental.pallas import tpu as pltpu
from jax.sharding import PartitionSpec as P

STEPS = 3
HALO = STEPS

flow_velocity = [
    (0, 0, 0),
    (1, 0, 0),
    (-1, 0, 0),
    (0, 1, 0),
    (0, -1, 0),
    (0, 0, 1),
    (0, 0, -1),
    (1, 1, 0),
    (-1, -1, 0),
    (1, -1, 0),
    (-1, 1, 0),
    (1, 0, 1),
    (-1, 0, -1),
    (1, 0, -1),
    (-1, 0, 1),
    (0, 1, 1),
    (0, -1, -1),
    (0, 1, -1),
    (0, -1, 1),
]
FLOW = len(flow_velocity)
all_velocity = flow_velocity + flow_velocity[:7]
COUNT = len(all_velocity)
KIND = COUNT
flow_plus = 1.25
flow_minus = 1.0 / 1.125
solute_plus = 1.0 / 1.75
solute_minus = 1.0 / 0.7
inlet_density = 1.05
outlet_density = 0.95
inlet_solute = 1.0


def mirrored(channel, sign_x, sign_y):
    if channel == KIND:
        return KIND
    cx, cy, cz = all_velocity[channel]
    wanted = (cx * sign_x, cy * sign_y, cz)
    if channel < FLOW:
        return flow_velocity.index(wanted)
    return FLOW + flow_velocity[:7].index(wanted)


face_x = [
    (c, d) for d in range(1, HALO + 1) for c in range(COUNT) if d - all_velocity[c][0] <= HALO - 1
] + [(KIND, d) for d in range(1, HALO)]
face_y = [
    (c, d) for d in range(1, HALO + 1) for c in range(COUNT) if d - all_velocity[c][1] <= HALO - 1
] + [(KIND, d) for d in range(1, HALO)]
corner = [
    (c, dx, dy)
    for dx in range(1, HALO + 1)
    for dy in range(1, HALO + 1)
    for c in range(COUNT)
    if dx - all_velocity[c][0] <= HALO - 1 and dy - all_velocity[c][1] <= HALO - 1
] + [(KIND, dx, dy) for dx in range(1, HALO) for dy in range(1, HALO)]
CORNER_ROWS = -(-len(corner) // 8) * 8


def collide(flow, solute, kind):
    pore = kind == 0.0
    solid = kind == 1.0
    inlet = kind == 2.0
    zero = jnp.zeros_like(kind)
    pairs = range(1, FLOW, 2)
    total = {i: flow[i] + flow[i + 1] for i in pairs}
    gap = {i: flow[i] - flow[i + 1] for i in pairs}
    density = (flow[0] + total[1] + total[3]) + (total[5] + total[7] + total[9])
    density = density + ((total[11] + total[13]) + (total[15] + total[17]))
    mom_x = (gap[1] + gap[7]) + (gap[9] + gap[11]) + gap[13]
    mom_y = (gap[3] + gap[7]) + (gap[15] - gap[9]) + gap[17]
    mom_z = (gap[5] + gap[11]) + (gap[15] - gap[13]) - gap[17]
    square = mom_x * mom_x + mom_y * mom_y + mom_z * mom_z
    wall = jnp.where(solid, 0.5, zero)
    even = jnp.where(pore, (1.0 - flow_plus) / 2.0, wall)
    odd = jnp.where(pore, (1.0 - flow_minus) / 2.0, -wall)
    border = jnp.where(inlet, inlet_density, jnp.where(solid, 0.0, outlet_density))
    base = jnp.where(pore, flow_plus * density - (1.5 * flow_plus) * square, border)
    base_18 = base * (1.0 / 18.0)
    base_36 = base * (1.0 / 36.0)
    scale = math.sqrt(4.5 * flow_plus / 36.0)
    held = jnp.where(pore, scale, zero)
    vel = (mom_x * held, mom_y * held, mom_z * held)
    along = 3.0 * flow_minus / (36.0 * scale)
    out = [None] * COUNT
    out[0] = (even + even) * flow[0] + base * (1.0 / 3.0)
    for i in pairs:
        cx, cy, cz = flow_velocity[i]
        parts = [(c, v) for c, v in zip((cx, cy, cz), vel) if c != 0]
        if len(parts) == 1:
            t = parts[0][1]
            a = even * total[i] + (base_18 + 2.0 * (t * t))
            b = odd * gap[i] + (2.0 * along) * t
        else:
            t = parts[0][1] + parts[1][1] if parts[1][0] > 0 else parts[0][1] - parts[1][1]
            a = even * total[i] + (base_36 + t * t)
            b = odd * gap[i] + along * t
        out[i] = a + b
        out[i + 1] = a - b
    total = {i: solute[i] + solute[i + 1] for i in (1, 3, 5)}
    gap = {i: solute[i] - solute[i + 1] for i in (1, 3, 5)}
    concentration = (solute[0] + total[1]) + (total[3] + total[5])
    even = jnp.where(pore, (1.0 - solute_plus) / 2.0, wall)
    odd = jnp.where(pore, (1.0 - solute_minus) / 2.0, -wall)
    border = jnp.where(inlet, inlet_solute, zero)
    base = jnp.where(pore, solute_plus * concentration, border) * 0.125
    drift = concentration * (0.5 * solute_minus / scale)
    out[FLOW] = (even + even) * solute[0] + (base + base)
    for i, t in zip((1, 3, 5), vel):
        a = even * total[i] + base
        b = odd * gap[i] + drift * t
        out[FLOW + i] = a + b
        out[FLOW + i + 1] = a - b
    return out


def depth_shift(section, along_z, lane):
    depth = section.shape[-1]
    if along_z == 1:
        return jnp.where(lane == 0, 0.0, pltpu.roll(section, 1, section.ndim - 1))
    if along_z == -1:
        return jnp.where(lane == depth - 1, 0.0, pltpu.roll(section, depth - 1, section.ndim - 1))
    return section


def store_shifted(values, lane, store):
    for c in range(COUNT):
        store(c, depth_shift(values[c], all_velocity[c][2], lane))


class Extended:
    def __init__(self, cells_x, cells_y):
        self.cells_x, self.cells_y = cells_x, cells_y
        self.pitch = cells_y + 2 * HALO
        self.rows = -(-((cells_x + 2 * HALO) * self.pitch + 16) // 8) * 8

    def row(self, x, y):
        return (x + HALO) * self.pitch + y + HALO


def first_kernel(ext, group, odd_ref, flow_hbm, solute_hbm, kind_hbm, post_ref, kinds_ref,
                 up_ref, down_ref, ya_ref, yb_ref, cup_ref, cdown_ref,
                 flow_ref, solute_ref, kind_ref, sems):
    cells_x, cells_y = ext.cells_x, ext.cells_y
    depth = kind_ref.shape[-1]
    lane = lax.broadcasted_iota(jnp.int32, (cells_y, depth), 1)
    copies = []
    for g in range(cells_x // group):
        planes = pl.ds(g * group, group)
        copies.append([
            pltpu.make_async_copy(kind_hbm.at[planes], kind_ref.at[planes], sems.at[g, 0]),
            pltpu.make_async_copy(flow_hbm.at[:, planes], flow_ref.at[:, planes], sems.at[g, 1]),
            pltpu.make_async_copy(
                solute_hbm.at[:, planes], solute_ref.at[:, planes], sems.at[g, 2]
            ),
        ])
        for copy in copies[-1]:
            copy.start()

    for x in range(cells_x):
        if x % group == 0:
            for copy in copies[x // group]:
                copy.wait()
        kind = kind_ref[x].astype(jnp.float32)
        rows = pl.ds(ext.row(x, 0), cells_y)
        kinds_ref[rows, :] = kind
        values = collide(
            [flow_ref[c, x] for c in range(FLOW)],
            [solute_ref[c, x] for c in range(COUNT - FLOW)],
            kind,
        )

        def store(c, value):
            post_ref[c, rows, :] = value

        store_shifted(values, lane, store)

    def held(c, where):
        return kinds_ref[where, :] if c == KIND else post_ref[c, where, :]

    def at(cells, sign, d):
        return cells - d if sign > 0 else d - 1

    for ref, sign in ((up_ref, 1), (down_ref, -1)):
        for k, (c, d) in enumerate(face_x):
            ref[k] = held(mirrored(c, sign, 1), pl.ds(ext.row(at(cells_x, sign, d), 0), cells_y))

    for odd_y in (0, 1):

        @pl.when(odd_ref[0] == odd_y)
        def _():
            for ref, sign in ((ya_ref, 1 - 2 * odd_y), (yb_ref, 2 * odd_y - 1)):
                for k, (c, d) in enumerate(face_y):
                    where = pl.ds(ext.row(0, at(cells_y, sign, d)), cells_x, stride=ext.pitch)
                    ref[k] = held(mirrored(c, 1, sign), where)
            sign_y = 2 * odd_y - 1
            for ref, sign_x in ((cup_ref, 1), (cdown_ref, -1)):
                for k, (c, dx, dy) in enumerate(corner):
                    row = ext.row(at(cells_x, sign_x, dx), at(cells_y, sign_y, dy))
                    ref[pl.ds(k, 1), :] = held(mirrored(c, sign_x, sign_y), pl.ds(row, 1))


def forward_kernel(cells_y, odd_ref, up_ref, down_ref, out_ref):
    for odd_y in (0, 1):

        @pl.when(odd_ref[0] == odd_y)
        def _():
            sign_y = 1 - 2 * odd_y
            for side, ref in enumerate((up_ref, down_ref)):
                for k, (c, dx, dy) in enumerate(corner):
                    y = cells_y - dy if sign_y > 0 else dy - 1
                    out_ref[side, pl.ds(k, 1), :] = ref[
                        face_x.index((mirrored(c, 1, sign_y), dx)), pl.ds(y, 1), :
                    ]


def beyond(cells, sign, d):
    return cells - 1 + d if sign > 0 else -d


def last_kernel(ext, odd_ref, _, __, up_ref, down_ref, ya_ref, yb_ref, cup_ref, cdown_ref,
                cpair_ref, density_ref, momentum_ref, concentration_ref, one_ref, kinds_ref,
                two_ref):
    cells_x, cells_y, pitch, row = ext.cells_x, ext.cells_y, ext.pitch, ext.row
    depth = one_ref.shape[-1]

    def put(c, where, value):
        if c == KIND:
            kinds_ref[where, :] = value
        else:
            one_ref[c, where, :] = value

    for ref, sign in ((up_ref, -1), (down_ref, 1)):
        for k, (c, d) in enumerate(face_x):
            put(mirrored(c, -sign, 1), pl.ds(row(beyond(cells_x, sign, d), 0), cells_y), ref[k])

    for odd_y in (0, 1):

        @pl.when(odd_ref[0] == odd_y)
        def _():
            for ref, sign in ((ya_ref, 1 - 2 * odd_y), (yb_ref, 2 * odd_y - 1)):
                for k, (c, d) in enumerate(face_y):
                    put(
                        mirrored(c, 1, -sign),
                        pl.ds(row(0, beyond(cells_y, sign, d)), cells_x, stride=pitch),
                        ref[k],
                    )
            pair, far = 1 - 2 * odd_y, 2 * odd_y - 1
            for ref, sign_x, sign_y in (
                (cup_ref, -1, far),
                (cdown_ref, 1, far),
                (cpair_ref.at[0], -1, pair),
                (cpair_ref.at[1], 1, pair),
            ):
                for k, (c, dx, dy) in enumerate(corner):
                    put(
                        mirrored(c, -sign_x, -sign_y),
                        pl.ds(row(beyond(cells_x, sign_x, dx), beyond(cells_y, sign_y, dy)), 1),
                        ref[pl.ds(k, 1), :],
                    )

    lane = lax.broadcasted_iota(jnp.int32, (8, depth), 1)

    def arriving(ref, c, start, size):
        cx, cy, _ = all_velocity[c]
        return ref[c, pl.ds(start - (cx * pitch + cy), size), :]

    def advance(source, target, width):
        first = row(-width, -width)
        for start in range(first, row(cells_x - 1 + width, cells_y - 1 + width) + 1, 8):
            values = [arriving(source, c, start, 8) for c in range(COUNT)]
            values = collide(values[:FLOW], values[FLOW:], kinds_ref[pl.ds(start, 8), :])

            def store(c, value):
                target[c, pl.ds(start, 8), :] = value

            if width > 1:
                store_shifted(values, lane, store)
            else:
                for c in range(COUNT):
                    store(c, values[c])

    source, target = one_ref, two_ref
    for width in range(HALO - 1, 0, -1):
        advance(source, target, width)
        source, target = target, source

    def summed(values, weights):
        total = None
        for along_z in (0, 1, -1):
            part = None
            for c, weight in weights.items():
                if weight == 0 or all_velocity[c][2] != along_z:
                    continue
                if part is None:
                    part = values[c] if weight > 0 else -values[c]
                else:
                    part = part + values[c] if weight > 0 else part - values[c]
            if part is not None:
                part = depth_shift(part, along_z, lane)
                total = part if total is None else total + part
        return total

    flow = range(FLOW)
    for x in range(cells_x):
        values = [arriving(source, c, row(x, 0), cells_y) for c in range(COUNT)]
        density_ref[x] = summed(values, {c: 1 for c in flow})
        for axis in range(3):
            momentum_ref[axis, x] = summed(values, {c: flow_velocity[c][axis] for c in flow})
        concentration_ref[x] = summed(values, {c: 1 for c in range(FLOW, COUNT)})


def higher(i, count):
    return (i + 1) % count


def lower(i, count):
    return (i - 1) % count


def near(i, count):
    return i ^ 1


def across(i, count):
    return (i + 1) % count if i % 2 else (i - 1) % count


def swapped(block, count_x, count_y, move_x, move_y):
    pairs = []
    for i in range(count_x):
        for j in range(count_y):
            to_x = move_x(i, count_x) if move_x else i
            to_y = move_y(j, count_y) if move_y else j
            pairs.append((i * count_y + j, to_x * count_y + to_y))
    return lax.ppermute(block, ("gx", "gy"), pairs)


def solution(mesh):
    count_x, count_y = mesh.shape["gx"], mesh.shape["gy"]
    assert count_y % 2 == 0

    def local(flow, solute, kind):
        _, cells_x, cells_y, depth = flow.shape
        f32 = jnp.float32
        shape = lambda *dims: jax.ShapeDtypeStruct(dims, f32)
        smem = pl.BlockSpec(memory_space=pltpu.SMEM)
        vmem = pl.BlockSpec(memory_space=pltpu.VMEM)
        hbm = pl.BlockSpec(memory_space=pltpu.HBM)
        params = pltpu.CompilerParams(vmem_limit_bytes=40 * 1024 * 1024)
        odd = jnp.reshape(lax.axis_index("gy") % 2, (1,)).astype(jnp.int32)
        ext = Extended(cells_x, cells_y)
        group = math.gcd(cells_x, 4)
        flow, solute, kind = (
            pltpu.with_memory_space_constraint(a, pltpu.HBM) for a in (flow, solute, kind)
        )
        post, kinds, up, down, ya, yb, cup, cdown = pl.pallas_call(
            functools.partial(first_kernel, ext, group),
            out_shape=[
                shape(COUNT, ext.rows, depth),
                shape(ext.rows, depth),
                shape(len(face_x), cells_y, depth),
                shape(len(face_x), cells_y, depth),
                shape(len(face_y), cells_x, depth),
                shape(len(face_y), cells_x, depth),
                shape(CORNER_ROWS, depth),
                shape(CORNER_ROWS, depth),
            ],
            in_specs=[smem, hbm, hbm, hbm],
            out_specs=[vmem] * 8,
            scratch_shapes=[
                pltpu.VMEM(flow.shape, f32),
                pltpu.VMEM(solute.shape, f32),
                pltpu.VMEM(kind.shape, kind.dtype),
                pltpu.SemaphoreType.DMA((cells_x // group, 3)),
            ],
            compiler_params=params,
        )(odd, flow, solute, kind)
        move = functools.partial(swapped, count_x=count_x, count_y=count_y)
        up = move(up, move_x=higher, move_y=None)
        down = move(down, move_x=lower, move_y=None)
        yb = move(yb, move_x=None, move_y=across)
        cup = move(cup, move_x=higher, move_y=across)
        cdown = move(cdown, move_x=lower, move_y=across)
        ya, up, down, yb, cup, cdown = lax.optimization_barrier((ya, up, down, yb, cup, cdown))
        ya = move(ya, move_x=None, move_y=near)
        cpair = pl.pallas_call(
            functools.partial(forward_kernel, cells_y),
            out_shape=shape(2, CORNER_ROWS, depth),
            in_specs=[smem, vmem, vmem],
            out_specs=vmem,
            compiler_params=params,
        )(odd, up, down)
        cpair = move(cpair, move_x=None, move_y=near)
        density, momentum, concentration, _, _ = pl.pallas_call(
            functools.partial(last_kernel, ext),
            out_shape=[
                shape(cells_x, cells_y, depth),
                shape(3, cells_x, cells_y, depth),
                shape(cells_x, cells_y, depth),
                shape(COUNT, ext.rows, depth),
                shape(ext.rows, depth),
            ],
            in_specs=[smem] + [vmem] * 9,
            out_specs=[vmem] * 5,
            scratch_shapes=[pltpu.VMEM((COUNT, ext.rows, depth), f32)],
            input_output_aliases={1: 3, 2: 4},
            compiler_params=params,
        )(odd, post, kinds, up, down, ya, yb, cup, cdown, cpair)
        return density, momentum, concentration

    placed = (P(None, "gx", "gy", None), P(None, "gx", "gy", None), P("gx", "gy", None))
    return jax.shard_map(
        local,
        mesh=mesh,
        in_specs=placed,
        out_specs=(P("gx", "gy", None), P(None, "gx", "gy", None), P("gx", "gy", None)),
        check_vma=False,
    )
```

```python
import functools
import math

import jax
import jax.numpy as jnp
from jax import lax
from jax.experimental import pallas as pl
from jax.experimental.pallas import tpu as pltpu
from jax.sharding import PartitionSpec as P

STEPS = 3
HALO = STEPS

flow_velocity = [
    (0, 0, 0),
    (1, 0, 0),
    (-1, 0, 0),
    (0, 1, 0),
    (0, -1, 0),
    (0, 0, 1),
    (0, 0, -1),
    (1, 1, 0),
    (-1, -1, 0),
    (1, -1, 0),
    (-1, 1, 0),
    (1, 0, 1),
    (-1, 0, -1),
    (1, 0, -1),
    (-1, 0, 1),
    (0, 1, 1),
    (0, -1, -1),
    (0, 1, -1),
    (0, -1, 1),
]
FLOW = len(flow_velocity)
all_velocity = flow_velocity + flow_velocity[:7]
COUNT = len(all_velocity)
KIND = COUNT
SUMS = {0: range(COUNT + 1, COUNT + 5), 1: range(COUNT + 5, COUNT + 9)}
flow_plus = 1.25
flow_minus = 1.0 / 1.125
solute_plus = 1.0 / 1.75
solute_minus = 1.0 / 0.7
inlet_density = 1.05
outlet_density = 0.95
inlet_solute = 1.0


def mirrored(channel, sign_x, sign_y):
    if channel >= KIND:
        return channel
    cx, cy, cz = all_velocity[channel]
    wanted = (cx * sign_x, cy * sign_y, cz)
    if channel < FLOW:
        return flow_velocity.index(wanted)
    return FLOW + flow_velocity[:7].index(wanted)


def moving(axis, toward):
    return [c for c in range(COUNT) if all_velocity[c][axis] == toward]


def needed(axis):
    outer = HALO - 1
    return (
        [(c, d) for d in range(1, outer) for c in range(COUNT)]
        + [(c, d) for d in (outer, HALO) for c in moving(axis, 1)]
        + [(c, outer) for c in SUMS[axis]]
        + [(KIND, d) for d in range(1, HALO)]
    )


face_x = needed(0)
face_y = needed(1)
ends_x = [c for c in moving(0, 0) if all_velocity[c][1] == 1]
ends_y = [c for c in moving(1, 0) if all_velocity[c][0] == 1]


def reach(channel):
    return HALO - 1 + (all_velocity[channel][1] if channel < COUNT else 0)


corner_start = [sum(reach(c) for c, _ in face_x[:k]) for k in range(len(face_x) + 1)]
ENDS_START = corner_start[-1]
CORNER_ROWS = -(-(ENDS_START + len(ends_x)) // 8) * 8
FACE_X_SUMS = face_x.index((SUMS[0][0], HALO - 1))
FACE_Y_SUMS = face_y.index((SUMS[1][0], HALO - 1))


def collide(flow, solute, kind):
    pore = kind == 0.0
    solid = kind == 1.0
    inlet = kind == 2.0
    zero = jnp.zeros_like(kind)
    pairs = range(1, FLOW, 2)
    total = {i: flow[i] + flow[i + 1] for i in pairs}
    gap = {i: flow[i] - flow[i + 1] for i in pairs}
    density = (flow[0] + total[1] + total[3]) + (total[5] + total[7] + total[9])
    density = density + ((total[11] + total[13]) + (total[15] + total[17]))
    mom_x = (gap[1] + gap[7]) + (gap[9] + gap[11]) + gap[13]
    mom_y = (gap[3] + gap[7]) + (gap[15] - gap[9]) + gap[17]
    mom_z = (gap[5] + gap[11]) + (gap[15] - gap[13]) - gap[17]
    square = mom_x * mom_x + mom_y * mom_y + mom_z * mom_z
    wall = jnp.where(solid, 0.5, zero)
    even = jnp.where(pore, (1.0 - flow_plus) / 2.0, wall)
    odd = jnp.where(pore, (1.0 - flow_minus) / 2.0, -wall)
    border = jnp.where(inlet, inlet_density, jnp.where(solid, 0.0, outlet_density))
    base = jnp.where(pore, flow_plus * density - (1.5 * flow_plus) * square, border)
    base_18 = base * (1.0 / 18.0)
    base_36 = base * (1.0 / 36.0)
    scale = math.sqrt(4.5 * flow_plus / 36.0)
    held = jnp.where(pore, scale, zero)
    vel = (mom_x * held, mom_y * held, mom_z * held)
    along = 3.0 * flow_minus / (36.0 * scale)
    out = [None] * COUNT
    out[0] = (even + even) * flow[0] + base * (1.0 / 3.0)
    for i in pairs:
        cx, cy, cz = flow_velocity[i]
        parts = [(c, v) for c, v in zip((cx, cy, cz), vel) if c != 0]
        if len(parts) == 1:
            t = parts[0][1]
            a = even * total[i] + (base_18 + 2.0 * (t * t))
            b = odd * gap[i] + (2.0 * along) * t
        else:
            t = parts[0][1] + parts[1][1] if parts[1][0] > 0 else parts[0][1] - parts[1][1]
            a = even * total[i] + (base_36 + t * t)
            b = odd * gap[i] + along * t
        out[i] = a + b
        out[i + 1] = a - b
    total = {i: solute[i] + solute[i + 1] for i in (1, 3, 5)}
    gap = {i: solute[i] - solute[i + 1] for i in (1, 3, 5)}
    concentration = (solute[0] + total[1]) + (total[3] + total[5])
    even = jnp.where(pore, (1.0 - solute_plus) / 2.0, wall)
    odd = jnp.where(pore, (1.0 - solute_minus) / 2.0, -wall)
    border = jnp.where(inlet, inlet_solute, zero)
    base = jnp.where(pore, solute_plus * concentration, border) * 0.125
    drift = concentration * (0.5 * solute_minus / scale)
    out[FLOW] = (even + even) * solute[0] + (base + base)
    for i, t in zip((1, 3, 5), vel):
        a = even * total[i] + base
        b = odd * gap[i] + drift * t
        out[FLOW + i] = a + b
        out[FLOW + i + 1] = a - b
    return out


def depth_shift(section, along_z, lane):
    depth = section.shape[-1]
    if along_z == 1:
        return jnp.where(lane == 0, 0.0, pltpu.roll(section, 1, section.ndim - 1))
    if along_z == -1:
        return jnp.where(lane == depth - 1, 0.0, pltpu.roll(section, depth - 1, section.ndim - 1))
    return section


def store_shifted(values, lane, store):
    for c in range(COUNT):
        store(c, depth_shift(values[c], all_velocity[c][2], lane))


class Extended:
    def __init__(self, cells_x, cells_y):
        self.cells_x, self.cells_y = cells_x, cells_y
        self.pitch = cells_y + 2 * HALO
        self.rows = -(-((cells_x + 2 * HALO) * self.pitch + 16) // 8) * 8

        self.face_y_rows = len(face_y) * cells_x + 2 * len(ends_y)
        self.inner_rows = cells_y - 2 * (HALO - 1)

    def row(self, x, y):
        return (x + HALO) * self.pitch + y + HALO

    def inner(self, channel):
        return HALO - 1 - (all_velocity[channel][1] if channel < COUNT else 0)


def first_kernel(ext, group, odd_ref, flow_hbm, solute_hbm, kind_hbm, post_ref, kinds_ref,
                 up_ref, down_ref, ya_ref, yb_ref, cup_ref, cdown_ref,
                 flow_ref, solute_ref, kind_ref, sums_ref, sems):
    cells_x, cells_y = ext.cells_x, ext.cells_y
    depth = kind_ref.shape[-1]
    lane = lax.broadcasted_iota(jnp.int32, (cells_y, depth), 1)
    copies = []
    for g in range(cells_x // group):
        planes = pl.ds(g * group, group)
        copies.append([
            pltpu.make_async_copy(kind_hbm.at[planes], kind_ref.at[planes], sems.at[g, 0]),
            pltpu.make_async_copy(flow_hbm.at[:, planes], flow_ref.at[:, planes], sems.at[g, 1]),
            pltpu.make_async_copy(
                solute_hbm.at[:, planes], solute_ref.at[:, planes], sems.at[g, 2]
            ),
        ])
        for copy in copies[-1]:
            copy.start()

    for x in range(cells_x):
        if x % group == 0:
            for copy in copies[x // group]:
                copy.wait()
        kind = kind_ref[x].astype(jnp.float32)
        rows = pl.ds(ext.row(x, 0), cells_y)
        kinds_ref[rows, :] = kind
        values = collide(
            [flow_ref[c, x] for c in range(FLOW)],
            [solute_ref[c, x] for c in range(COUNT - FLOW)],
            kind,
        )

        def store(c, value):
            post_ref[c, rows, :] = value

        store_shifted(values, lane, store)

    def sums(axis, where):
        across = 1 - axis
        cells = (cells_x, cells_y)[across]
        place = lax.broadcasted_iota(jnp.int32, (cells, depth), 0)
        parts = {}
        for move in (0, 1, -1):
            total = along = solute = None
            for c in moving(axis, 0):
                if all_velocity[c][across] != move:
                    continue
                value = post_ref[c, where(-move), :]
                if c >= FLOW:
                    solute = value if solute is None else solute + value
                    continue
                total = value if total is None else total + value
                cz = all_velocity[c][2]
                if cz != 0:
                    signed = value if cz > 0 else -value
                    along = signed if along is None else along + signed
            parts[move] = [total, along, solute]
            if move != 0:
                inside = place != (0 if move > 0 else cells - 1)
                parts[move] = [jnp.where(inside, p, 0.0) for p in parts[move]]
        total, along, solute = (parts[0][n] + parts[1][n] + parts[-1][n] for n in range(3))
        for c, value in zip(
            SUMS[axis], (total - along, parts[1][0] - parts[-1][0], along, solute)
        ):
            sums_ref[c - SUMS[0][0], where(0), :] = value

    def at(cells, sign, d):
        return cells - d if sign > 0 else d - 1

    def line_x(x):
        return lambda y: pl.ds(ext.row(x, y), cells_y)

    def line_y(y):
        return lambda x: pl.ds(ext.row(x, y), cells_x, stride=ext.pitch)

    zero = jnp.zeros((8, depth), jnp.float32)
    zeros = jnp.zeros((cells_x, depth), jnp.float32)
    for sign in (1, -1):
        sums(0, line_x(at(cells_x, sign, HALO - 1)))
        sums(1, line_y(at(cells_y, sign, HALO - 1)))
        for c in moving(0, 0):
            first = ext.row(beyond(cells_x, sign, HALO - 1), -HALO)
            for start in [*range(0, ext.pitch - 8, 8), ext.pitch - 8]:
                post_ref[c, pl.ds(first + start, 8), :] = zero
        for c in moving(1, 0):
            post_ref[c, line_y(beyond(cells_y, sign, HALO - 1))(0), :] = zeros

    def held(c, where):
        if c > KIND:
            return sums_ref[c - SUMS[0][0], where, :]
        return kinds_ref[where, :] if c == KIND else post_ref[c, where, :]

    for odd_y in (0, 1):

        @pl.when(odd_ref[0] == odd_y)
        def _():
            pair = 1 - 2 * odd_y
            for ref, sign_x in ((cup_ref, 1), (cdown_ref, -1)):
                for side, sign_y in enumerate((pair, -pair)):
                    for k, (c, d) in enumerate(face_x):
                        y = cells_y - reach(c) if sign_y > 0 else 0
                        where = pl.ds(ext.row(at(cells_x, sign_x, d), y), reach(c))
                        ref[side, pl.ds(corner_start[k], reach(c)), :] = held(
                            mirrored(c, sign_x, sign_y), where
                        )
                    for k, c in enumerate(ends_x):
                        row = ext.row(at(cells_x, sign_x, HALO - 1), at(cells_y, sign_y, 1))
                        ref[side, pl.ds(ENDS_START + k, 1), :] = held(
                            mirrored(c, 1, sign_y), pl.ds(row, 1)
                        )
            for ref, sign in ((ya_ref, pair), (yb_ref, -pair)):
                for k, (c, d) in enumerate(face_y):
                    ref[pl.ds(k * cells_x, cells_x), :] = held(
                        mirrored(c, 1, sign), line_y(at(cells_y, sign, d))(0)
                    )
                for side, sign_x in enumerate((1, -1)):
                    for k, c in enumerate(ends_y):
                        row = ext.row(at(cells_x, sign_x, 1), at(cells_y, sign, HALO - 1))
                        to = len(face_y) * cells_x + side * len(ends_y) + k
                        ref[pl.ds(to, 1), :] = held(mirrored(c, sign_x, 1), pl.ds(row, 1))

    for ref, sign in ((up_ref, 1), (down_ref, -1)):
        for k, (c, d) in enumerate(face_x):
            where = pl.ds(ext.row(at(cells_x, sign, d), ext.inner(c)), ext.inner_rows)
            ref[pl.ds(k * ext.inner_rows, ext.inner_rows), :] = held(mirrored(c, sign, 1), where)


def forward_kernel(cup_ref, cdown_ref, pair_ref, far_ref):
    for side, ref in enumerate((pair_ref, far_ref)):
        ref[0] = cup_ref[side]
        ref[1] = cdown_ref[side]


def beyond(cells, sign, d):
    return cells - 1 + d if sign > 0 else -d


def putter(one_ref, kinds_ref):
    def put(c, where, value):
        if c == KIND:
            kinds_ref[where, :] = value
        else:
            one_ref[c, where, :] = value

    return put


def put_sums(ext, put, x, y, count, values, carry):
    total, across, along, solute = values
    rows = pl.ds(ext.row(x, y), count)
    moved = across if carry > 0 else -across
    put(0, rows, total - moved)
    put(all_velocity.index((0, carry, 0)), pl.ds(ext.row(x, y - carry), count), moved)
    put(all_velocity.index((0, 0, 1)), rows, along)
    put(FLOW, rows, solute)


def put_corner(ext, put, ref, sign_x, sign_y, origin):
    for k, (c, d) in enumerate(face_x):
        x = beyond(ext.cells_x, sign_x, d)
        y = origin + (ext.cells_y - reach(c) if sign_y > 0 else 0)
        if c <= KIND:
            put(
                mirrored(c, -sign_x, sign_y),
                pl.ds(ext.row(x, y), reach(c)),
                ref[pl.ds(corner_start[k], reach(c)), :],
            )
        elif k == FACE_X_SUMS:
            for n in range(reach(c)):
                values = [ref[pl.ds(corner_start[k + i] + n, 1), :] for i in range(4)]
                carry = 1 if y + n < 0 or y + n == ext.cells_y - 1 else -1
                put_sums(ext, put, x, y + n, 1, values, carry)
    x = beyond(ext.cells_x, sign_x, HALO - 1)
    y = origin + (ext.cells_y - 1 if sign_y > 0 else 0)
    for k, c in enumerate(ends_x):
        put(mirrored(c, 1, sign_y), pl.ds(ext.row(x, y), 1), ref[pl.ds(ENDS_START + k, 1), :])


def put_inner(ext, put, ref, sign_x):
    for k, (c, d) in enumerate(face_x):
        x, y = beyond(ext.cells_x, sign_x, d), ext.inner(c)
        rows = [pl.ds((k + i) * ext.inner_rows, ext.inner_rows) for i in range(4)]
        if c <= KIND:
            put(
                mirrored(c, -sign_x, 1),
                pl.ds(ext.row(x, y), ext.inner_rows),
                ref[rows[0], :],
            )
        elif k == FACE_X_SUMS:
            put_sums(ext, put, x, y, ext.inner_rows, [ref[r, :] for r in rows], -1)


def put_face_y(ext, put, ref, sign_y):
    cells = ext.cells_x

    def line(x, y, count=cells):
        return pl.ds(ext.row(x, y), count, stride=ext.pitch)

    for k, (c, d) in enumerate(face_y):
        if c <= KIND:
            put(
                mirrored(c, 1, -sign_y),
                line(0, beyond(ext.cells_y, sign_y, d)),
                ref[pl.ds(k * cells, cells), :],
            )
    y = beyond(ext.cells_y, sign_y, HALO - 1)
    total, across, along, solute = (
        ref[pl.ds((FACE_Y_SUMS + i) * cells, cells), :] for i in range(4)
    )
    last = lax.broadcasted_iota(jnp.int32, across.shape, 0) == cells - 1
    back = all_velocity.index((-1, 0, 0))
    forth = all_velocity.index((1, 0, 0))
    put(0, line(0, y), total - jnp.where(last, across, -across))
    put(back, line(1, y, cells - 1), -across[: cells - 1])
    put(forth, pl.ds(ext.row(cells - 2, y), 1), across[cells - 1 :])
    put(all_velocity.index((0, 0, 1)), line(0, y), along)
    put(FLOW, line(0, y), solute)
    for side, sign_x in enumerate((1, -1)):
        x = cells - 1 if sign_x > 0 else 0
        for k, c in enumerate(ends_y):
            start = len(face_y) * cells + side * len(ends_y) + k
            put(mirrored(c, sign_x, 1), pl.ds(ext.row(x, y), 1), ref[pl.ds(start, 1), :])


def insert_kernel(ext, odd_ref, _, __, up_ref, down_ref, cup_ref, cdown_ref, ya_ref,
                  one_ref, kinds_ref):
    put = putter(one_ref, kinds_ref)
    put_inner(ext, put, up_ref, -1)
    put_inner(ext, put, down_ref, 1)
    for odd_y in (0, 1):

        @pl.when(odd_ref[0] == odd_y)
        def _():
            pair = 1 - 2 * odd_y
            for ref, sign_x in ((cup_ref, -1), (cdown_ref, 1)):
                for side, sign_y in enumerate((pair, -pair)):
                    put_corner(ext, put, ref.at[side], sign_x, sign_y, 0)
            put_face_y(ext, put, ya_ref.at[1 - odd_y], pair)


def last_kernel(ext, odd_ref, _, __, yb_ref, pair_ref, far_ref, density_ref, momentum_ref,
                concentration_ref, one_ref, kinds_ref, two_ref):
    cells_x, cells_y, pitch, row = ext.cells_x, ext.cells_y, ext.pitch, ext.row
    depth = one_ref.shape[-1]
    put = putter(one_ref, kinds_ref)

    for odd_y in (0, 1):

        @pl.when(odd_ref[0] == odd_y)
        def _():
            pair = 1 - 2 * odd_y
            put_face_y(ext, put, yb_ref, -pair)
            for ref, sign_y in ((pair_ref, pair), (far_ref, -pair)):
                for side, sign_x in enumerate((-1, 1)):
                    put_corner(ext, put, ref.at[side], sign_x, -sign_y, sign_y * cells_y)

    lane = lax.broadcasted_iota(jnp.int32, (8, depth), 1)

    def arriving(ref, c, start, size):
        cx, cy, _ = all_velocity[c]
        return ref[c, pl.ds(start - (cx * pitch + cy), size), :]

    def advance(source, target, width):
        first = row(-width, -width)
        for start in range(first, row(cells_x - 1 + width, cells_y - 1 + width) + 1, 8):
            values = [arriving(source, c, start, 8) for c in range(COUNT)]
            values = collide(values[:FLOW], values[FLOW:], kinds_ref[pl.ds(start, 8), :])

            def store(c, value):
                target[c, pl.ds(start, 8), :] = value

            if width > 1:
                store_shifted(values, lane, store)
            else:
                for c in range(COUNT):
                    store(c, values[c])

    source, target = one_ref, two_ref
    for width in range(HALO - 1, 0, -1):
        advance(source, target, width)
        source, target = target, source

    def summed(values, weights):
        total = None
        for along_z in (0, 1, -1):
            part = None
            for c, weight in weights.items():
                if weight == 0 or all_velocity[c][2] != along_z:
                    continue
                if part is None:
                    part = values[c] if weight > 0 else -values[c]
                else:
                    part = part + values[c] if weight > 0 else part - values[c]
            if part is not None:
                part = depth_shift(part, along_z, lane)
                total = part if total is None else total + part
        return total

    flow = range(FLOW)
    for x in range(cells_x):
        values = [arriving(source, c, row(x, 0), cells_y) for c in range(COUNT)]
        density_ref[x] = summed(values, {c: 1 for c in flow})
        for axis in range(3):
            momentum_ref[axis, x] = summed(values, {c: flow_velocity[c][axis] for c in flow})
        concentration_ref[x] = summed(values, {c: 1 for c in range(FLOW, COUNT)})


def higher(i, count):
    return (i + 1) % count


def lower(i, count):
    return (i - 1) % count


def near(i, count):
    return i ^ 1


def across(i, count):
    return (i + 1) % count if i % 2 else (i - 1) % count


def swapped(block, count_x, count_y, move_x, move_y):
    pairs = []
    for i in range(count_x):
        for j in range(count_y):
            to_x = move_x(i, count_x) if move_x else i
            to_y = move_y(j, count_y) if move_y else j
            pairs.append((i * count_y + j, to_x * count_y + to_y))
    return lax.ppermute(block, ("gx", "gy"), pairs)


def solution(mesh):
    count_x, count_y = mesh.shape["gx"], mesh.shape["gy"]
    assert count_y % 2 == 0

    def local(flow, solute, kind):
        _, cells_x, cells_y, depth = flow.shape
        f32 = jnp.float32
        shape = lambda *dims: jax.ShapeDtypeStruct(dims, f32)
        smem = pl.BlockSpec(memory_space=pltpu.SMEM)
        vmem = pl.BlockSpec(memory_space=pltpu.VMEM)
        hbm = pl.BlockSpec(memory_space=pltpu.HBM)
        params = pltpu.CompilerParams(vmem_limit_bytes=40 * 1024 * 1024)
        odd = jnp.reshape(lax.axis_index("gy") % 2, (1,)).astype(jnp.int32)
        ext = Extended(cells_x, cells_y)
        group = math.gcd(cells_x, 4)
        flow, solute, kind = (
            pltpu.with_memory_space_constraint(a, pltpu.HBM) for a in (flow, solute, kind)
        )
        post, kinds, up, down, ya, yb, cup, cdown = pl.pallas_call(
            functools.partial(first_kernel, ext, group),
            out_shape=[
                shape(COUNT, ext.rows, depth),
                shape(ext.rows, depth),
                shape(len(face_x) * ext.inner_rows, depth),
                shape(len(face_x) * ext.inner_rows, depth),
                shape(ext.face_y_rows, depth),
                shape(ext.face_y_rows, depth),
                shape(2, CORNER_ROWS, depth),
                shape(2, CORNER_ROWS, depth),
            ],
            in_specs=[smem, hbm, hbm, hbm],
            out_specs=[vmem] * 8,
            scratch_shapes=[
                pltpu.VMEM(flow.shape, f32),
                pltpu.VMEM(solute.shape, f32),
                pltpu.VMEM(kind.shape, kind.dtype),
                pltpu.VMEM((8, ext.rows, depth), f32),
                pltpu.SemaphoreType.DMA((cells_x // group, 3)),
            ],
            compiler_params=params,
        )(odd, flow, solute, kind)
        move = functools.partial(swapped, count_x=count_x, count_y=count_y)
        cup = move(cup, move_x=higher, move_y=None)
        cdown = move(cdown, move_x=lower, move_y=None)
        yb = move(yb, move_x=None, move_y=across)
        up = move(up, move_x=higher, move_y=None)
        down = move(down, move_x=lower, move_y=None)
        pair, far = pl.pallas_call(
            forward_kernel,
            out_shape=[shape(2, CORNER_ROWS, depth)] * 2,
            in_specs=[vmem, vmem],
            out_specs=[vmem, vmem],
            compiler_params=params,
        )(cup, cdown)
        far = move(far, move_x=None, move_y=across)
        pair = move(pair, move_x=None, move_y=near)
        ya = lax.all_gather(ya, "gy", axis_index_groups=[[j, j + 1] for j in range(0, count_y, 2)])
        post, kinds = pl.pallas_call(
            functools.partial(insert_kernel, ext),
            out_shape=[shape(COUNT, ext.rows, depth), shape(ext.rows, depth)],
            in_specs=[smem] + [vmem] * 7,
            out_specs=[vmem] * 2,
            input_output_aliases={1: 0, 2: 1},
            compiler_params=params,
        )(odd, post, kinds, up, down, cup, cdown, ya)
        density, momentum, concentration, _, _ = pl.pallas_call(
            functools.partial(last_kernel, ext),
            out_shape=[
                shape(cells_x, cells_y, depth),
                shape(3, cells_x, cells_y, depth),
                shape(cells_x, cells_y, depth),
                shape(COUNT, ext.rows, depth),
                shape(ext.rows, depth),
            ],
            in_specs=[smem] + [vmem] * 5,
            out_specs=[vmem] * 5,
            scratch_shapes=[pltpu.VMEM((COUNT, ext.rows, depth), f32)],
            input_output_aliases={1: 3, 2: 4},
            compiler_params=params,
        )(odd, post, kinds, yb, pair, far)
        return density, momentum, concentration

    placed = (P(None, "gx", "gy", None), P(None, "gx", "gy", None), P("gx", "gy", None))
    return jax.shard_map(
        local,
        mesh=mesh,
        in_specs=placed,
        out_specs=(P("gx", "gy", None), P(None, "gx", "gy", None), P("gx", "gy", None)),
        check_vma=False,
    )
```

```python
import functools
import math

import jax
import jax.numpy as jnp
from jax import lax
from jax.experimental import pallas as pl
from jax.experimental.pallas import tpu as pltpu
from jax.sharding import PartitionSpec as P

STEPS = 3
HALO = STEPS

flow_velocity = [
    (0, 0, 0),
    (1, 0, 0),
    (-1, 0, 0),
    (0, 1, 0),
    (0, -1, 0),
    (0, 0, 1),
    (0, 0, -1),
    (1, 1, 0),
    (-1, -1, 0),
    (1, -1, 0),
    (-1, 1, 0),
    (1, 0, 1),
    (-1, 0, -1),
    (1, 0, -1),
    (-1, 0, 1),
    (0, 1, 1),
    (0, -1, -1),
    (0, 1, -1),
    (0, -1, 1),
]
FLOW = len(flow_velocity)
all_velocity = flow_velocity + flow_velocity[:7]
COUNT = len(all_velocity)
KIND = COUNT
SUMS = {0: range(COUNT + 1, COUNT + 5), 1: range(COUNT + 5, COUNT + 9)}
flow_plus = 1.25
flow_minus = 1.0 / 1.125
solute_plus = 1.0 / 1.75
solute_minus = 1.0 / 0.7
inlet_density = 1.05
outlet_density = 0.95
inlet_solute = 1.0


def mirrored(channel, sign_x, sign_y):
    if channel >= KIND:
        return channel
    cx, cy, cz = all_velocity[channel]
    wanted = (cx * sign_x, cy * sign_y, cz)
    if channel < FLOW:
        return flow_velocity.index(wanted)
    return FLOW + flow_velocity[:7].index(wanted)


def moving(axis, toward):
    return [c for c in range(COUNT) if all_velocity[c][axis] == toward]


def needed(axis):
    outer = HALO - 1
    return (
        [(c, d) for d in range(1, outer) for c in range(COUNT)]
        + [(c, d) for d in (outer, HALO) for c in moving(axis, 1)]
        + [(c, outer) for c in SUMS[axis]]
        + [(KIND, d) for d in range(1, HALO)]
    )


face_x = needed(0)
face_y = needed(1)
ends_x = [c for c in moving(0, 0) if all_velocity[c][1] == 1]
ends_y = [c for c in moving(1, 0) if all_velocity[c][0] == 1]


def reach(channel):
    return HALO - 1 + (all_velocity[channel][1] if channel < COUNT else 0)


corner_start = [sum(reach(c) for c, _ in face_x[:k]) for k in range(len(face_x) + 1)]
ENDS_START = corner_start[-1]
CORNER_ROWS = -(-(ENDS_START + len(ends_x)) // 8) * 8
FACE_X_SUMS = face_x.index((SUMS[0][0], HALO - 1))
FACE_Y_SUMS = face_y.index((SUMS[1][0], HALO - 1))


def collide(flow, solute, kind):
    pore = kind == 0.0
    solid = kind == 1.0
    inlet = kind == 2.0
    zero = jnp.zeros_like(kind)
    pairs = range(1, FLOW, 2)
    total = {i: flow[i] + flow[i + 1] for i in pairs}
    gap = {i: flow[i] - flow[i + 1] for i in pairs}
    density = (flow[0] + total[1] + total[3]) + (total[5] + total[7] + total[9])
    density = density + ((total[11] + total[13]) + (total[15] + total[17]))
    mom_x = (gap[1] + gap[7]) + (gap[9] + gap[11]) + gap[13]
    mom_y = (gap[3] + gap[7]) + (gap[15] - gap[9]) + gap[17]
    mom_z = (gap[5] + gap[11]) + (gap[15] - gap[13]) - gap[17]
    square = mom_x * mom_x + mom_y * mom_y + mom_z * mom_z
    wall = jnp.where(solid, 0.5, zero)
    even = jnp.where(pore, (1.0 - flow_plus) / 2.0, wall)
    odd = jnp.where(pore, (1.0 - flow_minus) / 2.0, -wall)
    border = jnp.where(inlet, inlet_density, jnp.where(solid, 0.0, outlet_density))
    base = jnp.where(pore, flow_plus * density - (1.5 * flow_plus) * square, border)
    base_18 = base * (1.0 / 18.0)
    base_36 = base * (1.0 / 36.0)
    scale = math.sqrt(4.5 * flow_plus / 36.0)
    held = jnp.where(pore, scale, zero)
    vel = (mom_x * held, mom_y * held, mom_z * held)
    along = 3.0 * flow_minus / (36.0 * scale)
    out = [None] * COUNT
    out[0] = (even + even) * flow[0] + base * (1.0 / 3.0)
    for i in pairs:
        cx, cy, cz = flow_velocity[i]
        parts = [(c, v) for c, v in zip((cx, cy, cz), vel) if c != 0]
        if len(parts) == 1:
            t = parts[0][1]
            a = even * total[i] + (base_18 + 2.0 * (t * t))
            b = odd * gap[i] + (2.0 * along) * t
        else:
            t = parts[0][1] + parts[1][1] if parts[1][0] > 0 else parts[0][1] - parts[1][1]
            a = even * total[i] + (base_36 + t * t)
            b = odd * gap[i] + along * t
        out[i] = a + b
        out[i + 1] = a - b
    total = {i: solute[i] + solute[i + 1] for i in (1, 3, 5)}
    gap = {i: solute[i] - solute[i + 1] for i in (1, 3, 5)}
    concentration = (solute[0] + total[1]) + (total[3] + total[5])
    even = jnp.where(pore, (1.0 - solute_plus) / 2.0, wall)
    odd = jnp.where(pore, (1.0 - solute_minus) / 2.0, -wall)
    border = jnp.where(inlet, inlet_solute, zero)
    base = jnp.where(pore, solute_plus * concentration, border) * 0.125
    drift = concentration * (0.5 * solute_minus / scale)
    out[FLOW] = (even + even) * solute[0] + (base + base)
    for i, t in zip((1, 3, 5), vel):
        a = even * total[i] + base
        b = odd * gap[i] + drift * t
        out[FLOW + i] = a + b
        out[FLOW + i + 1] = a - b
    return out


def depth_shift(section, along_z, lane):
    depth = section.shape[-1]
    if along_z == 1:
        return jnp.where(lane == 0, 0.0, pltpu.roll(section, 1, section.ndim - 1))
    if along_z == -1:
        return jnp.where(lane == depth - 1, 0.0, pltpu.roll(section, depth - 1, section.ndim - 1))
    return section


def store_shifted(values, lane, store):
    for c in range(COUNT):
        store(c, depth_shift(values[c], all_velocity[c][2], lane))


class Extended:
    def __init__(self, cells_x, cells_y):
        self.cells_x, self.cells_y = cells_x, cells_y
        self.pitch = cells_y + 2 * HALO
        self.rows = -(-((cells_x + 2 * HALO) * self.pitch + 16) // 8) * 8

        self.face_y_rows = len(face_y) * cells_x + 2 * len(ends_y)
        self.inner_rows = cells_y - 2 * (HALO - 1)

    def row(self, x, y):
        return (x + HALO) * self.pitch + y + HALO

    def inner(self, channel):
        return HALO - 1 - (all_velocity[channel][1] if channel < COUNT else 0)


def first_kernel(ext, group, odd_ref, flow_hbm, solute_hbm, kind_hbm, post_ref, kinds_ref,
                 up_ref, down_ref, ya_ref, yb_ref, cup_ref, cdown_ref,
                 flow_ref, solute_ref, kind_ref, sums_ref, sems):
    cells_x, cells_y = ext.cells_x, ext.cells_y
    depth = kind_ref.shape[-1]
    lane = lax.broadcasted_iota(jnp.int32, (cells_y, depth), 1)
    copies = []
    for g in range(cells_x // group):
        planes = pl.ds(g * group, group)
        copies.append([
            pltpu.make_async_copy(kind_hbm.at[planes], kind_ref.at[planes], sems.at[g, 0]),
            pltpu.make_async_copy(flow_hbm.at[:, planes], flow_ref.at[:, planes], sems.at[g, 1]),
            pltpu.make_async_copy(
                solute_hbm.at[:, planes], solute_ref.at[:, planes], sems.at[g, 2]
            ),
        ])
        for copy in copies[-1]:
            copy.start()

    for x in range(cells_x):
        if x % group == 0:
            for copy in copies[x // group]:
                copy.wait()
        kind = kind_ref[x].astype(jnp.float32)
        rows = pl.ds(ext.row(x, 0), cells_y)
        kinds_ref[rows, :] = kind
        values = collide(
            [flow_ref[c, x] for c in range(FLOW)],
            [solute_ref[c, x] for c in range(COUNT - FLOW)],
            kind,
        )

        def store(c, value):
            post_ref[c, rows, :] = value

        store_shifted(values, lane, store)

    def sums(axis, where):
        across = 1 - axis
        cells = (cells_x, cells_y)[across]
        place = lax.broadcasted_iota(jnp.int32, (cells, depth), 0)
        parts = {}
        for move in (0, 1, -1):
            total = along = solute = None
            for c in moving(axis, 0):
                if all_velocity[c][across] != move:
                    continue
                value = post_ref[c, where(-move), :]
                if c >= FLOW:
                    solute = value if solute is None else solute + value
                    continue
                total = value if total is None else total + value
                cz = all_velocity[c][2]
                if cz != 0:
                    signed = value if cz > 0 else -value
                    along = signed if along is None else along + signed
            parts[move] = [total, along, solute]
            if move != 0:
                inside = place != (0 if move > 0 else cells - 1)
                parts[move] = [jnp.where(inside, p, 0.0) for p in parts[move]]
        total, along, solute = (parts[0][n] + parts[1][n] + parts[-1][n] for n in range(3))
        for c, value in zip(
            SUMS[axis], (total - along, parts[1][0] - parts[-1][0], along, solute)
        ):
            sums_ref[c - SUMS[0][0], where(0), :] = value

    def at(cells, sign, d):
        return cells - d if sign > 0 else d - 1

    def line_x(x):
        return lambda y: pl.ds(ext.row(x, y), cells_y)

    def line_y(y):
        return lambda x: pl.ds(ext.row(x, y), cells_x, stride=ext.pitch)

    zero = jnp.zeros((8, depth), jnp.float32)
    zeros = jnp.zeros((cells_x, depth), jnp.float32)
    for sign in (1, -1):
        sums(0, line_x(at(cells_x, sign, HALO - 1)))
        sums(1, line_y(at(cells_y, sign, HALO - 1)))
        for c in moving(0, 0):
            first = ext.row(beyond(cells_x, sign, HALO - 1), -HALO)
            for start in [*range(0, ext.pitch - 8, 8), ext.pitch - 8]:
                post_ref[c, pl.ds(first + start, 8), :] = zero
        for c in moving(1, 0):
            post_ref[c, line_y(beyond(cells_y, sign, HALO - 1))(0), :] = zeros

    def held(c, where):
        if c > KIND:
            return sums_ref[c - SUMS[0][0], where, :]
        return kinds_ref[where, :] if c == KIND else post_ref[c, where, :]

    for odd_y in (0, 1):

        @pl.when(odd_ref[0] == odd_y)
        def _():
            pair = 1 - 2 * odd_y
            for ref, sign_x in ((cup_ref, 1), (cdown_ref, -1)):
                for side, sign_y in enumerate((pair, -pair)):
                    for k, (c, d) in enumerate(face_x):
                        y = cells_y - reach(c) if sign_y > 0 else 0
                        where = pl.ds(ext.row(at(cells_x, sign_x, d), y), reach(c))
                        ref[side, pl.ds(corner_start[k], reach(c)), :] = held(
                            mirrored(c, sign_x, sign_y), where
                        )
                    for k, c in enumerate(ends_x):
                        row = ext.row(at(cells_x, sign_x, HALO - 1), at(cells_y, sign_y, 1))
                        ref[side, pl.ds(ENDS_START + k, 1), :] = held(
                            mirrored(c, 1, sign_y), pl.ds(row, 1)
                        )
            for ref, sign in ((ya_ref, pair), (yb_ref, -pair)):
                for k, (c, d) in enumerate(face_y):
                    ref[pl.ds(k * cells_x, cells_x), :] = held(
                        mirrored(c, 1, sign), line_y(at(cells_y, sign, d))(0)
                    )
                for side, sign_x in enumerate((1, -1)):
                    for k, c in enumerate(ends_y):
                        row = ext.row(at(cells_x, sign_x, 1), at(cells_y, sign, HALO - 1))
                        to = len(face_y) * cells_x + side * len(ends_y) + k
                        ref[pl.ds(to, 1), :] = held(mirrored(c, sign_x, 1), pl.ds(row, 1))

    for ref, sign in ((up_ref, 1), (down_ref, -1)):
        for k, (c, d) in enumerate(face_x):
            where = pl.ds(ext.row(at(cells_x, sign, d), ext.inner(c)), ext.inner_rows)
            ref[pl.ds(k * ext.inner_rows, ext.inner_rows), :] = held(mirrored(c, sign, 1), where)


def forward_kernel(cup_ref, cdown_ref, pair_ref, far_ref):
    for side, ref in enumerate((pair_ref, far_ref)):
        ref[0] = cup_ref[side]
        ref[1] = cdown_ref[side]


def beyond(cells, sign, d):
    return cells - 1 + d if sign > 0 else -d


def putter(one_ref, kinds_ref):
    def put(c, where, value):
        if c == KIND:
            kinds_ref[where, :] = value
        else:
            one_ref[c, where, :] = value

    return put


def put_sums(ext, put, x, y, count, values, carry):
    total, across, along, solute = values
    rows = pl.ds(ext.row(x, y), count)
    moved = across if carry > 0 else -across
    put(0, rows, total - moved)
    put(all_velocity.index((0, carry, 0)), pl.ds(ext.row(x, y - carry), count), moved)
    put(all_velocity.index((0, 0, 1)), rows, along)
    put(FLOW, rows, solute)


def put_corner(ext, put, ref, sign_x, sign_y, origin):
    for k, (c, d) in enumerate(face_x):
        x = beyond(ext.cells_x, sign_x, d)
        y = origin + (ext.cells_y - reach(c) if sign_y > 0 else 0)
        if c <= KIND:
            put(
                mirrored(c, -sign_x, sign_y),
                pl.ds(ext.row(x, y), reach(c)),
                ref[pl.ds(corner_start[k], reach(c)), :],
            )
        elif k == FACE_X_SUMS:
            for n in range(reach(c)):
                values = [ref[pl.ds(corner_start[k + i] + n, 1), :] for i in range(4)]
                carry = 1 if y + n < 0 or y + n == ext.cells_y - 1 else -1
                put_sums(ext, put, x, y + n, 1, values, carry)
    x = beyond(ext.cells_x, sign_x, HALO - 1)
    y = origin + (ext.cells_y - 1 if sign_y > 0 else 0)
    for k, c in enumerate(ends_x):
        put(mirrored(c, 1, sign_y), pl.ds(ext.row(x, y), 1), ref[pl.ds(ENDS_START + k, 1), :])


def put_inner(ext, put, ref, sign_x):
    for k, (c, d) in enumerate(face_x):
        x, y = beyond(ext.cells_x, sign_x, d), ext.inner(c)
        rows = [pl.ds((k + i) * ext.inner_rows, ext.inner_rows) for i in range(4)]
        if c <= KIND:
            put(
                mirrored(c, -sign_x, 1),
                pl.ds(ext.row(x, y), ext.inner_rows),
                ref[rows[0], :],
            )
        elif k == FACE_X_SUMS:
            put_sums(ext, put, x, y, ext.inner_rows, [ref[r, :] for r in rows], -1)


def put_face_y(ext, put, ref, sign_y):
    cells = ext.cells_x

    def line(x, y, count=cells):
        return pl.ds(ext.row(x, y), count, stride=ext.pitch)

    for k, (c, d) in enumerate(face_y):
        if c <= KIND:
            put(
                mirrored(c, 1, -sign_y),
                line(0, beyond(ext.cells_y, sign_y, d)),
                ref[pl.ds(k * cells, cells), :],
            )
    y = beyond(ext.cells_y, sign_y, HALO - 1)
    total, across, along, solute = (
        ref[pl.ds((FACE_Y_SUMS + i) * cells, cells), :] for i in range(4)
    )
    last = lax.broadcasted_iota(jnp.int32, across.shape, 0) == cells - 1
    back = all_velocity.index((-1, 0, 0))
    forth = all_velocity.index((1, 0, 0))
    put(0, line(0, y), total - jnp.where(last, across, -across))
    put(back, line(1, y, cells - 1), -across[: cells - 1])
    put(forth, pl.ds(ext.row(cells - 2, y), 1), across[cells - 1 :])
    put(all_velocity.index((0, 0, 1)), line(0, y), along)
    put(FLOW, line(0, y), solute)
    for side, sign_x in enumerate((1, -1)):
        x = cells - 1 if sign_x > 0 else 0
        for k, c in enumerate(ends_y):
            start = len(face_y) * cells + side * len(ends_y) + k
            put(mirrored(c, sign_x, 1), pl.ds(ext.row(x, y), 1), ref[pl.ds(start, 1), :])


def insert_kernel(ext, odd_ref, _, __, up_ref, down_ref, cup_ref, cdown_ref, ya_ref,
                  one_ref, kinds_ref):
    put = putter(one_ref, kinds_ref)
    put_inner(ext, put, up_ref, -1)
    put_inner(ext, put, down_ref, 1)
    for odd_y in (0, 1):

        @pl.when(odd_ref[0] == odd_y)
        def _():
            pair = 1 - 2 * odd_y
            for ref, sign_x in ((cup_ref, -1), (cdown_ref, 1)):
                for side, sign_y in enumerate((pair, -pair)):
                    put_corner(ext, put, ref.at[side], sign_x, sign_y, 0)
            put_face_y(ext, put, ya_ref.at[1 - odd_y], pair)


def arriving(ext, ref, c, start, count):
    cx, cy, _ = all_velocity[c]
    return ref[c, pl.ds(start - (cx * ext.pitch + cy), count), :]


def advance(ext, source, target, kinds_ref, first, shifted):
    rows = pl.ds(first, 8)
    values = [arriving(ext, source, c, first, 8) for c in range(COUNT)]
    values = collide(values[:FLOW], values[FLOW:], kinds_ref[rows, :])
    lane = lax.broadcasted_iota(jnp.int32, values[0].shape, 1)

    def store(c, value):
        target[c, rows, :] = value

    if shifted:
        store_shifted(values, lane, store)
    else:
        for c in range(COUNT):
            store(c, values[c])


def finish(ext, source, x, density_ref, momentum_ref, concentration_ref):
    values = [arriving(ext, source, c, ext.row(x, 0), ext.cells_y) for c in range(COUNT)]
    lane = lax.broadcasted_iota(jnp.int32, values[0].shape, 1)

    def summed(weights):
        total = None
        for along_z in (0, 1, -1):
            part = None
            for c, weight in weights.items():
                if weight == 0 or all_velocity[c][2] != along_z:
                    continue
                if part is None:
                    part = values[c] if weight > 0 else -values[c]
                else:
                    part = part + values[c] if weight > 0 else part - values[c]
            if part is not None:
                part = depth_shift(part, along_z, lane)
                total = part if total is None else total + part
        return total

    density_ref[x] = summed({c: 1 for c in range(FLOW)})
    for axis in range(3):
        momentum_ref[axis, x] = summed({c: flow_velocity[c][axis] for c in range(FLOW)})
    concentration_ref[x] = summed({c: 1 for c in range(FLOW, COUNT)})


def middle_kernel(ext, odd_ref, _, __, yb_ref, pair_ref, one_ref, kinds_ref, two_ref, three_ref,
                  density_ref, momentum_ref, concentration_ref):
    put = putter(one_ref, kinds_ref)
    for odd_y in (0, 1):

        @pl.when(odd_ref[0] == odd_y)
        def _():
            pair = 1 - 2 * odd_y
            put_face_y(ext, put, yb_ref, -pair)
            for side, sign_x in enumerate((-1, 1)):
                put_corner(ext, put, pair_ref.at[side], sign_x, -pair, pair * ext.cells_y)

    for source, target, width in ((one_ref, two_ref, 2), (two_ref, three_ref, 1)):
        end = ext.row(ext.cells_x - 1 + width, ext.cells_y - 1 + width)
        for first in range(ext.row(-width, -width), end + 1, 8):
            advance(ext, source, target, kinds_ref, first, width > 1)
    for x in range(ext.cells_x):
        finish(ext, three_ref, x, density_ref, momentum_ref, concentration_ref)


def last_kernel(ext, odd_ref, _, __, ___, ____, far_ref, early_density_ref, early_momentum_ref,
                early_concentration_ref, density_ref, momentum_ref, concentration_ref,
                one_ref, kinds_ref, two_ref, three_ref):
    cells_x, cells_y = ext.cells_x, ext.cells_y
    put = putter(one_ref, kinds_ref)
    for x in range(HALO, cells_x - HALO):
        density_ref[x] = early_density_ref[x]
        for axis in range(3):
            momentum_ref[axis, x] = early_momentum_ref[axis, x]
        concentration_ref[x] = early_concentration_ref[x]
    for odd_y in (0, 1):

        @pl.when(odd_ref[0] == odd_y)
        def _():
            far = 2 * odd_y - 1
            for side, sign_x in enumerate((-1, 1)):
                put_corner(ext, put, far_ref.at[side], sign_x, -far, far * cells_y)
            for source, target, width in ((one_ref, two_ref, 2), (two_ref, three_ref, 1)):
                y = cells_y + width - 8 if far > 0 else -width
                for k in range(HALO):
                    for x in (k - width, cells_x - 1 + width - k):
                        advance(ext, source, target, kinds_ref, ext.row(x, y), width > 1)

    for k in range(HALO):
        for x in (k, cells_x - 1 - k):
            finish(ext, three_ref, x, density_ref, momentum_ref, concentration_ref)


def higher(i, count):
    return (i + 1) % count


def lower(i, count):
    return (i - 1) % count


def near(i, count):
    return i ^ 1


def across(i, count):
    return (i + 1) % count if i % 2 else (i - 1) % count


def swapped(block, count_x, count_y, move_x, move_y):
    pairs = []
    for i in range(count_x):
        for j in range(count_y):
            to_x = move_x(i, count_x) if move_x else i
            to_y = move_y(j, count_y) if move_y else j
            pairs.append((i * count_y + j, to_x * count_y + to_y))
    return lax.ppermute(block, ("gx", "gy"), pairs)


def solution(mesh):
    count_x, count_y = mesh.shape["gx"], mesh.shape["gy"]
    assert count_y % 2 == 0

    def local(flow, solute, kind):
        _, cells_x, cells_y, depth = flow.shape
        f32 = jnp.float32
        shape = lambda *dims: jax.ShapeDtypeStruct(dims, f32)
        smem = pl.BlockSpec(memory_space=pltpu.SMEM)
        vmem = pl.BlockSpec(memory_space=pltpu.VMEM)
        hbm = pl.BlockSpec(memory_space=pltpu.HBM)
        params = pltpu.CompilerParams(vmem_limit_bytes=16 * 1024 * 1024)
        odd = jnp.reshape(lax.axis_index("gy") % 2, (1,)).astype(jnp.int32)
        ext = Extended(cells_x, cells_y)
        group = math.gcd(cells_x, 4)
        flow, solute, kind = (
            pltpu.with_memory_space_constraint(a, pltpu.HBM) for a in (flow, solute, kind)
        )
        post, kinds, up, down, ya, yb, cup, cdown = pl.pallas_call(
            functools.partial(first_kernel, ext, group),
            out_shape=[
                shape(COUNT, ext.rows, depth),
                shape(ext.rows, depth),
                shape(len(face_x) * ext.inner_rows, depth),
                shape(len(face_x) * ext.inner_rows, depth),
                shape(ext.face_y_rows, depth),
                shape(ext.face_y_rows, depth),
                shape(2, CORNER_ROWS, depth),
                shape(2, CORNER_ROWS, depth),
            ],
            in_specs=[smem, hbm, hbm, hbm],
            out_specs=[vmem] * 8,
            scratch_shapes=[
                pltpu.VMEM(flow.shape, f32),
                pltpu.VMEM(solute.shape, f32),
                pltpu.VMEM(kind.shape, kind.dtype),
                pltpu.VMEM((8, ext.rows, depth), f32),
                pltpu.SemaphoreType.DMA((cells_x // group, 3)),
            ],
            compiler_params=params,
        )(odd, flow, solute, kind)
        move = functools.partial(swapped, count_x=count_x, count_y=count_y)
        cup = move(cup, move_x=higher, move_y=None)
        cdown = move(cdown, move_x=lower, move_y=None)
        yb = move(yb, move_x=None, move_y=across)
        up = move(up, move_x=higher, move_y=None)
        down = move(down, move_x=lower, move_y=None)
        pair, far = pl.pallas_call(
            forward_kernel,
            out_shape=[shape(2, CORNER_ROWS, depth)] * 2,
            in_specs=[vmem, vmem],
            out_specs=[vmem, vmem],
            compiler_params=params,
        )(cup, cdown)
        far = move(far, move_x=None, move_y=across)
        pair = move(pair, move_x=None, move_y=near)
        ya = lax.all_gather(ya, "gy", axis_index_groups=[[j, j + 1] for j in range(0, count_y, 2)])
        post, kinds = pl.pallas_call(
            functools.partial(insert_kernel, ext),
            out_shape=[shape(COUNT, ext.rows, depth), shape(ext.rows, depth)],
            in_specs=[smem] + [vmem] * 7,
            out_specs=[vmem] * 2,
            input_output_aliases={1: 0, 2: 1},
            compiler_params=params,
        )(odd, post, kinds, up, down, cup, cdown, ya)
        moments = [
            shape(cells_x, cells_y, depth),
            shape(3, cells_x, cells_y, depth),
            shape(cells_x, cells_y, depth),
        ]
        one = shape(COUNT, ext.rows, depth)
        post, kinds, two, three, *early = pl.pallas_call(
            functools.partial(middle_kernel, ext),
            out_shape=[one, shape(ext.rows, depth), one, one] + moments,
            in_specs=[smem] + [vmem] * 4,
            out_specs=[vmem] * 7,
            input_output_aliases={1: 0, 2: 1},
            compiler_params=params,
        )(odd, post, kinds, yb, pair)
        density, momentum, concentration, *_ = pl.pallas_call(
            functools.partial(last_kernel, ext),
            out_shape=moments + [one, shape(ext.rows, depth), one, one],
            in_specs=[smem] + [vmem] * 8,
            out_specs=[vmem] * 7,
            input_output_aliases={1: 3, 2: 4, 3: 5, 4: 6},
            compiler_params=params,
        )(odd, post, kinds, two, three, far, *early)
        return density, momentum, concentration

    placed = (P(None, "gx", "gy", None), P(None, "gx", "gy", None), P("gx", "gy", None))
    return jax.shard_map(
        local,
        mesh=mesh,
        in_specs=placed,
        out_specs=(P("gx", "gy", None), P(None, "gx", "gy", None), P("gx", "gy", None)),
        check_vma=False,
    )
```

```python
import functools
import math

import jax
import jax.numpy as jnp
from jax import lax
from jax.experimental import pallas as pl
from jax.experimental.pallas import tpu as pltpu
from jax.sharding import PartitionSpec as P

STEPS = 3
HALO = STEPS

flow_velocity = [
    (0, 0, 0),
    (1, 0, 0),
    (-1, 0, 0),
    (0, 1, 0),
    (0, -1, 0),
    (0, 0, 1),
    (0, 0, -1),
    (1, 1, 0),
    (-1, -1, 0),
    (1, -1, 0),
    (-1, 1, 0),
    (1, 0, 1),
    (-1, 0, -1),
    (1, 0, -1),
    (-1, 0, 1),
    (0, 1, 1),
    (0, -1, -1),
    (0, 1, -1),
    (0, -1, 1),
]
FLOW = len(flow_velocity)
all_velocity = flow_velocity + flow_velocity[:7]
COUNT = len(all_velocity)
KIND = COUNT
SUMS = {0: range(COUNT + 1, COUNT + 5), 1: range(COUNT + 5, COUNT + 9)}
flow_plus = 1.25
flow_minus = 1.0 / 1.125
solute_plus = 1.0 / 1.75
solute_minus = 1.0 / 0.7
inlet_density = 1.05
outlet_density = 0.95
inlet_solute = 1.0


def mirrored(channel, sign_x, sign_y):
    if channel >= KIND:
        return channel
    cx, cy, cz = all_velocity[channel]
    wanted = (cx * sign_x, cy * sign_y, cz)
    if channel < FLOW:
        return flow_velocity.index(wanted)
    return FLOW + flow_velocity[:7].index(wanted)


def moving(axis, toward):
    return [c for c in range(COUNT) if all_velocity[c][axis] == toward]


def needed(axis):
    outer = HALO - 1
    return (
        [(c, d) for d in range(1, outer) for c in range(COUNT)]
        + [(c, d) for d in (outer, HALO) for c in moving(axis, 1)]
        + [(c, outer) for c in SUMS[axis]]
        + [(KIND, d) for d in range(1, HALO)]
    )


face_x = needed(0)
face_y = needed(1)
ends_x = [c for c in moving(0, 0) if all_velocity[c][1] == 1]
ends_y = [c for c in moving(1, 0) if all_velocity[c][0] == 1]


def reach(channel):
    return HALO - 1 + (all_velocity[channel][1] if channel < COUNT else 0)


corner_start = [sum(reach(c) for c, _ in face_x[:k]) for k in range(len(face_x) + 1)]
ENDS_START = corner_start[-1]
CORNER_ROWS = -(-(ENDS_START + len(ends_x)) // 8) * 8
FACE_X_SUMS = face_x.index((SUMS[0][0], HALO - 1))
FACE_Y_SUMS = face_y.index((SUMS[1][0], HALO - 1))


def collide(flow, solute, kind):
    pore = kind == 0.0
    solid = kind == 1.0
    inlet = kind == 2.0
    zero = jnp.zeros_like(kind)
    pairs = range(1, FLOW, 2)
    total = {i: flow[i] + flow[i + 1] for i in pairs}
    gap = {i: flow[i] - flow[i + 1] for i in pairs}
    density = (flow[0] + total[1] + total[3]) + (total[5] + total[7] + total[9])
    density = density + ((total[11] + total[13]) + (total[15] + total[17]))
    mom_x = (gap[1] + gap[7]) + (gap[9] + gap[11]) + gap[13]
    mom_y = (gap[3] + gap[7]) + (gap[15] - gap[9]) + gap[17]
    mom_z = (gap[5] + gap[11]) + (gap[15] - gap[13]) - gap[17]
    square = mom_x * mom_x + mom_y * mom_y + mom_z * mom_z
    wall = jnp.where(solid, 0.5, zero)
    even = jnp.where(pore, (1.0 - flow_plus) / 2.0, wall)
    odd = jnp.where(pore, (1.0 - flow_minus) / 2.0, -wall)
    border = jnp.where(inlet, inlet_density, jnp.where(solid, 0.0, outlet_density))
    base = jnp.where(pore, flow_plus * density - (1.5 * flow_plus) * square, border)
    base_18 = base * (1.0 / 18.0)
    base_36 = base * (1.0 / 36.0)
    scale = math.sqrt(4.5 * flow_plus / 36.0)
    held = jnp.where(pore, scale, zero)
    vel = (mom_x * held, mom_y * held, mom_z * held)
    along = 3.0 * flow_minus / (36.0 * scale)
    out = [None] * COUNT
    out[0] = (even + even) * flow[0] + base * (1.0 / 3.0)
    for i in pairs:
        cx, cy, cz = flow_velocity[i]
        parts = [(c, v) for c, v in zip((cx, cy, cz), vel) if c != 0]
        if len(parts) == 1:
            t = parts[0][1]
            a = even * total[i] + (base_18 + 2.0 * (t * t))
            b = odd * gap[i] + (2.0 * along) * t
        else:
            t = parts[0][1] + parts[1][1] if parts[1][0] > 0 else parts[0][1] - parts[1][1]
            a = even * total[i] + (base_36 + t * t)
            b = odd * gap[i] + along * t
        out[i] = a + b
        out[i + 1] = a - b
    total = {i: solute[i] + solute[i + 1] for i in (1, 3, 5)}
    gap = {i: solute[i] - solute[i + 1] for i in (1, 3, 5)}
    concentration = (solute[0] + total[1]) + (total[3] + total[5])
    even = jnp.where(pore, (1.0 - solute_plus) / 2.0, wall)
    odd = jnp.where(pore, (1.0 - solute_minus) / 2.0, -wall)
    border = jnp.where(inlet, inlet_solute, zero)
    base = jnp.where(pore, solute_plus * concentration, border) * 0.125
    drift = concentration * (0.5 * solute_minus / scale)
    out[FLOW] = (even + even) * solute[0] + (base + base)
    for i, t in zip((1, 3, 5), vel):
        a = even * total[i] + base
        b = odd * gap[i] + drift * t
        out[FLOW + i] = a + b
        out[FLOW + i + 1] = a - b
    return out


def depth_shift(section, along_z, lane):
    depth = section.shape[-1]
    if along_z == 1:
        return jnp.where(lane == 0, 0.0, pltpu.roll(section, 1, section.ndim - 1))
    if along_z == -1:
        return jnp.where(lane == depth - 1, 0.0, pltpu.roll(section, depth - 1, section.ndim - 1))
    return section


def store_shifted(values, lane, store):
    for c in range(COUNT):
        store(c, depth_shift(values[c], all_velocity[c][2], lane))


class Extended:
    def __init__(self, cells_x, cells_y):
        self.cells_x, self.cells_y = cells_x, cells_y
        self.pitch = cells_y + 2 * HALO
        self.rows = -(-((cells_x + 2 * HALO) * self.pitch + 16) // 8) * 8

        self.face_y_rows = len(face_y) * cells_x + 2 * len(ends_y)
        self.inner_rows = cells_y - 2 * (HALO - 1)

    def row(self, x, y):
        return (x + HALO) * self.pitch + y + HALO

    def inner(self, channel):
        return HALO - 1 - (all_velocity[channel][1] if channel < COUNT else 0)


def first_kernel(ext, group, odd_ref, flow_hbm, solute_hbm, kind_hbm, post_ref, kinds_ref,
                 up_ref, down_ref, ya_ref, yb_ref, cup_ref, cdown_ref,
                 flow_ref, solute_ref, kind_ref, sums_ref, sems):
    cells_x, cells_y = ext.cells_x, ext.cells_y
    depth = kind_ref.shape[-1]
    lane = lax.broadcasted_iota(jnp.int32, (cells_y, depth), 1)
    copies = []
    for g in range(cells_x // group):
        planes = pl.ds(g * group, group)
        copies.append([
            pltpu.make_async_copy(kind_hbm.at[planes], kind_ref.at[planes], sems.at[g, 0]),
            pltpu.make_async_copy(flow_hbm.at[:, planes], flow_ref.at[:, planes], sems.at[g, 1]),
            pltpu.make_async_copy(
                solute_hbm.at[:, planes], solute_ref.at[:, planes], sems.at[g, 2]
            ),
        ])
        for copy in copies[-1]:
            copy.start()

    for x in range(cells_x):
        if x % group == 0:
            for copy in copies[x // group]:
                copy.wait()
        kind = kind_ref[x].astype(jnp.float32)
        rows = pl.ds(ext.row(x, 0), cells_y)
        kinds_ref[rows, :] = kind
        values = collide(
            [flow_ref[c, x] for c in range(FLOW)],
            [solute_ref[c, x] for c in range(COUNT - FLOW)],
            kind,
        )

        def store(c, value):
            post_ref[c, rows, :] = value

        store_shifted(values, lane, store)

    def sums(axis, where):
        across = 1 - axis
        cells = (cells_x, cells_y)[across]
        place = lax.broadcasted_iota(jnp.int32, (cells, depth), 0)
        parts = {}
        for move in (0, 1, -1):
            total = along = solute = None
            for c in moving(axis, 0):
                if all_velocity[c][across] != move:
                    continue
                value = post_ref[c, where(-move), :]
                if c >= FLOW:
                    solute = value if solute is None else solute + value
                    continue
                total = value if total is None else total + value
                cz = all_velocity[c][2]
                if cz != 0:
                    signed = value if cz > 0 else -value
                    along = signed if along is None else along + signed
            parts[move] = [total, along, solute]
            if move != 0:
                inside = place != (0 if move > 0 else cells - 1)
                parts[move] = [jnp.where(inside, p, 0.0) for p in parts[move]]
        total, along, solute = (parts[0][n] + parts[1][n] + parts[-1][n] for n in range(3))
        for c, value in zip(
            SUMS[axis], (total - along, parts[1][0] - parts[-1][0], along, solute)
        ):
            sums_ref[c - SUMS[0][0], where(0), :] = value

    def at(cells, sign, d):
        return cells - d if sign > 0 else d - 1

    def line_x(x):
        return lambda y: pl.ds(ext.row(x, y), cells_y)

    def line_y(y):
        return lambda x: pl.ds(ext.row(x, y), cells_x, stride=ext.pitch)

    zero = jnp.zeros((8, depth), jnp.float32)
    zeros = jnp.zeros((cells_x, depth), jnp.float32)
    for sign in (1, -1):
        sums(0, line_x(at(cells_x, sign, HALO - 1)))
        sums(1, line_y(at(cells_y, sign, HALO - 1)))
        for c in moving(0, 0):
            first = ext.row(beyond(cells_x, sign, HALO - 1), -HALO)
            for start in [*range(0, ext.pitch - 8, 8), ext.pitch - 8]:
                post_ref[c, pl.ds(first + start, 8), :] = zero
        for c in moving(1, 0):
            post_ref[c, line_y(beyond(cells_y, sign, HALO - 1))(0), :] = zeros

    def held(c, where):
        if c > KIND:
            return sums_ref[c - SUMS[0][0], where, :]
        return kinds_ref[where, :] if c == KIND else post_ref[c, where, :]

    for odd_y in (0, 1):

        @pl.when(odd_ref[0] == odd_y)
        def _():
            pair = 1 - 2 * odd_y
            for ref, sign_x in ((cup_ref, 1), (cdown_ref, -1)):
                for side, sign_y in enumerate((pair, -pair)):
                    for k, (c, d) in enumerate(face_x):
                        y = cells_y - reach(c) if sign_y > 0 else 0
                        where = pl.ds(ext.row(at(cells_x, sign_x, d), y), reach(c))
                        ref[side, pl.ds(corner_start[k], reach(c)), :] = held(
                            mirrored(c, sign_x, sign_y), where
                        )
                    for k, c in enumerate(ends_x):
                        row = ext.row(at(cells_x, sign_x, HALO - 1), at(cells_y, sign_y, 1))
                        ref[side, pl.ds(ENDS_START + k, 1), :] = held(
                            mirrored(c, 1, sign_y), pl.ds(row, 1)
                        )
            for ref, sign in ((ya_ref, pair), (yb_ref, -pair)):
                for k, (c, d) in enumerate(face_y):
                    ref[pl.ds(k * cells_x, cells_x), :] = held(
                        mirrored(c, 1, sign), line_y(at(cells_y, sign, d))(0)
                    )
                for side, sign_x in enumerate((1, -1)):
                    for k, c in enumerate(ends_y):
                        row = ext.row(at(cells_x, sign_x, 1), at(cells_y, sign, HALO - 1))
                        to = len(face_y) * cells_x + side * len(ends_y) + k
                        ref[pl.ds(to, 1), :] = held(mirrored(c, sign_x, 1), pl.ds(row, 1))

    for ref, sign in ((up_ref, 1), (down_ref, -1)):
        for k, (c, d) in enumerate(face_x):
            where = pl.ds(ext.row(at(cells_x, sign, d), ext.inner(c)), ext.inner_rows)
            ref[pl.ds(k * ext.inner_rows, ext.inner_rows), :] = held(mirrored(c, sign, 1), where)


def forward_kernel(cup_ref, cdown_ref, _, ya_ref, far_ref):
    first = ya_ref.shape[0] - 2 * CORNER_ROWS
    for side, ref in enumerate((cup_ref, cdown_ref)):
        ya_ref[pl.ds(first + side * CORNER_ROWS, CORNER_ROWS), :] = ref[0]
        far_ref[side] = ref[1]


def beyond(cells, sign, d):
    return cells - 1 + d if sign > 0 else -d


def putter(one_ref, kinds_ref):
    def put(c, where, value):
        if c == KIND:
            kinds_ref[where, :] = value
        else:
            one_ref[c, where, :] = value

    return put


def put_sums(ext, put, x, y, count, values, carry):
    total, across, along, solute = values
    rows = pl.ds(ext.row(x, y), count)
    moved = across if carry > 0 else -across
    put(0, rows, total - moved)
    put(all_velocity.index((0, carry, 0)), pl.ds(ext.row(x, y - carry), count), moved)
    put(all_velocity.index((0, 0, 1)), rows, along)
    put(FLOW, rows, solute)


def put_corner(ext, put, ref, sign_x, sign_y, origin):
    for k, (c, d) in enumerate(face_x):
        x = beyond(ext.cells_x, sign_x, d)
        y = origin + (ext.cells_y - reach(c) if sign_y > 0 else 0)
        if c <= KIND:
            put(
                mirrored(c, -sign_x, sign_y),
                pl.ds(ext.row(x, y), reach(c)),
                ref[pl.ds(corner_start[k], reach(c)), :],
            )
        elif k == FACE_X_SUMS:
            for n in range(reach(c)):
                values = [ref[pl.ds(corner_start[k + i] + n, 1), :] for i in range(4)]
                carry = 1 if y + n < 0 or y + n == ext.cells_y - 1 else -1
                put_sums(ext, put, x, y + n, 1, values, carry)
    x = beyond(ext.cells_x, sign_x, HALO - 1)
    y = origin + (ext.cells_y - 1 if sign_y > 0 else 0)
    for k, c in enumerate(ends_x):
        put(mirrored(c, 1, sign_y), pl.ds(ext.row(x, y), 1), ref[pl.ds(ENDS_START + k, 1), :])


def put_inner(ext, put, ref, sign_x):
    for k, (c, d) in enumerate(face_x):
        x, y = beyond(ext.cells_x, sign_x, d), ext.inner(c)
        rows = [pl.ds((k + i) * ext.inner_rows, ext.inner_rows) for i in range(4)]
        if c <= KIND:
            put(
                mirrored(c, -sign_x, 1),
                pl.ds(ext.row(x, y), ext.inner_rows),
                ref[rows[0], :],
            )
        elif k == FACE_X_SUMS:
            put_sums(ext, put, x, y, ext.inner_rows, [ref[r, :] for r in rows], -1)


def put_face_y(ext, put, ref, sign_y):
    cells = ext.cells_x

    def line(x, y, count=cells):
        return pl.ds(ext.row(x, y), count, stride=ext.pitch)

    for k, (c, d) in enumerate(face_y):
        if c <= KIND:
            put(
                mirrored(c, 1, -sign_y),
                line(0, beyond(ext.cells_y, sign_y, d)),
                ref[pl.ds(k * cells, cells), :],
            )
    y = beyond(ext.cells_y, sign_y, HALO - 1)
    total, across, along, solute = (
        ref[pl.ds((FACE_Y_SUMS + i) * cells, cells), :] for i in range(4)
    )
    last = lax.broadcasted_iota(jnp.int32, across.shape, 0) == cells - 1
    back = all_velocity.index((-1, 0, 0))
    forth = all_velocity.index((1, 0, 0))
    put(0, line(0, y), total - jnp.where(last, across, -across))
    put(back, line(1, y, cells - 1), -across[: cells - 1])
    put(forth, pl.ds(ext.row(cells - 2, y), 1), across[cells - 1 :])
    put(all_velocity.index((0, 0, 1)), line(0, y), along)
    put(FLOW, line(0, y), solute)
    for side, sign_x in enumerate((1, -1)):
        x = cells - 1 if sign_x > 0 else 0
        for k, c in enumerate(ends_y):
            start = len(face_y) * cells + side * len(ends_y) + k
            put(mirrored(c, sign_x, 1), pl.ds(ext.row(x, y), 1), ref[pl.ds(start, 1), :])


def arriving(ext, ref, c, start, count):
    cx, cy, _ = all_velocity[c]
    return ref[c, pl.ds(start - (cx * ext.pitch + cy), count), :]


def advance(ext, source, target, kinds_ref, first, shifted):
    rows = pl.ds(first, 8)
    values = [arriving(ext, source, c, first, 8) for c in range(COUNT)]
    values = collide(values[:FLOW], values[FLOW:], kinds_ref[rows, :])
    lane = lax.broadcasted_iota(jnp.int32, values[0].shape, 1)

    def store(c, value):
        target[c, rows, :] = value

    if shifted:
        store_shifted(values, lane, store)
    else:
        for c in range(COUNT):
            store(c, values[c])


def finish(ext, source, x, density_ref, momentum_ref, concentration_ref):
    values = [arriving(ext, source, c, ext.row(x, 0), ext.cells_y) for c in range(COUNT)]
    lane = lax.broadcasted_iota(jnp.int32, values[0].shape, 1)

    def summed(weights):
        total = None
        for along_z in (0, 1, -1):
            part = None
            for c, weight in weights.items():
                if weight == 0 or all_velocity[c][2] != along_z:
                    continue
                if part is None:
                    part = values[c] if weight > 0 else -values[c]
                else:
                    part = part + values[c] if weight > 0 else part - values[c]
            if part is not None:
                part = depth_shift(part, along_z, lane)
                total = part if total is None else total + part
        return total

    density_ref[x] = summed({c: 1 for c in range(FLOW)})
    for axis in range(3):
        momentum_ref[axis, x] = summed({c: flow_velocity[c][axis] for c in range(FLOW)})
    concentration_ref[x] = summed({c: 1 for c in range(FLOW, COUNT)})


def middle_kernel(ext, odd_ref, _, __, up_ref, down_ref, cup_ref, cdown_ref, yb_ref, ya_ref,
                  one_ref, kinds_ref, two_ref, three_ref,
                  density_ref, momentum_ref, concentration_ref):
    put = putter(one_ref, kinds_ref)
    put_inner(ext, put, up_ref, -1)
    put_inner(ext, put, down_ref, 1)
    for odd_y in (0, 1):

        @pl.when(odd_ref[0] == odd_y)
        def _():
            pair = 1 - 2 * odd_y
            partner = ya_ref.at[1 - odd_y]
            put_face_y(ext, put, yb_ref, -pair)
            put_face_y(ext, put, partner, pair)
            for side, (ref, sign_x) in enumerate(((cup_ref, -1), (cdown_ref, 1))):
                put_corner(ext, put, ref.at[0], sign_x, pair, 0)
                put_corner(ext, put, ref.at[1], sign_x, -pair, 0)
                first = partner.shape[0] - (2 - side) * CORNER_ROWS
                corners = partner.at[pl.ds(first, CORNER_ROWS)]
                put_corner(ext, put, corners, sign_x, -pair, pair * ext.cells_y)

    for source, target, width in ((one_ref, two_ref, 2), (two_ref, three_ref, 1)):
        end = ext.row(ext.cells_x - 1 + width, ext.cells_y - 1 + width)
        for first in range(ext.row(-width, -width), end + 1, 8):
            advance(ext, source, target, kinds_ref, first, width > 1)
    for x in range(ext.cells_x):
        finish(ext, three_ref, x, density_ref, momentum_ref, concentration_ref)


def last_kernel(ext, odd_ref, _, __, ___, ____, far_ref, early_density_ref, early_momentum_ref,
                early_concentration_ref, density_ref, momentum_ref, concentration_ref,
                one_ref, kinds_ref, two_ref, three_ref):
    cells_x, cells_y = ext.cells_x, ext.cells_y
    put = putter(one_ref, kinds_ref)
    for x in range(HALO, cells_x - HALO):
        density_ref[x] = early_density_ref[x]
        for axis in range(3):
            momentum_ref[axis, x] = early_momentum_ref[axis, x]
        concentration_ref[x] = early_concentration_ref[x]
    for odd_y in (0, 1):

        @pl.when(odd_ref[0] == odd_y)
        def _():
            far = 2 * odd_y - 1
            for side, sign_x in enumerate((-1, 1)):
                put_corner(ext, put, far_ref.at[side], sign_x, -far, far * cells_y)
            for source, target, width in ((one_ref, two_ref, 2), (two_ref, three_ref, 1)):
                y = cells_y + width - 8 if far > 0 else -width
                for k in range(HALO):
                    for x in (k - width, cells_x - 1 + width - k):
                        advance(ext, source, target, kinds_ref, ext.row(x, y), width > 1)

    for k in range(HALO):
        for x in (k, cells_x - 1 - k):
            finish(ext, three_ref, x, density_ref, momentum_ref, concentration_ref)


def higher(i, count):
    return (i + 1) % count


def lower(i, count):
    return (i - 1) % count


def across(i, count):
    return (i + 1) % count if i % 2 else (i - 1) % count


def swapped(block, count_x, count_y, move_x, move_y):
    pairs = []
    for i in range(count_x):
        for j in range(count_y):
            to_x = move_x(i, count_x) if move_x else i
            to_y = move_y(j, count_y) if move_y else j
            pairs.append((i * count_y + j, to_x * count_y + to_y))
    return lax.ppermute(block, ("gx", "gy"), pairs)


def solution(mesh):
    count_x, count_y = mesh.shape["gx"], mesh.shape["gy"]
    assert count_y % 2 == 0

    def local(flow, solute, kind):
        _, cells_x, cells_y, depth = flow.shape
        f32 = jnp.float32
        shape = lambda *dims: jax.ShapeDtypeStruct(dims, f32)
        smem = pl.BlockSpec(memory_space=pltpu.SMEM)
        vmem = pl.BlockSpec(memory_space=pltpu.VMEM)
        hbm = pl.BlockSpec(memory_space=pltpu.HBM)
        params = pltpu.CompilerParams(vmem_limit_bytes=16 * 1024 * 1024)
        odd = jnp.reshape(lax.axis_index("gy") % 2, (1,)).astype(jnp.int32)
        ext = Extended(cells_x, cells_y)
        group = math.gcd(cells_x, 4)
        flow, solute, kind = (
            pltpu.with_memory_space_constraint(a, pltpu.HBM) for a in (flow, solute, kind)
        )
        post, kinds, up, down, ya, yb, cup, cdown = pl.pallas_call(
            functools.partial(first_kernel, ext, group),
            out_shape=[
                shape(COUNT, ext.rows, depth),
                shape(ext.rows, depth),
                shape(len(face_x) * ext.inner_rows, depth),
                shape(len(face_x) * ext.inner_rows, depth),
                shape(ext.face_y_rows + 2 * CORNER_ROWS, depth),
                shape(ext.face_y_rows, depth),
                shape(2, CORNER_ROWS, depth),
                shape(2, CORNER_ROWS, depth),
            ],
            in_specs=[smem, hbm, hbm, hbm],
            out_specs=[vmem] * 8,
            scratch_shapes=[
                pltpu.VMEM(flow.shape, f32),
                pltpu.VMEM(solute.shape, f32),
                pltpu.VMEM(kind.shape, kind.dtype),
                pltpu.VMEM((8, ext.rows, depth), f32),
                pltpu.SemaphoreType.DMA((cells_x // group, 3)),
            ],
            compiler_params=params,
        )(odd, flow, solute, kind)
        move = functools.partial(swapped, count_x=count_x, count_y=count_y)
        cup = move(cup, move_x=higher, move_y=None)
        cdown = move(cdown, move_x=lower, move_y=None)
        yb = move(yb, move_x=None, move_y=across)
        up = move(up, move_x=higher, move_y=None)
        down = move(down, move_x=lower, move_y=None)
        ya, far = pl.pallas_call(
            forward_kernel,
            out_shape=[shape(*ya.shape), shape(2, CORNER_ROWS, depth)],
            in_specs=[vmem] * 3,
            out_specs=[vmem] * 2,
            input_output_aliases={2: 0},
            compiler_params=params,
        )(cup, cdown, ya)
        far = move(far, move_x=None, move_y=across)
        ya = lax.all_gather(ya, "gy", axis_index_groups=[[j, j + 1] for j in range(0, count_y, 2)])
        moments = [
            shape(cells_x, cells_y, depth),
            shape(3, cells_x, cells_y, depth),
            shape(cells_x, cells_y, depth),
        ]
        one = shape(COUNT, ext.rows, depth)
        post, kinds, two, three, *early = pl.pallas_call(
            functools.partial(middle_kernel, ext),
            out_shape=[one, shape(ext.rows, depth), one, one] + moments,
            in_specs=[smem] + [vmem] * 8,
            out_specs=[vmem] * 7,
            input_output_aliases={1: 0, 2: 1},
            compiler_params=params,
        )(odd, post, kinds, up, down, cup, cdown, yb, ya)
        density, momentum, concentration, *_ = pl.pallas_call(
            functools.partial(last_kernel, ext),
            out_shape=moments + [one, shape(ext.rows, depth), one, one],
            in_specs=[smem] + [vmem] * 8,
            out_specs=[vmem] * 7,
            input_output_aliases={1: 3, 2: 4, 3: 5, 4: 6},
            compiler_params=params,
        )(odd, post, kinds, two, three, far, *early)
        return density, momentum, concentration

    placed = (P(None, "gx", "gy", None), P(None, "gx", "gy", None), P("gx", "gy", None))
    return jax.shard_map(
        local,
        mesh=mesh,
        in_specs=placed,
        out_specs=(P("gx", "gy", None), P(None, "gx", "gy", None), P("gx", "gy", None)),
        check_vma=False,
    )
```

```python
import functools
import math

import jax
import jax.numpy as jnp
from jax import lax
from jax.experimental import pallas as pl
from jax.experimental.pallas import tpu as pltpu
from jax.sharding import PartitionSpec as P

STEPS = 3
HALO = STEPS

flow_velocity = [
    (0, 0, 0),
    (1, 0, 0),
    (-1, 0, 0),
    (0, 1, 0),
    (0, -1, 0),
    (0, 0, 1),
    (0, 0, -1),
    (1, 1, 0),
    (-1, -1, 0),
    (1, -1, 0),
    (-1, 1, 0),
    (1, 0, 1),
    (-1, 0, -1),
    (1, 0, -1),
    (-1, 0, 1),
    (0, 1, 1),
    (0, -1, -1),
    (0, 1, -1),
    (0, -1, 1),
]
FLOW = len(flow_velocity)
all_velocity = flow_velocity + flow_velocity[:7]
COUNT = len(all_velocity)
KIND = COUNT
SUMS = {0: range(COUNT + 1, COUNT + 5), 1: range(COUNT + 5, COUNT + 9)}
flow_plus = 1.25
flow_minus = 1.0 / 1.125
solute_plus = 1.0 / 1.75
solute_minus = 1.0 / 0.7
inlet_density = 1.05
outlet_density = 0.95
inlet_solute = 1.0


def mirrored(channel, sign_x, sign_y):
    if channel >= KIND:
        return channel
    cx, cy, cz = all_velocity[channel]
    wanted = (cx * sign_x, cy * sign_y, cz)
    if channel < FLOW:
        return flow_velocity.index(wanted)
    return FLOW + flow_velocity[:7].index(wanted)


def moving(axis, toward):
    return [c for c in range(COUNT) if all_velocity[c][axis] == toward]


def needed(axis):
    outer = HALO - 1
    return (
        [(c, d) for d in range(1, outer) for c in range(COUNT)]
        + [(c, d) for d in (outer, HALO) for c in moving(axis, 1)]
        + [(c, outer) for c in SUMS[axis]]
        + [(KIND, d) for d in range(1, HALO)]
    )


face_x = needed(0)
face_y = needed(1)
ends_x = [c for c in moving(0, 0) if all_velocity[c][1] == 1]
ends_y = [c for c in moving(1, 0) if all_velocity[c][0] == 1]


def reach(channel):
    return HALO - 1 + (all_velocity[channel][1] if channel < COUNT else 0)


corner_start = [sum(reach(c) for c, _ in face_x[:k]) for k in range(len(face_x) + 1)]
ENDS_START = corner_start[-1]
CORNER_ROWS = -(-(ENDS_START + len(ends_x)) // 8) * 8
FACE_X_SUMS = face_x.index((SUMS[0][0], HALO - 1))
FACE_Y_SUMS = face_y.index((SUMS[1][0], HALO - 1))


def collide(flow, solute, kind):
    pore = kind == 0.0
    solid = kind == 1.0
    inlet = kind == 2.0
    zero = jnp.zeros_like(kind)
    pairs = range(1, FLOW, 2)
    total = {i: flow[i] + flow[i + 1] for i in pairs}
    gap = {i: flow[i] - flow[i + 1] for i in pairs}
    density = (flow[0] + total[1] + total[3]) + (total[5] + total[7] + total[9])
    density = density + ((total[11] + total[13]) + (total[15] + total[17]))
    mom_x = (gap[1] + gap[7]) + (gap[9] + gap[11]) + gap[13]
    mom_y = (gap[3] + gap[7]) + (gap[15] - gap[9]) + gap[17]
    mom_z = (gap[5] + gap[11]) + (gap[15] - gap[13]) - gap[17]
    square = mom_x * mom_x + mom_y * mom_y + mom_z * mom_z
    wall = jnp.where(solid, 0.5, zero)
    even = jnp.where(pore, (1.0 - flow_plus) / 2.0, wall)
    odd = jnp.where(pore, (1.0 - flow_minus) / 2.0, -wall)
    border = jnp.where(inlet, inlet_density, jnp.where(solid, 0.0, outlet_density))
    base = jnp.where(pore, flow_plus * density - (1.5 * flow_plus) * square, border)
    base_18 = base * (1.0 / 18.0)
    base_36 = base * (1.0 / 36.0)
    scale = math.sqrt(4.5 * flow_plus / 36.0)
    held = jnp.where(pore, scale, zero)
    vel = (mom_x * held, mom_y * held, mom_z * held)
    along = 3.0 * flow_minus / (36.0 * scale)
    out = [None] * COUNT
    out[0] = (even + even) * flow[0] + base * (1.0 / 3.0)
    for i in pairs:
        cx, cy, cz = flow_velocity[i]
        parts = [(c, v) for c, v in zip((cx, cy, cz), vel) if c != 0]
        if len(parts) == 1:
            t = parts[0][1]
            a = even * total[i] + (base_18 + 2.0 * (t * t))
            b = odd * gap[i] + (2.0 * along) * t
        else:
            t = parts[0][1] + parts[1][1] if parts[1][0] > 0 else parts[0][1] - parts[1][1]
            a = even * total[i] + (base_36 + t * t)
            b = odd * gap[i] + along * t
        out[i] = a + b
        out[i + 1] = a - b
    total = {i: solute[i] + solute[i + 1] for i in (1, 3, 5)}
    gap = {i: solute[i] - solute[i + 1] for i in (1, 3, 5)}
    concentration = (solute[0] + total[1]) + (total[3] + total[5])
    even = jnp.where(pore, (1.0 - solute_plus) / 2.0, wall)
    odd = jnp.where(pore, (1.0 - solute_minus) / 2.0, -wall)
    border = jnp.where(inlet, inlet_solute, zero)
    base = jnp.where(pore, solute_plus * concentration, border) * 0.125
    drift = concentration * (0.5 * solute_minus / scale)
    out[FLOW] = (even + even) * solute[0] + (base + base)
    for i, t in zip((1, 3, 5), vel):
        a = even * total[i] + base
        b = odd * gap[i] + drift * t
        out[FLOW + i] = a + b
        out[FLOW + i + 1] = a - b
    return out


def depth_shift(section, along_z, lane):
    depth = section.shape[-1]
    if along_z == 1:
        return jnp.where(lane == 0, 0.0, pltpu.roll(section, 1, section.ndim - 1))
    if along_z == -1:
        return jnp.where(lane == depth - 1, 0.0, pltpu.roll(section, depth - 1, section.ndim - 1))
    return section


def store_shifted(values, lane, store):
    for c in range(COUNT):
        store(c, depth_shift(values[c], all_velocity[c][2], lane))


class Extended:
    def __init__(self, cells_x, cells_y, halo=HALO):
        self.cells_x, self.cells_y, self.halo = cells_x, cells_y, halo
        self.pitch = cells_y + 2 * halo
        self.rows = -(-((cells_x + 2 * halo) * self.pitch + 16) // 8) * 8
        self.face_y_rows = len(face_y) * cells_x + 2 * len(ends_y)
        self.inner_rows = cells_y - 2 * (HALO - 1)

    def row(self, x, y):
        return (x + self.halo) * self.pitch + y + self.halo

    def runs(self, first, count):
        found = []
        for k in range(count):
            x, y = divmod(first + k, self.pitch)
            if found and y > 0:
                found[-1][1] += 1
            else:
                found.append([k, 1, x - self.halo, y - self.halo])
        return found

    def inner(self, channel):
        return HALO - 1 - (all_velocity[channel][1] if channel < COUNT else 0)


def first_kernel(ext, group, odd_ref, flow_hbm, solute_hbm, kind_hbm, post_ref, kinds_ref,
                 up_ref, down_ref, ya_ref, yb_ref, cup_ref, cdown_ref,
                 flow_ref, solute_ref, kind_ref, sums_ref, sems):
    cells_x, cells_y = ext.cells_x, ext.cells_y
    depth = kind_ref.shape[-1]
    lane = lax.broadcasted_iota(jnp.int32, (cells_y, depth), 1)
    copies = []
    for g in range(cells_x // group):
        planes = pl.ds(g * group, group)
        copies.append([
            pltpu.make_async_copy(kind_hbm.at[planes], kind_ref.at[planes], sems.at[g, 0]),
            pltpu.make_async_copy(flow_hbm.at[:, planes], flow_ref.at[:, planes], sems.at[g, 1]),
            pltpu.make_async_copy(
                solute_hbm.at[:, planes], solute_ref.at[:, planes], sems.at[g, 2]
            ),
        ])
        for copy in copies[-1]:
            copy.start()

    for x in range(cells_x):
        if x % group == 0:
            for copy in copies[x // group]:
                copy.wait()
        kind = kind_ref[x].astype(jnp.float32)
        rows = pl.ds(ext.row(x, 0), cells_y)
        kinds_ref[rows, :] = kind
        values = collide(
            [flow_ref[c, x] for c in range(FLOW)],
            [solute_ref[c, x] for c in range(COUNT - FLOW)],
            kind,
        )

        def store(c, value):
            post_ref[c, rows, :] = value

        store_shifted(values, lane, store)

    def sums(axis, where):
        across = 1 - axis
        cells = (cells_x, cells_y)[across]
        place = lax.broadcasted_iota(jnp.int32, (cells, depth), 0)
        parts = {}
        for move in (0, 1, -1):
            total = along = solute = None
            for c in moving(axis, 0):
                if all_velocity[c][across] != move:
                    continue
                value = post_ref[c, where(-move), :]
                if c >= FLOW:
                    solute = value if solute is None else solute + value
                    continue
                total = value if total is None else total + value
                cz = all_velocity[c][2]
                if cz != 0:
                    signed = value if cz > 0 else -value
                    along = signed if along is None else along + signed
            parts[move] = [total, along, solute]
            if move != 0:
                inside = place != (0 if move > 0 else cells - 1)
                parts[move] = [jnp.where(inside, p, 0.0) for p in parts[move]]
        total, along, solute = (parts[0][n] + parts[1][n] + parts[-1][n] for n in range(3))
        for c, value in zip(
            SUMS[axis], (total - along, parts[1][0] - parts[-1][0], along, solute)
        ):
            sums_ref[c - SUMS[0][0], where(0), :] = value

    def at(cells, sign, d):
        return cells - d if sign > 0 else d - 1

    def line_x(x):
        return lambda y: pl.ds(ext.row(x, y), cells_y)

    def line_y(y):
        return lambda x: pl.ds(ext.row(x, y), cells_x, stride=ext.pitch)

    zero = jnp.zeros((8, depth), jnp.float32)
    zeros = jnp.zeros((cells_x, depth), jnp.float32)
    for sign in (1, -1):
        sums(0, line_x(at(cells_x, sign, HALO - 1)))
        sums(1, line_y(at(cells_y, sign, HALO - 1)))
        for c in moving(0, 0):
            first = ext.row(beyond(cells_x, sign, HALO - 1), -HALO)
            for start in [*range(0, ext.pitch - 8, 8), ext.pitch - 8]:
                post_ref[c, pl.ds(first + start, 8), :] = zero
        for c in moving(1, 0):
            post_ref[c, line_y(beyond(cells_y, sign, HALO - 1))(0), :] = zeros

    def held(c, where):
        if c > KIND:
            return sums_ref[c - SUMS[0][0], where, :]
        return kinds_ref[where, :] if c == KIND else post_ref[c, where, :]

    for odd_y in (0, 1):

        @pl.when(odd_ref[0] == odd_y)
        def _():
            pair = 1 - 2 * odd_y
            for ref, sign_x in ((cup_ref, 1), (cdown_ref, -1)):
                for side, sign_y in enumerate((pair, -pair)):
                    for k, (c, d) in enumerate(face_x):
                        y = cells_y - reach(c) if sign_y > 0 else 0
                        where = pl.ds(ext.row(at(cells_x, sign_x, d), y), reach(c))
                        ref[side, pl.ds(corner_start[k], reach(c)), :] = held(
                            mirrored(c, sign_x, sign_y), where
                        )
                    for k, c in enumerate(ends_x):
                        row = ext.row(at(cells_x, sign_x, HALO - 1), at(cells_y, sign_y, 1))
                        ref[side, pl.ds(ENDS_START + k, 1), :] = held(
                            mirrored(c, 1, sign_y), pl.ds(row, 1)
                        )
            for ref, sign in ((ya_ref, pair), (yb_ref, -pair)):
                for k, (c, d) in enumerate(face_y):
                    ref[pl.ds(k * cells_x, cells_x), :] = held(
                        mirrored(c, 1, sign), line_y(at(cells_y, sign, d))(0)
                    )
                for side, sign_x in enumerate((1, -1)):
                    for k, c in enumerate(ends_y):
                        row = ext.row(at(cells_x, sign_x, 1), at(cells_y, sign, HALO - 1))
                        to = len(face_y) * cells_x + side * len(ends_y) + k
                        ref[pl.ds(to, 1), :] = held(mirrored(c, sign_x, 1), pl.ds(row, 1))

    for ref, sign in ((up_ref, 1), (down_ref, -1)):
        for k, (c, d) in enumerate(face_x):
            where = pl.ds(ext.row(at(cells_x, sign, d), ext.inner(c)), ext.inner_rows)
            ref[pl.ds(k * ext.inner_rows, ext.inner_rows), :] = held(mirrored(c, sign, 1), where)


def forward_kernel(cup_ref, cdown_ref, _, __, ya_ref, far_ref):
    first = ya_ref.shape[0] - 2 * CORNER_ROWS
    for side, ref in enumerate((cup_ref, cdown_ref)):
        ya_ref[pl.ds(first + side * CORNER_ROWS, CORNER_ROWS), :] = ref[0]
        far_ref[side] = ref[1]


def beyond(cells, sign, d):
    return cells - 1 + d if sign > 0 else -d


def putter(one_ref, kinds_ref):
    def put(c, where, value):
        if c == KIND:
            kinds_ref[where, :] = value
        else:
            one_ref[c, where, :] = value

    return put


def put_sums(ext, put, x, y, count, values, carry):
    total, across, along, solute = values
    rows = pl.ds(ext.row(x, y), count)
    moved = across if carry > 0 else -across
    put(0, rows, total - moved)
    put(all_velocity.index((0, carry, 0)), pl.ds(ext.row(x, y - carry), count), moved)
    put(all_velocity.index((0, 0, 1)), rows, along)
    put(FLOW, rows, solute)


def put_corner(ext, put, ref, sign_x, sign_y, origin):
    for k, (c, d) in enumerate(face_x):
        x = beyond(ext.cells_x, sign_x, d)
        y = origin + (ext.cells_y - reach(c) if sign_y > 0 else 0)
        if c <= KIND:
            put(
                mirrored(c, -sign_x, sign_y),
                pl.ds(ext.row(x, y), reach(c)),
                ref[pl.ds(corner_start[k], reach(c)), :],
            )
        elif k == FACE_X_SUMS:
            for n in range(reach(c)):
                values = [ref[pl.ds(corner_start[k + i] + n, 1), :] for i in range(4)]
                carry = 1 if y + n < 0 or y + n == ext.cells_y - 1 else -1
                put_sums(ext, put, x, y + n, 1, values, carry)
    x = beyond(ext.cells_x, sign_x, HALO - 1)
    y = origin + (ext.cells_y - 1 if sign_y > 0 else 0)
    for k, c in enumerate(ends_x):
        put(mirrored(c, 1, sign_y), pl.ds(ext.row(x, y), 1), ref[pl.ds(ENDS_START + k, 1), :])


def put_inner(ext, put, ref, sign_x):
    for k, (c, d) in enumerate(face_x):
        x, y = beyond(ext.cells_x, sign_x, d), ext.inner(c)
        rows = [pl.ds((k + i) * ext.inner_rows, ext.inner_rows) for i in range(4)]
        if c <= KIND:
            put(
                mirrored(c, -sign_x, 1),
                pl.ds(ext.row(x, y), ext.inner_rows),
                ref[rows[0], :],
            )
        elif k == FACE_X_SUMS:
            put_sums(ext, put, x, y, ext.inner_rows, [ref[r, :] for r in rows], -1)


def put_face_y(ext, put, ref, sign_y):
    cells = ext.cells_x

    def line(x, y, count=cells):
        return pl.ds(ext.row(x, y), count, stride=ext.pitch)

    for k, (c, d) in enumerate(face_y):
        if c <= KIND:
            put(
                mirrored(c, 1, -sign_y),
                line(0, beyond(ext.cells_y, sign_y, d)),
                ref[pl.ds(k * cells, cells), :],
            )
    y = beyond(ext.cells_y, sign_y, HALO - 1)
    total, across, along, solute = (
        ref[pl.ds((FACE_Y_SUMS + i) * cells, cells), :] for i in range(4)
    )
    last = lax.broadcasted_iota(jnp.int32, across.shape, 0) == cells - 1
    back = all_velocity.index((-1, 0, 0))
    forth = all_velocity.index((1, 0, 0))
    put(0, line(0, y), total - jnp.where(last, across, -across))
    put(back, line(1, y, cells - 1), -across[: cells - 1])
    put(forth, pl.ds(ext.row(cells - 2, y), 1), across[cells - 1 :])
    put(all_velocity.index((0, 0, 1)), line(0, y), along)
    put(FLOW, line(0, y), solute)
    for side, sign_x in enumerate((1, -1)):
        x = cells - 1 if sign_x > 0 else 0
        for k, c in enumerate(ends_y):
            start = len(face_y) * cells + side * len(ends_y) + k
            put(mirrored(c, sign_x, 1), pl.ds(ext.row(x, y), 1), ref[pl.ds(start, 1), :])


def arriving(ext, ref, c, start, count):
    cx, cy, _ = all_velocity[c]
    return ref[c, pl.ds(start - (cx * ext.pitch + cy), count), :]


def advance(ext, source, first, kind):
    values = [arriving(ext, source, c, first, 8) for c in range(COUNT)]
    return collide(values[:FLOW], values[FLOW:], kind)


def second_step(ext, near, one_ref, two_ref, kinds_ref, first):
    values = advance(ext, one_ref, first, kinds_ref[pl.ds(first, 8), :])
    lane = lax.broadcasted_iota(jnp.int32, values[0].shape, 1)
    pieces = []
    for offset, count, x, y in ext.runs(first, 8):
        low, high = max(y, -near.halo), min(y + count, ext.cells_y + near.halo)
        if low < high and -near.halo <= x < ext.cells_x + near.halo:
            pieces.append((offset + low - y, high - low, near.row(x, low)))

    def store(c, value):
        for offset, count, row in pieces:
            two_ref[c, pl.ds(row, count), :] = value[offset : offset + count]

    store_shifted(values, lane, store)


def third_step(near, two_ref, three_ref, kind, first):
    for c, value in enumerate(advance(near, two_ref, first, kind)):
        three_ref[c, pl.ds(first, 8), :] = value


def finish(ext, source, x, density_ref, momentum_ref, concentration_ref):
    values = [arriving(ext, source, c, ext.row(x, 0), ext.cells_y) for c in range(COUNT)]
    lane = lax.broadcasted_iota(jnp.int32, values[0].shape, 1)

    def summed(weights):
        total = None
        for along_z in (0, 1, -1):
            part = None
            for c, weight in weights.items():
                if weight == 0 or all_velocity[c][2] != along_z:
                    continue
                if part is None:
                    part = values[c] if weight > 0 else -values[c]
                else:
                    part = part + values[c] if weight > 0 else part - values[c]
            if part is not None:
                part = depth_shift(part, along_z, lane)
                total = part if total is None else total + part
        return total

    density_ref[x] = summed({c: 1 for c in range(FLOW)})
    for axis in range(3):
        momentum_ref[axis, x] = summed({c: flow_velocity[c][axis] for c in range(FLOW)})
    concentration_ref[x] = summed({c: 1 for c in range(FLOW, COUNT)})


def interior_kernel(ext, near, post_ref, kinds_ref, two_ref, three_ref, token_ref):
    for x in range(1, ext.cells_x - 1):
        second_step(ext, near, post_ref, two_ref, kinds_ref, ext.row(x, 0))
    for x in range(2, ext.cells_x - 2):
        kind = kinds_ref[pl.ds(ext.row(x, 0), ext.cells_y), :]
        third_step(near, two_ref, three_ref, kind, near.row(x, 0))
    token_ref[...] = jnp.zeros_like(token_ref)


def middle_kernel(ext, near, odd_ref, _, __, ___, ____, up_ref, down_ref, cup_ref, cdown_ref,
                  yb_ref, ya_ref, one_ref, kinds_ref, two_ref, three_ref,
                  density_ref, momentum_ref, concentration_ref, near_kinds_ref):
    put = putter(one_ref, kinds_ref)
    put_inner(ext, put, up_ref, -1)
    put_inner(ext, put, down_ref, 1)
    for odd_y in (0, 1):

        @pl.when(odd_ref[0] == odd_y)
        def _():
            pair = 1 - 2 * odd_y
            partner = ya_ref.at[1 - odd_y]
            put_face_y(ext, put, yb_ref, -pair)
            put_face_y(ext, put, partner, pair)
            for side, (ref, sign_x) in enumerate(((cup_ref, -1), (cdown_ref, 1))):
                put_corner(ext, put, ref.at[0], sign_x, pair, 0)
                put_corner(ext, put, ref.at[1], sign_x, -pair, 0)
                first = partner.shape[0] - (2 - side) * CORNER_ROWS
                corners = partner.at[pl.ds(first, CORNER_ROWS)]
                put_corner(ext, put, corners, sign_x, -pair, pair * ext.cells_y)

    last_x, last_y = ext.cells_x - 1, ext.cells_y - 1
    for space, depth in ((ext, 1), (near, 2)):
        halo = 3 - depth
        runs = [
            (space.row(-halo, -halo), space.row(depth, depth - 1)),
            (space.row(last_x - depth, last_y - depth + 1), space.row(last_x + halo, last_y + halo)),
        ] + [
            (space.row(x, last_y - depth + 1), space.row(x + 1, depth - 1))
            for x in range(depth, last_x - depth)
        ]
        if space is near:
            for x in range(-halo, ext.cells_x + halo):
                for y in (-halo, last_y + halo - 7):
                    near_kinds_ref[pl.ds(near.row(x, y), 8), :] = kinds_ref[pl.ds(ext.row(x, y), 8), :]
        for start, end in runs:
            for first in range(start, end + 1, 8):
                if space is ext:
                    second_step(ext, near, one_ref, two_ref, kinds_ref, first)
                else:
                    kind = near_kinds_ref[pl.ds(first, 8), :]
                    third_step(near, two_ref, three_ref, kind, first)
    for x in range(ext.cells_x):
        finish(near, three_ref, x, density_ref, momentum_ref, concentration_ref)


def last_kernel(ext, near, odd_ref, _, __, ___, ____, far_ref, early_density_ref, early_momentum_ref,
                early_concentration_ref, density_ref, momentum_ref, concentration_ref,
                one_ref, kinds_ref, two_ref, three_ref):
    cells_x, cells_y = ext.cells_x, ext.cells_y
    put = putter(one_ref, kinds_ref)
    for x in range(HALO, cells_x - HALO):
        density_ref[x] = early_density_ref[x]
        for axis in range(3):
            momentum_ref[axis, x] = early_momentum_ref[axis, x]
        concentration_ref[x] = early_concentration_ref[x]
    for odd_y in (0, 1):

        @pl.when(odd_ref[0] == odd_y)
        def _():
            far = 2 * odd_y - 1
            for side, sign_x in enumerate((-1, 1)):
                put_corner(ext, put, far_ref.at[side], sign_x, -far, far * cells_y)
            for width in (2, 1):
                y = cells_y + width - 8 if far > 0 else -width
                for k in range(HALO):
                    for x in (k - width, cells_x - 1 + width - k):
                        if width == 2:
                            second_step(ext, near, one_ref, two_ref, kinds_ref, ext.row(x, y))
                        else:
                            kind = kinds_ref[pl.ds(ext.row(x, y), 8), :]
                            third_step(near, two_ref, three_ref, kind, near.row(x, y))

    for k in range(HALO):
        for x in (k, cells_x - 1 - k):
            finish(near, three_ref, x, density_ref, momentum_ref, concentration_ref)


def higher(i, count):
    return (i + 1) % count


def lower(i, count):
    return (i - 1) % count


def across(i, count):
    return (i + 1) % count if i % 2 else (i - 1) % count


def swapped(block, count_x, count_y, move_x, move_y):
    pairs = []
    for i in range(count_x):
        for j in range(count_y):
            to_x = move_x(i, count_x) if move_x else i
            to_y = move_y(j, count_y) if move_y else j
            pairs.append((i * count_y + j, to_x * count_y + to_y))
    return lax.ppermute(block, ("gx", "gy"), pairs)


def solution(mesh):
    count_x, count_y = mesh.shape["gx"], mesh.shape["gy"]
    assert count_y % 2 == 0

    def local(flow, solute, kind):
        _, cells_x, cells_y, depth = flow.shape
        f32 = jnp.float32
        shape = lambda *dims: jax.ShapeDtypeStruct(dims, f32)
        smem = pl.BlockSpec(memory_space=pltpu.SMEM)
        vmem = pl.BlockSpec(memory_space=pltpu.VMEM)
        hbm = pl.BlockSpec(memory_space=pltpu.HBM)
        params = pltpu.CompilerParams(vmem_limit_bytes=16 * 1024 * 1024)
        odd = jnp.reshape(lax.axis_index("gy") % 2, (1,)).astype(jnp.int32)
        ext = Extended(cells_x, cells_y)
        group = math.gcd(cells_x, 4)
        flow, solute, kind = (
            pltpu.with_memory_space_constraint(a, pltpu.HBM) for a in (flow, solute, kind)
        )
        post, kinds, up, down, ya, yb, cup, cdown = pl.pallas_call(
            functools.partial(first_kernel, ext, group),
            out_shape=[
                shape(COUNT, ext.rows, depth),
                shape(ext.rows, depth),
                shape(len(face_x) * ext.inner_rows, depth),
                shape(len(face_x) * ext.inner_rows, depth),
                shape(ext.face_y_rows + 2 * CORNER_ROWS, depth),
                shape(ext.face_y_rows, depth),
                shape(2, CORNER_ROWS, depth),
                shape(2, CORNER_ROWS, depth),
            ],
            in_specs=[smem, hbm, hbm, hbm],
            out_specs=[vmem] * 8,
            scratch_shapes=[
                pltpu.VMEM(flow.shape, f32),
                pltpu.VMEM(solute.shape, f32),
                pltpu.VMEM(kind.shape, kind.dtype),
                pltpu.VMEM((8, ext.rows, depth), f32),
                pltpu.SemaphoreType.DMA((cells_x // group, 3)),
            ],
            compiler_params=params,
        )(odd, flow, solute, kind)
        move = functools.partial(swapped, count_x=count_x, count_y=count_y)
        cup = move(cup, move_x=higher, move_y=None)
        cdown = move(cdown, move_x=lower, move_y=None)
        yb = move(yb, move_x=None, move_y=across)
        up = move(up, move_x=higher, move_y=None)
        down = move(down, move_x=lower, move_y=None)
        near = Extended(cells_x, cells_y, HALO - 1)
        one = shape(COUNT, ext.rows, depth)
        two_shape = shape(COUNT, near.rows, depth)
        two, three, token = pl.pallas_call(
            functools.partial(interior_kernel, ext, near),
            out_shape=[two_shape, two_shape, shape(8, depth)],
            in_specs=[vmem] * 2,
            out_specs=[vmem] * 3,
            compiler_params=params,
        )(post, kinds)
        ya, far = pl.pallas_call(
            forward_kernel,
            out_shape=[shape(*ya.shape), shape(2, CORNER_ROWS, depth)],
            in_specs=[vmem] * 4,
            out_specs=[vmem] * 2,
            input_output_aliases={3: 0},
            compiler_params=params,
        )(cup, cdown, token, ya)
        far = move(far, move_x=None, move_y=across)
        ya = lax.all_gather(ya, "gy", axis_index_groups=[[j, j + 1] for j in range(0, count_y, 2)])
        moments = [
            shape(cells_x, cells_y, depth),
            shape(3, cells_x, cells_y, depth),
            shape(cells_x, cells_y, depth),
        ]
        post, kinds, two, three, *early = pl.pallas_call(
            functools.partial(middle_kernel, ext, near),
            out_shape=[one, shape(ext.rows, depth), two_shape, two_shape] + moments,
            in_specs=[smem] + [vmem] * 10,
            out_specs=[vmem] * 7,
            scratch_shapes=[pltpu.VMEM((near.rows, depth), f32)],
            input_output_aliases={1: 0, 2: 1, 3: 2, 4: 3},
            compiler_params=params,
        )(odd, post, kinds, two, three, up, down, cup, cdown, yb, ya)
        density, momentum, concentration, *_ = pl.pallas_call(
            functools.partial(last_kernel, ext, near),
            out_shape=moments + [one, shape(ext.rows, depth), two_shape, two_shape],
            in_specs=[smem] + [vmem] * 8,
            out_specs=[vmem] * 7,
            input_output_aliases={1: 3, 2: 4, 3: 5, 4: 6},
            compiler_params=params,
        )(odd, post, kinds, two, three, far, *early)
        return density, momentum, concentration

    placed = (P(None, "gx", "gy", None), P(None, "gx", "gy", None), P("gx", "gy", None))
    return jax.shard_map(
        local,
        mesh=mesh,
        in_specs=placed,
        out_specs=(P("gx", "gy", None), P(None, "gx", "gy", None), P("gx", "gy", None)),
        check_vma=False,
    )
```

```python
import functools
import math

import jax
import jax.numpy as jnp
from jax import lax
from jax.experimental import pallas as pl
from jax.experimental.pallas import tpu as pltpu
from jax.sharding import PartitionSpec as P

STEPS = 3
HALO = STEPS

flow_velocity = [
    (0, 0, 0),
    (1, 0, 0),
    (-1, 0, 0),
    (0, 1, 0),
    (0, -1, 0),
    (0, 0, 1),
    (0, 0, -1),
    (1, 1, 0),
    (-1, -1, 0),
    (1, -1, 0),
    (-1, 1, 0),
    (1, 0, 1),
    (-1, 0, -1),
    (1, 0, -1),
    (-1, 0, 1),
    (0, 1, 1),
    (0, -1, -1),
    (0, 1, -1),
    (0, -1, 1),
]
FLOW = len(flow_velocity)
all_velocity = flow_velocity + flow_velocity[:7]
COUNT = len(all_velocity)
KIND = COUNT
SUMS = {0: range(COUNT + 1, COUNT + 5), 1: range(COUNT + 5, COUNT + 9)}
flow_plus = 1.25
flow_minus = 1.0 / 1.125
solute_plus = 1.0 / 1.75
solute_minus = 1.0 / 0.7
inlet_density = 1.05
outlet_density = 0.95
inlet_solute = 1.0


def mirrored(channel, sign_x, sign_y):
    if channel >= KIND:
        return channel
    cx, cy, cz = all_velocity[channel]
    wanted = (cx * sign_x, cy * sign_y, cz)
    if channel < FLOW:
        return flow_velocity.index(wanted)
    return FLOW + flow_velocity[:7].index(wanted)


def moving(axis, toward):
    return [c for c in range(COUNT) if all_velocity[c][axis] == toward]


def needed(axis):
    outer = HALO - 1
    return (
        [(c, d) for d in range(1, outer) for c in range(COUNT)]
        + [(c, d) for d in (outer, HALO) for c in moving(axis, 1)]
        + [(c, outer) for c in SUMS[axis]]
        + [(KIND, d) for d in range(1, HALO)]
    )


face_x = needed(0)
face_y = needed(1)
ends_x = [c for c in moving(0, 0) if all_velocity[c][1] == 1]
ends_y = [c for c in moving(1, 0) if all_velocity[c][0] == 1]


def reach(channel):
    return HALO - 1 + (all_velocity[channel][1] if channel < COUNT else 0)


corner_start = [sum(reach(c) for c, _ in face_x[:k]) for k in range(len(face_x) + 1)]
ENDS_START = corner_start[-1]
CORNER_ROWS = -(-(ENDS_START + len(ends_x)) // 8) * 8
FACE_X_SUMS = face_x.index((SUMS[0][0], HALO - 1))
FACE_Y_SUMS = face_y.index((SUMS[1][0], HALO - 1))


def collide(flow, solute, kind):
    pore = kind == 0.0
    solid = kind == 1.0
    inlet = kind == 2.0
    zero = jnp.zeros_like(kind)
    pairs = range(1, FLOW, 2)
    total = {i: flow[i] + flow[i + 1] for i in pairs}
    gap = {i: flow[i] - flow[i + 1] for i in pairs}
    density = (flow[0] + total[1] + total[3]) + (total[5] + total[7] + total[9])
    density = density + ((total[11] + total[13]) + (total[15] + total[17]))
    mom_x = (gap[1] + gap[7]) + (gap[9] + gap[11]) + gap[13]
    mom_y = (gap[3] + gap[7]) + (gap[15] - gap[9]) + gap[17]
    mom_z = (gap[5] + gap[11]) + (gap[15] - gap[13]) - gap[17]
    square = mom_x * mom_x + mom_y * mom_y + mom_z * mom_z
    wall = jnp.where(solid, 0.5, zero)
    even = jnp.where(pore, (1.0 - flow_plus) / 2.0, wall)
    odd = jnp.where(pore, (1.0 - flow_minus) / 2.0, -wall)
    border = jnp.where(inlet, inlet_density, jnp.where(solid, 0.0, outlet_density))
    base = jnp.where(pore, flow_plus * density - (1.5 * flow_plus) * square, border)
    base_18 = base * (1.0 / 18.0)
    base_36 = base * (1.0 / 36.0)
    scale = math.sqrt(4.5 * flow_plus / 36.0)
    held = jnp.where(pore, scale, zero)
    vel = (mom_x * held, mom_y * held, mom_z * held)
    along = 3.0 * flow_minus / (36.0 * scale)
    out = [None] * COUNT
    out[0] = (even + even) * flow[0] + base * (1.0 / 3.0)
    for i in pairs:
        cx, cy, cz = flow_velocity[i]
        parts = [(c, v) for c, v in zip((cx, cy, cz), vel) if c != 0]
        if len(parts) == 1:
            t = parts[0][1]
            a = even * total[i] + (base_18 + 2.0 * (t * t))
            b = odd * gap[i] + (2.0 * along) * t
        else:
            t = parts[0][1] + parts[1][1] if parts[1][0] > 0 else parts[0][1] - parts[1][1]
            a = even * total[i] + (base_36 + t * t)
            b = odd * gap[i] + along * t
        out[i] = a + b
        out[i + 1] = a - b
    total = {i: solute[i] + solute[i + 1] for i in (1, 3, 5)}
    gap = {i: solute[i] - solute[i + 1] for i in (1, 3, 5)}
    concentration = (solute[0] + total[1]) + (total[3] + total[5])
    even = jnp.where(pore, (1.0 - solute_plus) / 2.0, wall)
    odd = jnp.where(pore, (1.0 - solute_minus) / 2.0, -wall)
    border = jnp.where(inlet, inlet_solute, zero)
    base = jnp.where(pore, solute_plus * concentration, border) * 0.125
    drift = concentration * (0.5 * solute_minus / scale)
    out[FLOW] = (even + even) * solute[0] + (base + base)
    for i, t in zip((1, 3, 5), vel):
        a = even * total[i] + base
        b = odd * gap[i] + drift * t
        out[FLOW + i] = a + b
        out[FLOW + i + 1] = a - b
    return out


def depth_shift(section, along_z, lane):
    depth = section.shape[-1]
    if along_z == 1:
        return jnp.where(lane == 0, 0.0, pltpu.roll(section, 1, section.ndim - 1))
    if along_z == -1:
        return jnp.where(lane == depth - 1, 0.0, pltpu.roll(section, depth - 1, section.ndim - 1))
    return section


def store_shifted(values, lane, store):
    for c in range(COUNT):
        store(c, depth_shift(values[c], all_velocity[c][2], lane))


class Extended:
    def __init__(self, cells_x, cells_y, halo=HALO):
        self.cells_x, self.cells_y, self.halo = cells_x, cells_y, halo
        self.pitch = cells_y + 2 * halo
        self.rows = -(-((cells_x + 2 * halo) * self.pitch + 16) // 8) * 8
        self.face_y_rows = len(face_y) * cells_x + 2 * len(ends_y)
        self.inner_rows = cells_y - 2 * (HALO - 1)

    def row(self, x, y):
        return (x + self.halo) * self.pitch + y + self.halo

    def runs(self, first, count):
        found = []
        for k in range(count):
            x, y = divmod(first + k, self.pitch)
            if found and y > 0:
                found[-1][1] += 1
            else:
                found.append([k, 1, x - self.halo, y - self.halo])
        return found

    def inner(self, channel):
        return HALO - 1 - (all_velocity[channel][1] if channel < COUNT else 0)


def inside(cells, sign, d):
    return cells - d if sign > 0 else d - 1


def beyond(cells, sign, d):
    return cells - 1 + d if sign > 0 else -d


def line_x(ext, x):
    return lambda y: pl.ds(ext.row(x, y), ext.cells_y)


def line_y(ext, y):
    return lambda x: pl.ds(ext.row(x, y), ext.cells_x, stride=ext.pitch)


def reader(post_ref, kinds_ref, sums_ref):
    def held(c, where):
        if c > KIND:
            return sums_ref[c - SUMS[0][0], where, :]
        return kinds_ref[where, :] if c == KIND else post_ref[c, where, :]

    return held


def put_line_sums(axis, cells, where, post_ref, sums_ref):
    across = 1 - axis
    place = lax.broadcasted_iota(jnp.int32, (cells, post_ref.shape[-1]), 0)
    parts = {}
    for move in (0, 1, -1):
        total = along = solute = None
        for c in moving(axis, 0):
            if all_velocity[c][across] != move:
                continue
            value = post_ref[c, where(-move), :]
            if c >= FLOW:
                solute = value if solute is None else solute + value
                continue
            total = value if total is None else total + value
            cz = all_velocity[c][2]
            if cz != 0:
                signed = value if cz > 0 else -value
                along = signed if along is None else along + signed
        parts[move] = [total, along, solute]
        if move != 0:
            inside = place != (0 if move > 0 else cells - 1)
            parts[move] = [jnp.where(inside, p, 0.0) for p in parts[move]]
    total, along, solute = (parts[0][n] + parts[1][n] + parts[-1][n] for n in range(3))
    for c, value in zip(
        SUMS[axis], (total - along, parts[1][0] - parts[-1][0], along, solute)
    ):
        sums_ref[c - SUMS[0][0], where(0), :] = value


def pack_face_y(ext, sign, post_ref, kinds_ref, sums_ref, ref):
    held = reader(post_ref, kinds_ref, sums_ref)
    put_line_sums(
        1, ext.cells_x, line_y(ext, inside(ext.cells_y, sign, HALO - 1)), post_ref, sums_ref
    )
    for k, (c, d) in enumerate(face_y):
        ref[pl.ds(k * ext.cells_x, ext.cells_x), :] = held(
            mirrored(c, 1, sign), line_y(ext, inside(ext.cells_y, sign, d))(0)
        )
    for side, sign_x in enumerate((1, -1)):
        for k, c in enumerate(ends_y):
            row = ext.row(inside(ext.cells_x, sign_x, 1), inside(ext.cells_y, sign, HALO - 1))
            to = len(face_y) * ext.cells_x + side * len(ends_y) + k
            ref[pl.ds(to, 1), :] = held(mirrored(c, sign_x, 1), pl.ds(row, 1))


def first_kernel(ext, groups, odd_ref, flow_hbm, solute_hbm, kind_hbm, post_ref, kinds_ref,
                 up_ref, down_ref, yb_ref, cup_ref, cdown_ref,
                 flow_ref, solute_ref, kind_ref, sums_ref, sems):
    cells_x, cells_y = ext.cells_x, ext.cells_y
    depth = kind_ref.shape[-1]
    lane = lax.broadcasted_iota(jnp.int32, (cells_y, depth), 1)
    copies = {}
    for g, (first, count) in enumerate(groups):
        planes = pl.ds(first, count)
        copies[first] = [
            pltpu.make_async_copy(flow_hbm.at[:, planes], flow_ref.at[:, planes], sems.at[g, 0]),
            pltpu.make_async_copy(
                solute_hbm.at[:, planes], solute_ref.at[:, planes], sems.at[g, 1]
            ),
        ]
    copies[0].append(pltpu.make_async_copy(kind_hbm, kind_ref, sems.at[0, 2]))
    for copy in [copy for group in copies.values() for copy in group]:
        copy.start()

    for x in range(cells_x):
        for copy in copies.get(x, []):
            copy.wait()
        kind = kind_ref[x].astype(jnp.float32)
        rows = pl.ds(ext.row(x, 0), cells_y)
        kinds_ref[rows, :] = kind
        values = collide(
            [flow_ref[c, x] for c in range(FLOW)],
            [solute_ref[c, x] for c in range(COUNT - FLOW)],
            kind,
        )

        def store(c, value):
            post_ref[c, rows, :] = value

        store_shifted(values, lane, store)

    held = reader(post_ref, kinds_ref, sums_ref)
    for sign in (1, -1):
        put_line_sums(
            0, cells_y, line_x(ext, inside(cells_x, sign, HALO - 1)), post_ref, sums_ref
        )
    for odd_y in (0, 1):

        @pl.when(odd_ref[0] == odd_y)
        def _():
            pair = 1 - 2 * odd_y
            pack_face_y(ext, -pair, post_ref, kinds_ref, sums_ref, yb_ref)
            for ref, sign_x in ((cup_ref, 1), (cdown_ref, -1)):
                for side, sign_y in enumerate((pair, -pair)):
                    for k, (c, d) in enumerate(face_x):
                        y = cells_y - reach(c) if sign_y > 0 else 0
                        where = pl.ds(ext.row(inside(cells_x, sign_x, d), y), reach(c))
                        ref[side, pl.ds(corner_start[k], reach(c)), :] = held(
                            mirrored(c, sign_x, sign_y), where
                        )
                    for k, c in enumerate(ends_x):
                        row = ext.row(
                            inside(cells_x, sign_x, HALO - 1), inside(cells_y, sign_y, 1)
                        )
                        ref[side, pl.ds(ENDS_START + k, 1), :] = held(
                            mirrored(c, 1, sign_y), pl.ds(row, 1)
                        )

    for ref, sign in ((up_ref, 1), (down_ref, -1)):
        for k, (c, d) in enumerate(face_x):
            where = pl.ds(ext.row(inside(cells_x, sign, d), ext.inner(c)), ext.inner_rows)
            ref[pl.ds(k * ext.inner_rows, ext.inner_rows), :] = held(mirrored(c, sign, 1), where)


def forward_kernel(cup_ref, cdown_ref, _, ya_ref, far_ref):
    first = ya_ref.shape[0] - 2 * CORNER_ROWS
    for side, ref in enumerate((cup_ref, cdown_ref)):
        ya_ref[pl.ds(first + side * CORNER_ROWS, CORNER_ROWS), :] = ref[0]
        far_ref[side] = ref[1]


def putter(one_ref, kinds_ref):
    def put(c, where, value):
        if c == KIND:
            kinds_ref[where, :] = value
        else:
            one_ref[c, where, :] = value

    return put


def put_sums(ext, put, x, y, count, values, carry):
    total, across, along, solute = values
    rows = pl.ds(ext.row(x, y), count)
    moved = across if carry > 0 else -across
    put(0, rows, total - moved)
    put(all_velocity.index((0, carry, 0)), pl.ds(ext.row(x, y - carry), count), moved)
    put(all_velocity.index((0, 0, 1)), rows, along)
    put(FLOW, rows, solute)


def put_corner(ext, put, ref, sign_x, sign_y, origin):
    for k, (c, d) in enumerate(face_x):
        x = beyond(ext.cells_x, sign_x, d)
        y = origin + (ext.cells_y - reach(c) if sign_y > 0 else 0)
        if c <= KIND:
            put(
                mirrored(c, -sign_x, sign_y),
                pl.ds(ext.row(x, y), reach(c)),
                ref[pl.ds(corner_start[k], reach(c)), :],
            )
        elif k == FACE_X_SUMS:
            for n in range(reach(c)):
                values = [ref[pl.ds(corner_start[k + i] + n, 1), :] for i in range(4)]
                carry = 1 if y + n < 0 or y + n == ext.cells_y - 1 else -1
                put_sums(ext, put, x, y + n, 1, values, carry)
    x = beyond(ext.cells_x, sign_x, HALO - 1)
    y = origin + (ext.cells_y - 1 if sign_y > 0 else 0)
    for k, c in enumerate(ends_x):
        put(mirrored(c, 1, sign_y), pl.ds(ext.row(x, y), 1), ref[pl.ds(ENDS_START + k, 1), :])


def put_inner(ext, put, ref, sign_x):
    for k, (c, d) in enumerate(face_x):
        x, y = beyond(ext.cells_x, sign_x, d), ext.inner(c)
        rows = [pl.ds((k + i) * ext.inner_rows, ext.inner_rows) for i in range(4)]
        if c <= KIND:
            put(
                mirrored(c, -sign_x, 1),
                pl.ds(ext.row(x, y), ext.inner_rows),
                ref[rows[0], :],
            )
        elif k == FACE_X_SUMS:
            put_sums(ext, put, x, y, ext.inner_rows, [ref[r, :] for r in rows], -1)


def put_face_y(ext, put, ref, sign_y):
    cells = ext.cells_x

    def line(x, y, count=cells):
        return pl.ds(ext.row(x, y), count, stride=ext.pitch)

    for k, (c, d) in enumerate(face_y):
        if c <= KIND:
            put(
                mirrored(c, 1, -sign_y),
                line(0, beyond(ext.cells_y, sign_y, d)),
                ref[pl.ds(k * cells, cells), :],
            )
    y = beyond(ext.cells_y, sign_y, HALO - 1)
    total, across, along, solute = (
        ref[pl.ds((FACE_Y_SUMS + i) * cells, cells), :] for i in range(4)
    )
    last = lax.broadcasted_iota(jnp.int32, across.shape, 0) == cells - 1
    back = all_velocity.index((-1, 0, 0))
    forth = all_velocity.index((1, 0, 0))
    put(0, line(0, y), total - jnp.where(last, across, -across))
    put(back, line(1, y, cells - 1), -across[: cells - 1])
    put(forth, pl.ds(ext.row(cells - 2, y), 1), across[cells - 1 :])
    put(all_velocity.index((0, 0, 1)), line(0, y), along)
    put(FLOW, line(0, y), solute)
    for side, sign_x in enumerate((1, -1)):
        x = cells - 1 if sign_x > 0 else 0
        for k, c in enumerate(ends_y):
            start = len(face_y) * cells + side * len(ends_y) + k
            put(mirrored(c, sign_x, 1), pl.ds(ext.row(x, y), 1), ref[pl.ds(start, 1), :])


def arriving(ext, ref, c, start, count):
    cx, cy, _ = all_velocity[c]
    return ref[c, pl.ds(start - (cx * ext.pitch + cy), count), :]


def advance(ext, source, first, kind):
    values = [arriving(ext, source, c, first, 8) for c in range(COUNT)]
    return collide(values[:FLOW], values[FLOW:], kind)


def second_step(ext, near, one_ref, two_ref, kinds_ref, first):
    values = advance(ext, one_ref, first, kinds_ref[pl.ds(first, 8), :])
    lane = lax.broadcasted_iota(jnp.int32, values[0].shape, 1)
    pieces = []
    for offset, count, x, y in ext.runs(first, 8):
        low, high = max(y, -near.halo), min(y + count, ext.cells_y + near.halo)
        if low < high and -near.halo <= x < ext.cells_x + near.halo:
            pieces.append((offset + low - y, high - low, near.row(x, low)))

    def store(c, value):
        for offset, count, row in pieces:
            two_ref[c, pl.ds(row, count), :] = value[offset : offset + count]

    store_shifted(values, lane, store)


def third_step(near, two_ref, three_ref, kind, first):
    for c, value in enumerate(advance(near, two_ref, first, kind)):
        three_ref[c, pl.ds(first, 8), :] = value


def finish(ext, source, x, density_ref, momentum_ref, concentration_ref):
    values = [arriving(ext, source, c, ext.row(x, 0), ext.cells_y) for c in range(COUNT)]
    lane = lax.broadcasted_iota(jnp.int32, values[0].shape, 1)

    def summed(weights):
        total = None
        for along_z in (0, 1, -1):
            part = None
            for c, weight in weights.items():
                if weight == 0 or all_velocity[c][2] != along_z:
                    continue
                if part is None:
                    part = values[c] if weight > 0 else -values[c]
                else:
                    part = part + values[c] if weight > 0 else part - values[c]
            if part is not None:
                part = depth_shift(part, along_z, lane)
                total = part if total is None else total + part
        return total

    density_ref[x] = summed({c: 1 for c in range(FLOW)})
    for axis in range(3):
        momentum_ref[axis, x] = summed({c: flow_velocity[c][axis] for c in range(FLOW)})
    concentration_ref[x] = summed({c: 1 for c in range(FLOW, COUNT)})


def interior_kernel(ext, near, odd_ref, post_ref, kinds_ref, two_ref, three_ref, ya_ref, sums_ref):
    for odd_y in (0, 1):

        @pl.when(odd_ref[0] == odd_y)
        def _():
            pack_face_y(ext, 1 - 2 * odd_y, post_ref, kinds_ref, sums_ref, ya_ref)

    for x in range(1, ext.cells_x - 1):
        second_step(ext, near, post_ref, two_ref, kinds_ref, ext.row(x, 0))
    for x in range(2, ext.cells_x - 2):
        kind = kinds_ref[pl.ds(ext.row(x, 0), ext.cells_y), :]
        third_step(near, two_ref, three_ref, kind, near.row(x, 0))


def middle_kernel(ext, near, odd_ref, _, __, ___, ____, up_ref, down_ref, cup_ref, cdown_ref,
                  yb_ref, ya_ref, one_ref, kinds_ref, two_ref, three_ref,
                  density_ref, momentum_ref, concentration_ref, near_kinds_ref):
    put = putter(one_ref, kinds_ref)
    cells_x, cells_y, depth = ext.cells_x, ext.cells_y, one_ref.shape[-1]
    zero = jnp.zeros((8, depth), jnp.float32)
    zeros = jnp.zeros((cells_x, depth), jnp.float32)
    for sign in (1, -1):
        for c in moving(0, 0):
            first = ext.row(beyond(cells_x, sign, HALO - 1), -HALO)
            for start in [*range(0, ext.pitch - 8, 8), ext.pitch - 8]:
                put(c, pl.ds(first + start, 8), zero)
        for c in moving(1, 0):
            put(c, line_y(ext, beyond(cells_y, sign, HALO - 1))(0), zeros)
    put_inner(ext, put, up_ref, -1)
    put_inner(ext, put, down_ref, 1)
    for odd_y in (0, 1):

        @pl.when(odd_ref[0] == odd_y)
        def _():
            pair = 1 - 2 * odd_y
            partner = ya_ref.at[1 - odd_y]
            put_face_y(ext, put, yb_ref, -pair)
            put_face_y(ext, put, partner, pair)
            for side, (ref, sign_x) in enumerate(((cup_ref, -1), (cdown_ref, 1))):
                put_corner(ext, put, ref.at[0], sign_x, pair, 0)
                put_corner(ext, put, ref.at[1], sign_x, -pair, 0)
                first = partner.shape[0] - (2 - side) * CORNER_ROWS
                corners = partner.at[pl.ds(first, CORNER_ROWS)]
                put_corner(ext, put, corners, sign_x, -pair, pair * ext.cells_y)

    last_x, last_y = ext.cells_x - 1, ext.cells_y - 1
    for space, depth in ((ext, 1), (near, 2)):
        halo = 3 - depth
        runs = [
            (space.row(-halo, -halo), space.row(depth, depth - 1)),
            (space.row(last_x - depth, last_y - depth + 1), space.row(last_x + halo, last_y + halo)),
        ] + [
            (space.row(x, last_y - depth + 1), space.row(x + 1, depth - 1))
            for x in range(depth, last_x - depth)
        ]
        if space is near:
            for x in range(-halo, ext.cells_x + halo):
                for y in (-halo, last_y + halo - 7):
                    near_kinds_ref[pl.ds(near.row(x, y), 8), :] = kinds_ref[pl.ds(ext.row(x, y), 8), :]
        for start, end in runs:
            for first in range(start, end + 1, 8):
                if space is ext:
                    second_step(ext, near, one_ref, two_ref, kinds_ref, first)
                else:
                    kind = near_kinds_ref[pl.ds(first, 8), :]
                    third_step(near, two_ref, three_ref, kind, first)
    for x in range(HALO, ext.cells_x - HALO):
        finish(near, three_ref, x, density_ref, momentum_ref, concentration_ref)


def last_kernel(ext, near, odd_ref, _, __, ___, ____, far_ref, early_density_ref, early_momentum_ref,
                early_concentration_ref, density_hbm, momentum_hbm, concentration_hbm,
                one_ref, kinds_ref, two_ref, three_ref,
                density_ref, momentum_ref, concentration_ref, sems):
    cells_x, cells_y = ext.cells_x, ext.cells_y
    put = putter(one_ref, kinds_ref)
    copies = []

    def send(planes, density, momentum, concentration):
        for source, target in (
            (density.at[planes], density_hbm.at[planes]),
            (momentum.at[:, planes], momentum_hbm.at[:, planes]),
            (concentration.at[planes], concentration_hbm.at[planes]),
        ):
            copies.append(pltpu.make_async_copy(source, target, sems.at[len(copies)]))
            copies[-1].start()

    send(
        pl.ds(HALO, cells_x - 2 * HALO),
        early_density_ref, early_momentum_ref, early_concentration_ref,
    )
    for odd_y in (0, 1):

        @pl.when(odd_ref[0] == odd_y)
        def _():
            far = 2 * odd_y - 1
            for side, sign_x in enumerate((-1, 1)):
                put_corner(ext, put, far_ref.at[side], sign_x, -far, far * cells_y)
            for width in (2, 1):
                y = cells_y + width - 8 if far > 0 else -width
                for k in range(HALO):
                    for x in (k - width, cells_x - 1 + width - k):
                        if width == 2:
                            second_step(ext, near, one_ref, two_ref, kinds_ref, ext.row(x, y))
                        else:
                            kind = kinds_ref[pl.ds(ext.row(x, y), 8), :]
                            third_step(near, two_ref, three_ref, kind, near.row(x, y))

    for first in (0, cells_x - HALO):
        for x in range(first, first + HALO):
            finish(near, three_ref, x, density_ref, momentum_ref, concentration_ref)
        send(pl.ds(first, HALO), density_ref, momentum_ref, concentration_ref)
    for copy in copies:
        copy.wait()


def higher(i, count):
    return (i + 1) % count


def lower(i, count):
    return (i - 1) % count


def across(i, count):
    return (i + 1) % count if i % 2 else (i - 1) % count


def swapped(block, count_x, count_y, move_x, move_y):
    pairs = []
    for i in range(count_x):
        for j in range(count_y):
            to_x = move_x(i, count_x) if move_x else i
            to_y = move_y(j, count_y) if move_y else j
            pairs.append((i * count_y + j, to_x * count_y + to_y))
    return lax.ppermute(block, ("gx", "gy"), pairs)


def solution(mesh):
    count_x, count_y = mesh.shape["gx"], mesh.shape["gy"]
    assert count_y % 2 == 0

    def local(flow, solute, kind):
        _, cells_x, cells_y, depth = flow.shape
        f32 = jnp.float32
        shape = lambda *dims: jax.ShapeDtypeStruct(dims, f32)
        smem = pl.BlockSpec(memory_space=pltpu.SMEM)
        vmem = pl.BlockSpec(memory_space=pltpu.VMEM)
        hbm = pl.BlockSpec(memory_space=pltpu.HBM)
        params = pltpu.CompilerParams(vmem_limit_bytes=16 * 1024 * 1024)
        odd = jnp.reshape(lax.axis_index("gy") % 2, (1,)).astype(jnp.int32)
        ext = Extended(cells_x, cells_y)
        split = cells_x * 5 // 8
        groups = [(0, split), (split, cells_x - split)]
        flow, solute, kind = (
            pltpu.with_memory_space_constraint(a, pltpu.HBM) for a in (flow, solute, kind)
        )
        post, kinds, up, down, yb, cup, cdown = pl.pallas_call(
            functools.partial(first_kernel, ext, groups),
            out_shape=[
                shape(COUNT, ext.rows, depth),
                shape(ext.rows, depth),
                shape(len(face_x) * ext.inner_rows, depth),
                shape(len(face_x) * ext.inner_rows, depth),
                shape(ext.face_y_rows, depth),
                shape(2, CORNER_ROWS, depth),
                shape(2, CORNER_ROWS, depth),
            ],
            in_specs=[smem, hbm, hbm, hbm],
            out_specs=[vmem] * 7,
            scratch_shapes=[
                pltpu.VMEM(flow.shape, f32),
                pltpu.VMEM(solute.shape, f32),
                pltpu.VMEM(kind.shape, kind.dtype),
                pltpu.VMEM((8, ext.rows, depth), f32),
                pltpu.SemaphoreType.DMA((len(groups), 3)),
            ],
            compiler_params=params,
        )(odd, flow, solute, kind)
        move = functools.partial(swapped, count_x=count_x, count_y=count_y)
        cup = move(cup, move_x=higher, move_y=None)
        cdown = move(cdown, move_x=lower, move_y=None)
        yb = move(yb, move_x=None, move_y=across)
        up = move(up, move_x=higher, move_y=None)
        down = move(down, move_x=lower, move_y=None)
        near = Extended(cells_x, cells_y, HALO - 1)
        one = shape(COUNT, ext.rows, depth)
        two_shape = shape(COUNT, near.rows, depth)
        two, three, ya = pl.pallas_call(
            functools.partial(interior_kernel, ext, near),
            out_shape=[two_shape, two_shape, shape(ext.face_y_rows + 2 * CORNER_ROWS, depth)],
            in_specs=[smem] + [vmem] * 2,
            out_specs=[vmem] * 3,
            scratch_shapes=[pltpu.VMEM((8, ext.rows, depth), f32)],
            compiler_params=params,
        )(odd, post, kinds)
        ya, far = pl.pallas_call(
            forward_kernel,
            out_shape=[shape(*ya.shape), shape(2, CORNER_ROWS, depth)],
            in_specs=[vmem] * 3,
            out_specs=[vmem] * 2,
            input_output_aliases={2: 0},
            compiler_params=params,
        )(cup, cdown, ya)
        far = move(far, move_x=None, move_y=across)
        ya = lax.all_gather(ya, "gy", axis_index_groups=[[j, j + 1] for j in range(0, count_y, 2)])
        moments = [
            shape(cells_x, cells_y, depth),
            shape(3, cells_x, cells_y, depth),
            shape(cells_x, cells_y, depth),
        ]
        post, kinds, two, three, *early = pl.pallas_call(
            functools.partial(middle_kernel, ext, near),
            out_shape=[one, shape(ext.rows, depth), two_shape, two_shape] + moments,
            in_specs=[smem] + [vmem] * 10,
            out_specs=[vmem] * 7,
            scratch_shapes=[pltpu.VMEM((near.rows, depth), f32)],
            input_output_aliases={1: 0, 2: 1, 3: 2, 4: 3},
            compiler_params=params,
        )(odd, post, kinds, two, three, up, down, cup, cdown, yb, ya)
        density, momentum, concentration, *_ = pl.pallas_call(
            functools.partial(last_kernel, ext, near),
            out_shape=moments + [one, shape(ext.rows, depth), two_shape, two_shape],
            in_specs=[smem] + [vmem] * 8,
            out_specs=[hbm] * 3 + [vmem] * 4,
            scratch_shapes=[pltpu.VMEM(m.shape, f32) for m in moments]
            + [pltpu.SemaphoreType.DMA((9,))],
            input_output_aliases={1: 3, 2: 4, 3: 5, 4: 6},
            compiler_params=params,
        )(odd, post, kinds, two, three, far, *early)
        return density, momentum, concentration

    placed = (P(None, "gx", "gy", None), P(None, "gx", "gy", None), P("gx", "gy", None))
    return jax.shard_map(
        local,
        mesh=mesh,
        in_specs=placed,
        out_specs=(P("gx", "gy", None), P(None, "gx", "gy", None), P("gx", "gy", None)),
        check_vma=False,
    )
```

```python
import functools
import math

import jax
import jax.numpy as jnp
from jax import lax
from jax.experimental import pallas as pl
from jax.experimental.pallas import tpu as pltpu
from jax.sharding import PartitionSpec as P

STEPS = 3
HALO = STEPS

flow_velocity = [
    (0, 0, 0),
    (1, 0, 0),
    (-1, 0, 0),
    (0, 1, 0),
    (0, -1, 0),
    (0, 0, 1),
    (0, 0, -1),
    (1, 1, 0),
    (-1, -1, 0),
    (1, -1, 0),
    (-1, 1, 0),
    (1, 0, 1),
    (-1, 0, -1),
    (1, 0, -1),
    (-1, 0, 1),
    (0, 1, 1),
    (0, -1, -1),
    (0, 1, -1),
    (0, -1, 1),
]
FLOW = len(flow_velocity)
all_velocity = flow_velocity + flow_velocity[:7]
COUNT = len(all_velocity)
KIND = COUNT
SUMS = {0: range(COUNT + 1, COUNT + 5), 1: range(COUNT + 5, COUNT + 9)}
flow_plus = 1.25
flow_minus = 1.0 / 1.125
solute_plus = 1.0 / 1.75
solute_minus = 1.0 / 0.7
inlet_density = 1.05
outlet_density = 0.95
inlet_solute = 1.0


def mirrored(channel, sign_x, sign_y):
    if channel >= KIND:
        return channel
    cx, cy, cz = all_velocity[channel]
    wanted = (cx * sign_x, cy * sign_y, cz)
    if channel < FLOW:
        return flow_velocity.index(wanted)
    return FLOW + flow_velocity[:7].index(wanted)


def moving(axis, toward):
    return [c for c in range(COUNT) if all_velocity[c][axis] == toward]


def needed(axis):
    outer = HALO - 1
    return (
        [(c, d) for d in range(1, outer) for c in range(COUNT)]
        + [(c, d) for d in (outer, HALO) for c in moving(axis, 1)]
        + [(c, outer) for c in SUMS[axis]]
        + [(KIND, d) for d in range(1, HALO)]
    )


face_x = needed(0)
face_y = needed(1)
ends_x = [c for c in moving(0, 0) if all_velocity[c][1] == 1]
ends_y = [c for c in moving(1, 0) if all_velocity[c][0] == 1]


def reach(channel):
    return HALO - 1 + (all_velocity[channel][1] if channel < COUNT else 0)


corner_start = [sum(reach(c) for c, _ in face_x[:k]) for k in range(len(face_x) + 1)]
ENDS_START = corner_start[-1]
CORNER_ROWS = ENDS_START + len(ends_x)
FACE_X_SUMS = face_x.index((SUMS[0][0], HALO - 1))
FACE_Y_SUMS = face_y.index((SUMS[1][0], HALO - 1))


def collide(flow, solute, kind):
    pore = kind == 0.0
    solid = kind == 1.0
    inlet = kind == 2.0
    zero = jnp.zeros_like(kind)
    pairs = range(1, FLOW, 2)
    total = {i: flow[i] + flow[i + 1] for i in pairs}
    gap = {i: flow[i] - flow[i + 1] for i in pairs}
    density = (flow[0] + total[1] + total[3]) + (total[5] + total[7] + total[9])
    density = density + ((total[11] + total[13]) + (total[15] + total[17]))
    mom_x = (gap[1] + gap[7]) + (gap[9] + gap[11]) + gap[13]
    mom_y = (gap[3] + gap[7]) + (gap[15] - gap[9]) + gap[17]
    mom_z = (gap[5] + gap[11]) + (gap[15] - gap[13]) - gap[17]
    square = mom_x * mom_x + mom_y * mom_y + mom_z * mom_z
    wall = jnp.where(solid, 0.5, zero)
    even = jnp.where(pore, (1.0 - flow_plus) / 2.0, wall)
    odd = jnp.where(pore, (1.0 - flow_minus) / 2.0, -wall)
    border = jnp.where(inlet, inlet_density, jnp.where(solid, 0.0, outlet_density))
    base = jnp.where(pore, flow_plus * density - (1.5 * flow_plus) * square, border)
    base_18 = base * (1.0 / 18.0)
    base_36 = base * (1.0 / 36.0)
    scale = math.sqrt(4.5 * flow_plus / 36.0)
    held = jnp.where(pore, scale, zero)
    vel = (mom_x * held, mom_y * held, mom_z * held)
    along = 3.0 * flow_minus / (36.0 * scale)
    out = [None] * COUNT
    out[0] = (even + even) * flow[0] + base * (1.0 / 3.0)
    for i in pairs:
        cx, cy, cz = flow_velocity[i]
        parts = [(c, v) for c, v in zip((cx, cy, cz), vel) if c != 0]
        if len(parts) == 1:
            t = parts[0][1]
            a = even * total[i] + (base_18 + 2.0 * (t * t))
            b = odd * gap[i] + (2.0 * along) * t
        else:
            t = parts[0][1] + parts[1][1] if parts[1][0] > 0 else parts[0][1] - parts[1][1]
            a = even * total[i] + (base_36 + t * t)
            b = odd * gap[i] + along * t
        out[i] = a + b
        out[i + 1] = a - b
    total = {i: solute[i] + solute[i + 1] for i in (1, 3, 5)}
    gap = {i: solute[i] - solute[i + 1] for i in (1, 3, 5)}
    concentration = (solute[0] + total[1]) + (total[3] + total[5])
    even = jnp.where(pore, (1.0 - solute_plus) / 2.0, wall)
    odd = jnp.where(pore, (1.0 - solute_minus) / 2.0, -wall)
    border = jnp.where(inlet, inlet_solute, zero)
    base = jnp.where(pore, solute_plus * concentration, border) * 0.125
    drift = concentration * (0.5 * solute_minus / scale)
    out[FLOW] = (even + even) * solute[0] + (base + base)
    for i, t in zip((1, 3, 5), vel):
        a = even * total[i] + base
        b = odd * gap[i] + drift * t
        out[FLOW + i] = a + b
        out[FLOW + i + 1] = a - b
    return out


def depth_shift(section, along_z, lane):
    depth = section.shape[-1]
    if along_z == 1:
        return jnp.where(lane == 0, 0.0, pltpu.roll(section, 1, section.ndim - 1))
    if along_z == -1:
        return jnp.where(lane == depth - 1, 0.0, pltpu.roll(section, depth - 1, section.ndim - 1))
    return section


def store_shifted(values, lane, store):
    for c in range(COUNT):
        store(c, depth_shift(values[c], all_velocity[c][2], lane))


class Extended:
    def __init__(self, cells_x, cells_y, halo=HALO):
        self.cells_x, self.cells_y, self.halo = cells_x, cells_y, halo
        self.pitch = cells_y + 2 * halo
        self.rows = -(-((cells_x + 2 * halo) * self.pitch + 16) // 8) * 8
        self.face_y_rows = len(face_y) * cells_x + 2 * len(ends_y)
        self.inner_rows = cells_y - 2 * (HALO - 1)

    def row(self, x, y):
        return (x + self.halo) * self.pitch + y + self.halo

    def runs(self, first, count):
        found = []
        for k in range(count):
            x, y = divmod(first + k, self.pitch)
            if found and y > 0:
                found[-1][1] += 1
            else:
                found.append([k, 1, x - self.halo, y - self.halo])
        return found

    def inner(self, channel):
        return HALO - 1 - (all_velocity[channel][1] if channel < COUNT else 0)


def inside(cells, sign, d):
    return cells - d if sign > 0 else d - 1


def beyond(cells, sign, d):
    return cells - 1 + d if sign > 0 else -d


def line_x(ext, x):
    return lambda y: pl.ds(ext.row(x, y), ext.cells_y)


def line_y(ext, y):
    return lambda x: pl.ds(ext.row(x, y), ext.cells_x, stride=ext.pitch)


def reader(post_ref, kinds_ref, sums_ref):
    def held(c, where):
        if c > KIND:
            return sums_ref[c - SUMS[0][0], where, :]
        return kinds_ref[where, :] if c == KIND else post_ref[c, where, :]

    return held


def put_line_sums(axis, cells, where, post_ref, sums_ref):
    across = 1 - axis
    place = lax.broadcasted_iota(jnp.int32, (cells, post_ref.shape[-1]), 0)
    parts = {}
    for move in (0, 1, -1):
        total = along = solute = None
        for c in moving(axis, 0):
            if all_velocity[c][across] != move:
                continue
            value = post_ref[c, where(-move), :]
            if c >= FLOW:
                solute = value if solute is None else solute + value
                continue
            total = value if total is None else total + value
            cz = all_velocity[c][2]
            if cz != 0:
                signed = value if cz > 0 else -value
                along = signed if along is None else along + signed
        parts[move] = [total, along, solute]
        if move != 0:
            inside = place != (0 if move > 0 else cells - 1)
            parts[move] = [jnp.where(inside, p, 0.0) for p in parts[move]]
    total, along, solute = (parts[0][n] + parts[1][n] + parts[-1][n] for n in range(3))
    for c, value in zip(
        SUMS[axis], (total - along, parts[1][0] - parts[-1][0], along, solute)
    ):
        sums_ref[c - SUMS[0][0], where(0), :] = value


def pack_face_y(ext, sign, post_ref, kinds_ref, sums_ref, ref):
    held = reader(post_ref, kinds_ref, sums_ref)
    put_line_sums(
        1, ext.cells_x, line_y(ext, inside(ext.cells_y, sign, HALO - 1)), post_ref, sums_ref
    )
    for k, (c, d) in enumerate(face_y):
        ref[pl.ds(k * ext.cells_x, ext.cells_x), :] = held(
            mirrored(c, 1, sign), line_y(ext, inside(ext.cells_y, sign, d))(0)
        )
    for side, sign_x in enumerate((1, -1)):
        for k, c in enumerate(ends_y):
            row = ext.row(inside(ext.cells_x, sign_x, 1), inside(ext.cells_y, sign, HALO - 1))
            to = len(face_y) * ext.cells_x + side * len(ends_y) + k
            ref[pl.ds(to, 1), :] = held(mirrored(c, sign_x, 1), pl.ds(row, 1))


def first_kernel(ext, groups, odd_ref, flow_hbm, solute_hbm, kind_hbm, post_ref, kinds_ref,
                 up_ref, down_ref, yb_ref, cup_ref, cdown_ref,
                 flow_ref, solute_ref, kind_ref, sums_ref, sems):
    cells_x, cells_y = ext.cells_x, ext.cells_y
    depth = kind_ref.shape[-1]
    lane = lax.broadcasted_iota(jnp.int32, (cells_y, depth), 1)
    copies = {}
    for g, (first, count) in enumerate(groups):
        planes = pl.ds(first, count)
        copies[first] = [
            pltpu.make_async_copy(flow_hbm.at[:, planes], flow_ref.at[:, planes], sems.at[g, 0]),
            pltpu.make_async_copy(
                solute_hbm.at[:, planes], solute_ref.at[:, planes], sems.at[g, 1]
            ),
        ]
    copies[0].append(pltpu.make_async_copy(kind_hbm, kind_ref, sems.at[0, 2]))
    for copy in [copy for group in copies.values() for copy in group]:
        copy.start()

    for x in range(cells_x):
        for copy in copies.get(x, []):
            copy.wait()
        kind = kind_ref[x].astype(jnp.float32)
        rows = pl.ds(ext.row(x, 0), cells_y)
        kinds_ref[rows, :] = kind
        values = collide(
            [flow_ref[c, x] for c in range(FLOW)],
            [solute_ref[c, x] for c in range(COUNT - FLOW)],
            kind,
        )

        def store(c, value):
            post_ref[c, rows, :] = value

        store_shifted(values, lane, store)

    held = reader(post_ref, kinds_ref, sums_ref)
    for sign in (1, -1):
        put_line_sums(
            0, cells_y, line_x(ext, inside(cells_x, sign, HALO - 1)), post_ref, sums_ref
        )
    for odd_y in (0, 1):

        @pl.when(odd_ref[0] == odd_y)
        def _():
            pair = 1 - 2 * odd_y
            pack_face_y(ext, -pair, post_ref, kinds_ref, sums_ref, yb_ref)
            for ref, sign_x in ((cup_ref, 1), (cdown_ref, -1)):
                for side, sign_y in enumerate((pair, -pair)):
                    for k, (c, d) in enumerate(face_x):
                        y = cells_y - reach(c) if sign_y > 0 else 0
                        where = pl.ds(ext.row(inside(cells_x, sign_x, d), y), reach(c))
                        ref[pl.ds(side * CORNER_ROWS + corner_start[k], reach(c)), :] = held(
                            mirrored(c, sign_x, sign_y), where
                        )
                    for k, c in enumerate(ends_x):
                        row = ext.row(
                            inside(cells_x, sign_x, HALO - 1), inside(cells_y, sign_y, 1)
                        )
                        ref[pl.ds(side * CORNER_ROWS + ENDS_START + k, 1), :] = held(
                            mirrored(c, 1, sign_y), pl.ds(row, 1)
                        )

    for ref, sign in ((up_ref, 1), (down_ref, -1)):
        for k, (c, d) in enumerate(face_x):
            where = pl.ds(ext.row(inside(cells_x, sign, d), ext.inner(c)), ext.inner_rows)
            ref[pl.ds(k * ext.inner_rows, ext.inner_rows), :] = held(mirrored(c, sign, 1), where)


def forward_kernel(cup_ref, cdown_ref, _, ya_ref, far_ref):
    first = ya_ref.shape[0] - 2 * CORNER_ROWS
    for side, ref in enumerate((cup_ref, cdown_ref)):
        rows = pl.ds(side * CORNER_ROWS, CORNER_ROWS)
        ya_ref[pl.ds(first + side * CORNER_ROWS, CORNER_ROWS), :] = ref[pl.ds(0, CORNER_ROWS), :]
        far_ref[rows, :] = ref[pl.ds(CORNER_ROWS, CORNER_ROWS), :]


def putter(one_ref, kinds_ref):
    def put(c, where, value):
        if c == KIND:
            kinds_ref[where, :] = value
        else:
            one_ref[c, where, :] = value

    return put


def put_sums(ext, put, x, y, count, values, carry):
    total, across, along, solute = values
    rows = pl.ds(ext.row(x, y), count)
    moved = across if carry > 0 else -across
    put(0, rows, total - moved)
    put(all_velocity.index((0, carry, 0)), pl.ds(ext.row(x, y - carry), count), moved)
    put(all_velocity.index((0, 0, 1)), rows, along)
    put(FLOW, rows, solute)


def put_corner(ext, put, ref, base, sign_x, sign_y, origin):
    for k, (c, d) in enumerate(face_x):
        x = beyond(ext.cells_x, sign_x, d)
        y = origin + (ext.cells_y - reach(c) if sign_y > 0 else 0)
        if c <= KIND:
            put(
                mirrored(c, -sign_x, sign_y),
                pl.ds(ext.row(x, y), reach(c)),
                ref[pl.ds(base + corner_start[k], reach(c)), :],
            )
        elif k == FACE_X_SUMS:
            for n in range(reach(c)):
                values = [ref[pl.ds(base + corner_start[k + i] + n, 1), :] for i in range(4)]
                carry = 1 if y + n < 0 or y + n == ext.cells_y - 1 else -1
                put_sums(ext, put, x, y + n, 1, values, carry)
    x = beyond(ext.cells_x, sign_x, HALO - 1)
    y = origin + (ext.cells_y - 1 if sign_y > 0 else 0)
    for k, c in enumerate(ends_x):
        put(mirrored(c, 1, sign_y), pl.ds(ext.row(x, y), 1), ref[pl.ds(base + ENDS_START + k, 1), :])


def put_inner(ext, put, ref, sign_x):
    for k, (c, d) in enumerate(face_x):
        x, y = beyond(ext.cells_x, sign_x, d), ext.inner(c)
        rows = [pl.ds((k + i) * ext.inner_rows, ext.inner_rows) for i in range(4)]
        if c <= KIND:
            put(
                mirrored(c, -sign_x, 1),
                pl.ds(ext.row(x, y), ext.inner_rows),
                ref[rows[0], :],
            )
        elif k == FACE_X_SUMS:
            put_sums(ext, put, x, y, ext.inner_rows, [ref[r, :] for r in rows], -1)


def put_face_y(ext, put, ref, sign_y):
    cells = ext.cells_x

    def line(x, y, count=cells):
        return pl.ds(ext.row(x, y), count, stride=ext.pitch)

    for k, (c, d) in enumerate(face_y):
        if c <= KIND:
            put(
                mirrored(c, 1, -sign_y),
                line(0, beyond(ext.cells_y, sign_y, d)),
                ref[pl.ds(k * cells, cells), :],
            )
    y = beyond(ext.cells_y, sign_y, HALO - 1)
    total, across, along, solute = (
        ref[pl.ds((FACE_Y_SUMS + i) * cells, cells), :] for i in range(4)
    )
    last = lax.broadcasted_iota(jnp.int32, across.shape, 0) == cells - 1
    back = all_velocity.index((-1, 0, 0))
    forth = all_velocity.index((1, 0, 0))
    put(0, line(0, y), total - jnp.where(last, across, -across))
    put(back, line(1, y, cells - 1), -across[: cells - 1])
    put(forth, pl.ds(ext.row(cells - 2, y), 1), across[cells - 1 :])
    put(all_velocity.index((0, 0, 1)), line(0, y), along)
    put(FLOW, line(0, y), solute)
    for side, sign_x in enumerate((1, -1)):
        x = cells - 1 if sign_x > 0 else 0
        for k, c in enumerate(ends_y):
            start = len(face_y) * cells + side * len(ends_y) + k
            put(mirrored(c, sign_x, 1), pl.ds(ext.row(x, y), 1), ref[pl.ds(start, 1), :])


def arriving(ext, ref, c, start, count):
    cx, cy, _ = all_velocity[c]
    return ref[c, pl.ds(start - (cx * ext.pitch + cy), count), :]


def advance(ext, source, first, kind):
    values = [arriving(ext, source, c, first, 8) for c in range(COUNT)]
    return collide(values[:FLOW], values[FLOW:], kind)


def second_step(ext, near, one_ref, two_ref, kinds_ref, first):
    values = advance(ext, one_ref, first, kinds_ref[pl.ds(first, 8), :])
    lane = lax.broadcasted_iota(jnp.int32, values[0].shape, 1)
    pieces = []
    for offset, count, x, y in ext.runs(first, 8):
        low, high = max(y, -near.halo), min(y + count, ext.cells_y + near.halo)
        if low < high and -near.halo <= x < ext.cells_x + near.halo:
            pieces.append((offset + low - y, high - low, near.row(x, low)))

    def store(c, value):
        for offset, count, row in pieces:
            two_ref[c, pl.ds(row, count), :] = value[offset : offset + count]

    store_shifted(values, lane, store)


def third_step(near, two_ref, three_ref, kind, first):
    for c, value in enumerate(advance(near, two_ref, first, kind)):
        three_ref[c, pl.ds(first, 8), :] = value


def finish(ext, source, x, density_ref, momentum_ref, concentration_ref):
    values = [arriving(ext, source, c, ext.row(x, 0), ext.cells_y) for c in range(COUNT)]
    lane = lax.broadcasted_iota(jnp.int32, values[0].shape, 1)

    def summed(weights):
        total = None
        for along_z in (0, 1, -1):
            part = None
            for c, weight in weights.items():
                if weight == 0 or all_velocity[c][2] != along_z:
                    continue
                if part is None:
                    part = values[c] if weight > 0 else -values[c]
                else:
                    part = part + values[c] if weight > 0 else part - values[c]
            if part is not None:
                part = depth_shift(part, along_z, lane)
                total = part if total is None else total + part
        return total

    density_ref[x] = summed({c: 1 for c in range(FLOW)})
    for axis in range(3):
        momentum_ref[axis, x] = summed({c: flow_velocity[c][axis] for c in range(FLOW)})
    concentration_ref[x] = summed({c: 1 for c in range(FLOW, COUNT)})


def interior_kernel(ext, near, odd_ref, post_ref, kinds_ref, two_ref, three_ref, ya_ref, sums_ref):
    for odd_y in (0, 1):

        @pl.when(odd_ref[0] == odd_y)
        def _():
            pack_face_y(ext, 1 - 2 * odd_y, post_ref, kinds_ref, sums_ref, ya_ref)

    for x in range(1, ext.cells_x - 1):
        second_step(ext, near, post_ref, two_ref, kinds_ref, ext.row(x, 0))
    for x in range(2, ext.cells_x - 2):
        kind = kinds_ref[pl.ds(ext.row(x, 0), ext.cells_y), :]
        third_step(near, two_ref, three_ref, kind, near.row(x, 0))


def middle_kernel(ext, near, odd_ref, _, __, ___, ____, up_ref, down_ref, cup_ref, cdown_ref,
                  yb_ref, ya_ref, one_ref, kinds_ref, two_ref, three_ref,
                  density_ref, momentum_ref, concentration_ref, near_kinds_ref):
    put = putter(one_ref, kinds_ref)
    cells_x, cells_y, depth = ext.cells_x, ext.cells_y, one_ref.shape[-1]
    zero = jnp.zeros((8, depth), jnp.float32)
    zeros = jnp.zeros((cells_x, depth), jnp.float32)
    for sign in (1, -1):
        for c in moving(0, 0):
            first = ext.row(beyond(cells_x, sign, HALO - 1), -HALO)
            for start in [*range(0, ext.pitch - 8, 8), ext.pitch - 8]:
                put(c, pl.ds(first + start, 8), zero)
        for c in moving(1, 0):
            put(c, line_y(ext, beyond(cells_y, sign, HALO - 1))(0), zeros)
    put_inner(ext, put, up_ref, -1)
    put_inner(ext, put, down_ref, 1)
    for odd_y in (0, 1):

        @pl.when(odd_ref[0] == odd_y)
        def _():
            pair = 1 - 2 * odd_y
            partner = ya_ref.at[1 - odd_y]
            put_face_y(ext, put, yb_ref, -pair)
            put_face_y(ext, put, partner, pair)
            for side, (ref, sign_x) in enumerate(((cup_ref, -1), (cdown_ref, 1))):
                put_corner(ext, put, ref, 0, sign_x, pair, 0)
                put_corner(ext, put, ref, CORNER_ROWS, sign_x, -pair, 0)
                first = partner.shape[0] - (2 - side) * CORNER_ROWS
                put_corner(ext, put, partner, first, sign_x, -pair, pair * ext.cells_y)

    last_x, last_y = ext.cells_x - 1, ext.cells_y - 1
    for space, depth in ((ext, 1), (near, 2)):
        halo = 3 - depth
        runs = [
            (space.row(-halo, -halo), space.row(depth, depth - 1)),
            (space.row(last_x - depth, last_y - depth + 1), space.row(last_x + halo, last_y + halo)),
        ] + [
            (space.row(x, last_y - depth + 1), space.row(x + 1, depth - 1))
            for x in range(depth, last_x - depth)
        ]
        if space is near:
            for x in range(-halo, ext.cells_x + halo):
                for y in (-halo, last_y + halo - 7):
                    near_kinds_ref[pl.ds(near.row(x, y), 8), :] = kinds_ref[pl.ds(ext.row(x, y), 8), :]
        for start, end in runs:
            for first in range(start, end + 1, 8):
                if space is ext:
                    second_step(ext, near, one_ref, two_ref, kinds_ref, first)
                else:
                    kind = near_kinds_ref[pl.ds(first, 8), :]
                    third_step(near, two_ref, three_ref, kind, first)
    for x in range(HALO, ext.cells_x - HALO):
        finish(near, three_ref, x, density_ref, momentum_ref, concentration_ref)


def last_kernel(ext, near, odd_ref, _, __, ___, ____, far_ref, early_density_ref, early_momentum_ref,
                early_concentration_ref, density_hbm, momentum_hbm, concentration_hbm,
                one_ref, kinds_ref, two_ref, three_ref,
                density_ref, momentum_ref, concentration_ref, sems):
    cells_x, cells_y = ext.cells_x, ext.cells_y
    put = putter(one_ref, kinds_ref)
    copies = []

    def send(planes, density, momentum, concentration):
        for source, target in (
            (density.at[planes], density_hbm.at[planes]),
            (momentum.at[:, planes], momentum_hbm.at[:, planes]),
            (concentration.at[planes], concentration_hbm.at[planes]),
        ):
            copies.append(pltpu.make_async_copy(source, target, sems.at[len(copies)]))
            copies[-1].start()

    send(
        pl.ds(HALO, cells_x - 2 * HALO),
        early_density_ref, early_momentum_ref, early_concentration_ref,
    )
    for odd_y in (0, 1):

        @pl.when(odd_ref[0] == odd_y)
        def _():
            far = 2 * odd_y - 1
            for side, sign_x in enumerate((-1, 1)):
                put_corner(
                    ext, put, far_ref, side * CORNER_ROWS, sign_x, -far, far * cells_y
                )
            for width in (2, 1):
                y = cells_y + width - 8 if far > 0 else -width
                for k in range(HALO):
                    for x in (k - width, cells_x - 1 + width - k):
                        if width == 2:
                            second_step(ext, near, one_ref, two_ref, kinds_ref, ext.row(x, y))
                        else:
                            kind = kinds_ref[pl.ds(ext.row(x, y), 8), :]
                            third_step(near, two_ref, three_ref, kind, near.row(x, y))

    for first in (0, cells_x - HALO):
        for x in range(first, first + HALO):
            finish(near, three_ref, x, density_ref, momentum_ref, concentration_ref)
        send(pl.ds(first, HALO), density_ref, momentum_ref, concentration_ref)
    for copy in copies:
        copy.wait()


def higher(i, count):
    return (i + 1) % count


def lower(i, count):
    return (i - 1) % count


def across(i, count):
    return (i + 1) % count if i % 2 else (i - 1) % count


def swapped(block, count_x, count_y, move_x, move_y):
    pairs = []
    for i in range(count_x):
        for j in range(count_y):
            to_x = move_x(i, count_x) if move_x else i
            to_y = move_y(j, count_y) if move_y else j
            pairs.append((i * count_y + j, to_x * count_y + to_y))
    return lax.ppermute(block, ("gx", "gy"), pairs)


def solution(mesh):
    count_x, count_y = mesh.shape["gx"], mesh.shape["gy"]
    assert count_y % 2 == 0

    def local(flow, solute, kind):
        _, cells_x, cells_y, depth = flow.shape
        f32 = jnp.float32
        shape = lambda *dims: jax.ShapeDtypeStruct(dims, f32)
        smem = pl.BlockSpec(memory_space=pltpu.SMEM)
        vmem = pl.BlockSpec(memory_space=pltpu.VMEM)
        hbm = pl.BlockSpec(memory_space=pltpu.HBM)
        params = pltpu.CompilerParams(vmem_limit_bytes=16 * 1024 * 1024)
        odd = jnp.reshape(lax.axis_index("gy") % 2, (1,)).astype(jnp.int32)
        ext = Extended(cells_x, cells_y)
        split = cells_x * 5 // 8
        groups = [(0, split), (split, cells_x - split)]
        flow, solute, kind = (
            pltpu.with_memory_space_constraint(a, pltpu.HBM) for a in (flow, solute, kind)
        )
        post, kinds, up, down, yb, cup, cdown = pl.pallas_call(
            functools.partial(first_kernel, ext, groups),
            out_shape=[
                shape(COUNT, ext.rows, depth),
                shape(ext.rows, depth),
                shape(len(face_x) * ext.inner_rows, depth),
                shape(len(face_x) * ext.inner_rows, depth),
                shape(ext.face_y_rows, depth),
                shape(2 * CORNER_ROWS, depth),
                shape(2 * CORNER_ROWS, depth),
            ],
            in_specs=[smem, hbm, hbm, hbm],
            out_specs=[vmem] * 7,
            scratch_shapes=[
                pltpu.VMEM(flow.shape, f32),
                pltpu.VMEM(solute.shape, f32),
                pltpu.VMEM(kind.shape, kind.dtype),
                pltpu.VMEM((8, ext.rows, depth), f32),
                pltpu.SemaphoreType.DMA((len(groups), 3)),
            ],
            compiler_params=params,
        )(odd, flow, solute, kind)
        move = functools.partial(swapped, count_x=count_x, count_y=count_y)
        cup = move(cup, move_x=higher, move_y=None)
        cdown = move(cdown, move_x=lower, move_y=None)
        yb = move(yb, move_x=None, move_y=across)
        up = move(up, move_x=higher, move_y=None)
        down = move(down, move_x=lower, move_y=None)
        near = Extended(cells_x, cells_y, HALO - 1)
        one = shape(COUNT, ext.rows, depth)
        two_shape = shape(COUNT, near.rows, depth)
        two, three, ya = pl.pallas_call(
            functools.partial(interior_kernel, ext, near),
            out_shape=[two_shape, two_shape, shape(ext.face_y_rows + 2 * CORNER_ROWS, depth)],
            in_specs=[smem] + [vmem] * 2,
            out_specs=[vmem] * 3,
            scratch_shapes=[pltpu.VMEM((8, ext.rows, depth), f32)],
            compiler_params=params,
        )(odd, post, kinds)
        ya, far = pl.pallas_call(
            forward_kernel,
            out_shape=[shape(*ya.shape), shape(2 * CORNER_ROWS, depth)],
            in_specs=[vmem] * 3,
            out_specs=[vmem] * 2,
            input_output_aliases={2: 0},
            compiler_params=params,
        )(cup, cdown, ya)
        far = move(far, move_x=None, move_y=across)
        ya = lax.all_gather(ya, "gy", axis_index_groups=[[j, j + 1] for j in range(0, count_y, 2)])
        moments = [
            shape(cells_x, cells_y, depth),
            shape(3, cells_x, cells_y, depth),
            shape(cells_x, cells_y, depth),
        ]
        post, kinds, two, three, *early = pl.pallas_call(
            functools.partial(middle_kernel, ext, near),
            out_shape=[one, shape(ext.rows, depth), two_shape, two_shape] + moments,
            in_specs=[smem] + [vmem] * 10,
            out_specs=[vmem] * 7,
            scratch_shapes=[pltpu.VMEM((near.rows, depth), f32)],
            input_output_aliases={1: 0, 2: 1, 3: 2, 4: 3},
            compiler_params=params,
        )(odd, post, kinds, two, three, up, down, cup, cdown, yb, ya)
        density, momentum, concentration, *_ = pl.pallas_call(
            functools.partial(last_kernel, ext, near),
            out_shape=moments + [one, shape(ext.rows, depth), two_shape, two_shape],
            in_specs=[smem] + [vmem] * 8,
            out_specs=[hbm] * 3 + [vmem] * 4,
            scratch_shapes=[pltpu.VMEM(m.shape, f32) for m in moments]
            + [pltpu.SemaphoreType.DMA((9,))],
            input_output_aliases={1: 3, 2: 4, 3: 5, 4: 6},
            compiler_params=params,
        )(odd, post, kinds, two, three, far, *early)
        return density, momentum, concentration

    placed = (P(None, "gx", "gy", None), P(None, "gx", "gy", None), P("gx", "gy", None))
    return jax.shard_map(
        local,
        mesh=mesh,
        in_specs=placed,
        out_specs=(P("gx", "gy", None), P(None, "gx", "gy", None), P("gx", "gy", None)),
        check_vma=False,
    )
```

```python
import functools
import math

import jax
import jax.numpy as jnp
from jax import lax
from jax.experimental import pallas as pl
from jax.experimental.pallas import tpu as pltpu
from jax.sharding import PartitionSpec as P

STEPS = 3
HALO = STEPS

flow_velocity = [
    (0, 0, 0),
    (1, 0, 0),
    (-1, 0, 0),
    (0, 1, 0),
    (0, -1, 0),
    (0, 0, 1),
    (0, 0, -1),
    (1, 1, 0),
    (-1, -1, 0),
    (1, -1, 0),
    (-1, 1, 0),
    (1, 0, 1),
    (-1, 0, -1),
    (1, 0, -1),
    (-1, 0, 1),
    (0, 1, 1),
    (0, -1, -1),
    (0, 1, -1),
    (0, -1, 1),
]
FLOW = len(flow_velocity)
all_velocity = flow_velocity + flow_velocity[:7]
COUNT = len(all_velocity)
KIND = COUNT
SUMS = {0: range(COUNT + 1, COUNT + 5), 1: range(COUNT + 5, COUNT + 9)}
flow_plus = 1.25
flow_minus = 1.0 / 1.125
solute_plus = 1.0 / 1.75
solute_minus = 1.0 / 0.7
inlet_density = 1.05
outlet_density = 0.95
inlet_solute = 1.0


def mirrored(channel, sign_x, sign_y):
    if channel >= KIND:
        return channel
    cx, cy, cz = all_velocity[channel]
    wanted = (cx * sign_x, cy * sign_y, cz)
    if channel < FLOW:
        return flow_velocity.index(wanted)
    return FLOW + flow_velocity[:7].index(wanted)


def moving(axis, toward):
    return [c for c in range(COUNT) if all_velocity[c][axis] == toward]


def needed(axis):
    outer = HALO - 1
    return (
        [(c, d) for d in range(1, outer) for c in range(COUNT)]
        + [(c, d) for d in (outer, HALO) for c in moving(axis, 1)]
        + [(c, outer) for c in SUMS[axis]]
        + [(KIND, d) for d in range(1, HALO)]
    )


face_x = needed(0)
face_y = needed(1)
ends_x = [c for c in moving(0, 0) if all_velocity[c][1] == 1]
ends_y = [c for c in moving(1, 0) if all_velocity[c][0] == 1]


def reach(channel):
    return HALO - 1 + (all_velocity[channel][1] if channel < COUNT else 0)


corner_start = [sum(reach(c) for c, _ in face_x[:k]) for k in range(len(face_x) + 1)]
ENDS_START = corner_start[-1]
CORNER_ROWS = ENDS_START + len(ends_x)
FACE_X_SUMS = face_x.index((SUMS[0][0], HALO - 1))
FACE_Y_SUMS = face_y.index((SUMS[1][0], HALO - 1))


def collide(flow, solute, kind):
    pore = kind == 0.0
    solid = kind == 1.0
    inlet = kind == 2.0
    zero = jnp.zeros_like(kind)
    pairs = range(1, FLOW, 2)
    total = {i: flow[i] + flow[i + 1] for i in pairs}
    gap = {i: flow[i] - flow[i + 1] for i in pairs}
    density = (flow[0] + total[1] + total[3]) + (total[5] + total[7] + total[9])
    density = density + ((total[11] + total[13]) + (total[15] + total[17]))
    mom_x = (gap[1] + gap[7]) + (gap[9] + gap[11]) + gap[13]
    mom_y = (gap[3] + gap[7]) + (gap[15] - gap[9]) + gap[17]
    mom_z = (gap[5] + gap[11]) + (gap[15] - gap[13]) - gap[17]
    wall = jnp.where(solid, 0.5, zero)
    even = jnp.where(pore, (1.0 - flow_plus) / 2.0, wall)
    odd = jnp.where(pore, (1.0 - flow_minus) / 2.0, -wall)
    border = jnp.where(inlet, inlet_density, jnp.where(solid, 0.0, outlet_density))
    scale = math.sqrt(4.5 * flow_plus / 36.0)
    held = jnp.where(pore, scale, zero)
    vel = (mom_x * held, mom_y * held, mom_z * held)
    squares = [v * v for v in vel]
    square = squares[0] + squares[1] + squares[2]
    base = jnp.where(pore, flow_plus * density - (1.5 * flow_plus / scale**2) * square, border)
    base_18 = base * (1.0 / 18.0)
    base_36 = base * (1.0 / 36.0)
    along = 3.0 * flow_minus / (36.0 * scale)
    out = [None] * COUNT
    out[0] = (even + even) * flow[0] + base * (1.0 / 3.0)
    for i in pairs:
        cx, cy, cz = flow_velocity[i]
        parts = [(c, v) for c, v in zip((cx, cy, cz), vel) if c != 0]
        if len(parts) == 1:
            t = parts[0][1]
            a = even * total[i] + (base_18 + 2.0 * squares[i // 2])
            b = odd * gap[i] + (2.0 * along) * t
        else:
            t = parts[0][1] + parts[1][1] if parts[1][0] > 0 else parts[0][1] - parts[1][1]
            a = even * total[i] + (base_36 + t * t)
            b = odd * gap[i] + along * t
        out[i] = a + b
        out[i + 1] = a - b
    total = {i: solute[i] + solute[i + 1] for i in (1, 3, 5)}
    gap = {i: solute[i] - solute[i + 1] for i in (1, 3, 5)}
    concentration = (solute[0] + total[1]) + (total[3] + total[5])
    even = jnp.where(pore, (1.0 - solute_plus) / 2.0, wall)
    odd = jnp.where(pore, (1.0 - solute_minus) / 2.0, -wall)
    border = jnp.where(inlet, inlet_solute, zero)
    base = jnp.where(pore, solute_plus * concentration, border) * 0.125
    drift = concentration * (0.5 * solute_minus / scale)
    out[FLOW] = (even + even) * solute[0] + (base + base)
    for i, t in zip((1, 3, 5), vel):
        a = even * total[i] + base
        b = odd * gap[i] + drift * t
        out[FLOW + i] = a + b
        out[FLOW + i + 1] = a - b
    return out


def depth_shift(section, along_z, lane):
    depth = section.shape[-1]
    if along_z == 1:
        return jnp.where(lane == 0, 0.0, pltpu.roll(section, 1, section.ndim - 1))
    if along_z == -1:
        return jnp.where(lane == depth - 1, 0.0, pltpu.roll(section, depth - 1, section.ndim - 1))
    return section


def store_shifted(values, lane, store):
    for c in range(COUNT):
        store(c, depth_shift(values[c], all_velocity[c][2], lane))


class Extended:
    def __init__(self, cells_x, cells_y, halo=HALO):
        self.cells_x, self.cells_y, self.halo = cells_x, cells_y, halo
        self.pitch = cells_y + 2 * halo
        self.rows = -(-((cells_x + 2 * halo) * self.pitch + 16) // 8) * 8
        self.face_y_rows = len(face_y) * cells_x + 2 * len(ends_y)
        self.inner_rows = cells_y - 2 * (HALO - 1)

    def row(self, x, y):
        return (x + self.halo) * self.pitch + y + self.halo

    def runs(self, first, count):
        found = []
        for k in range(count):
            x, y = divmod(first + k, self.pitch)
            if found and y > 0:
                found[-1][1] += 1
            else:
                found.append([k, 1, x - self.halo, y - self.halo])
        return found

    def inner(self, channel):
        return HALO - 1 - (all_velocity[channel][1] if channel < COUNT else 0)


def inside(cells, sign, d):
    return cells - d if sign > 0 else d - 1


def beyond(cells, sign, d):
    return cells - 1 + d if sign > 0 else -d


def line_x(ext, x):
    return lambda y: pl.ds(ext.row(x, y), ext.cells_y)


def line_y(ext, y):
    return lambda x: pl.ds(ext.row(x, y), ext.cells_x, stride=ext.pitch)


def reader(post_ref, kinds_ref, sums_ref):
    def held(c, where):
        if c > KIND:
            return sums_ref[c - SUMS[0][0], where, :]
        return kinds_ref[where, :] if c == KIND else post_ref[c, where, :]

    return held


def put_line_sums(axis, cells, where, post_ref, sums_ref):
    across = 1 - axis
    place = lax.broadcasted_iota(jnp.int32, (cells, post_ref.shape[-1]), 0)
    parts = {}
    for move in (0, 1, -1):
        total = along = solute = None
        for c in moving(axis, 0):
            if all_velocity[c][across] != move:
                continue
            value = post_ref[c, where(-move), :]
            if c >= FLOW:
                solute = value if solute is None else solute + value
                continue
            total = value if total is None else total + value
            cz = all_velocity[c][2]
            if cz != 0:
                signed = value if cz > 0 else -value
                along = signed if along is None else along + signed
        parts[move] = [total, along, solute]
        if move != 0:
            inside = place != (0 if move > 0 else cells - 1)
            parts[move] = [jnp.where(inside, p, 0.0) for p in parts[move]]
    total, along, solute = (parts[0][n] + parts[1][n] + parts[-1][n] for n in range(3))
    for c, value in zip(
        SUMS[axis], (total - along, parts[1][0] - parts[-1][0], along, solute)
    ):
        sums_ref[c - SUMS[0][0], where(0), :] = value


def pack_face_y(ext, sign, post_ref, kinds_ref, sums_ref, ref):
    held = reader(post_ref, kinds_ref, sums_ref)
    put_line_sums(
        1, ext.cells_x, line_y(ext, inside(ext.cells_y, sign, HALO - 1)), post_ref, sums_ref
    )
    for k, (c, d) in enumerate(face_y):
        ref[pl.ds(k * ext.cells_x, ext.cells_x), :] = held(
            mirrored(c, 1, sign), line_y(ext, inside(ext.cells_y, sign, d))(0)
        )
    for side, sign_x in enumerate((1, -1)):
        for k, c in enumerate(ends_y):
            row = ext.row(inside(ext.cells_x, sign_x, 1), inside(ext.cells_y, sign, HALO - 1))
            to = len(face_y) * ext.cells_x + side * len(ends_y) + k
            ref[pl.ds(to, 1), :] = held(mirrored(c, sign_x, 1), pl.ds(row, 1))


def first_kernel(ext, groups, odd_ref, flow_hbm, solute_hbm, kind_hbm, post_ref, kinds_ref,
                 up_ref, down_ref, yb_ref, cup_ref, cdown_ref,
                 flow_ref, solute_ref, kind_ref, sums_ref, sems):
    cells_x, cells_y = ext.cells_x, ext.cells_y
    depth = kind_ref.shape[-1]
    lane = lax.broadcasted_iota(jnp.int32, (cells_y, depth), 1)
    copies = {}
    for g, (first, count) in enumerate(groups):
        planes = pl.ds(first, count)
        copies[first] = [
            pltpu.make_async_copy(flow_hbm.at[:, planes], flow_ref.at[:, planes], sems.at[g, 0]),
            pltpu.make_async_copy(
                solute_hbm.at[:, planes], solute_ref.at[:, planes], sems.at[g, 1]
            ),
        ]
    copies[0].append(pltpu.make_async_copy(kind_hbm, kind_ref, sems.at[0, 2]))
    for copy in [copy for group in copies.values() for copy in group]:
        copy.start()

    for x in range(cells_x):
        for copy in copies.get(x, []):
            copy.wait()
        kind = kind_ref[x].astype(jnp.float32)
        rows = pl.ds(ext.row(x, 0), cells_y)
        kinds_ref[rows, :] = kind
        values = collide(
            [flow_ref[c, x] for c in range(FLOW)],
            [solute_ref[c, x] for c in range(COUNT - FLOW)],
            kind,
        )

        def store(c, value):
            post_ref[c, rows, :] = value

        store_shifted(values, lane, store)

    held = reader(post_ref, kinds_ref, sums_ref)
    for sign in (1, -1):
        put_line_sums(
            0, cells_y, line_x(ext, inside(cells_x, sign, HALO - 1)), post_ref, sums_ref
        )
    for odd_y in (0, 1):

        @pl.when(odd_ref[0] == odd_y)
        def _():
            pair = 1 - 2 * odd_y
            pack_face_y(ext, -pair, post_ref, kinds_ref, sums_ref, yb_ref)
            for ref, sign_x in ((cup_ref, 1), (cdown_ref, -1)):
                for side, sign_y in enumerate((pair, -pair)):
                    for k, (c, d) in enumerate(face_x):
                        y = cells_y - reach(c) if sign_y > 0 else 0
                        where = pl.ds(ext.row(inside(cells_x, sign_x, d), y), reach(c))
                        ref[pl.ds(side * CORNER_ROWS + corner_start[k], reach(c)), :] = held(
                            mirrored(c, sign_x, sign_y), where
                        )
                    for k, c in enumerate(ends_x):
                        row = ext.row(
                            inside(cells_x, sign_x, HALO - 1), inside(cells_y, sign_y, 1)
                        )
                        ref[pl.ds(side * CORNER_ROWS + ENDS_START + k, 1), :] = held(
                            mirrored(c, 1, sign_y), pl.ds(row, 1)
                        )

    for ref, sign in ((up_ref, 1), (down_ref, -1)):
        for k, (c, d) in enumerate(face_x):
            where = pl.ds(ext.row(inside(cells_x, sign, d), ext.inner(c)), ext.inner_rows)
            ref[pl.ds(k * ext.inner_rows, ext.inner_rows), :] = held(mirrored(c, sign, 1), where)


def forward_kernel(cup_ref, cdown_ref, _, ya_ref, far_ref):
    first = ya_ref.shape[0] - 2 * CORNER_ROWS
    for side, ref in enumerate((cup_ref, cdown_ref)):
        rows = pl.ds(side * CORNER_ROWS, CORNER_ROWS)
        ya_ref[pl.ds(first + side * CORNER_ROWS, CORNER_ROWS), :] = ref[pl.ds(0, CORNER_ROWS), :]
        far_ref[rows, :] = ref[pl.ds(CORNER_ROWS, CORNER_ROWS), :]


def putter(one_ref, kinds_ref):
    def put(c, where, value):
        if c == KIND:
            kinds_ref[where, :] = value
        else:
            one_ref[c, where, :] = value

    return put


def put_sums(ext, put, x, y, count, values, carry):
    total, across, along, solute = values
    rows = pl.ds(ext.row(x, y), count)
    moved = across if carry > 0 else -across
    put(0, rows, total - moved)
    put(all_velocity.index((0, carry, 0)), pl.ds(ext.row(x, y - carry), count), moved)
    put(all_velocity.index((0, 0, 1)), rows, along)
    put(FLOW, rows, solute)


def put_corner(ext, put, ref, base, sign_x, sign_y, origin):
    for k, (c, d) in enumerate(face_x):
        x = beyond(ext.cells_x, sign_x, d)
        y = origin + (ext.cells_y - reach(c) if sign_y > 0 else 0)
        if c <= KIND:
            put(
                mirrored(c, -sign_x, sign_y),
                pl.ds(ext.row(x, y), reach(c)),
                ref[pl.ds(base + corner_start[k], reach(c)), :],
            )
        elif k == FACE_X_SUMS:
            for n in range(reach(c)):
                values = [ref[pl.ds(base + corner_start[k + i] + n, 1), :] for i in range(4)]
                carry = 1 if y + n < 0 or y + n == ext.cells_y - 1 else -1
                put_sums(ext, put, x, y + n, 1, values, carry)
    x = beyond(ext.cells_x, sign_x, HALO - 1)
    y = origin + (ext.cells_y - 1 if sign_y > 0 else 0)
    for k, c in enumerate(ends_x):
        put(mirrored(c, 1, sign_y), pl.ds(ext.row(x, y), 1), ref[pl.ds(base + ENDS_START + k, 1), :])


def put_inner(ext, put, ref, sign_x):
    for k, (c, d) in enumerate(face_x):
        x, y = beyond(ext.cells_x, sign_x, d), ext.inner(c)
        rows = [pl.ds((k + i) * ext.inner_rows, ext.inner_rows) for i in range(4)]
        if c <= KIND:
            put(
                mirrored(c, -sign_x, 1),
                pl.ds(ext.row(x, y), ext.inner_rows),
                ref[rows[0], :],
            )
        elif k == FACE_X_SUMS:
            put_sums(ext, put, x, y, ext.inner_rows, [ref[r, :] for r in rows], -1)


def put_face_y(ext, put, ref, sign_y):
    cells = ext.cells_x

    def line(x, y, count=cells):
        return pl.ds(ext.row(x, y), count, stride=ext.pitch)

    for k, (c, d) in enumerate(face_y):
        if c <= KIND:
            put(
                mirrored(c, 1, -sign_y),
                line(0, beyond(ext.cells_y, sign_y, d)),
                ref[pl.ds(k * cells, cells), :],
            )
    y = beyond(ext.cells_y, sign_y, HALO - 1)
    total, across, along, solute = (
        ref[pl.ds((FACE_Y_SUMS + i) * cells, cells), :] for i in range(4)
    )
    last = lax.broadcasted_iota(jnp.int32, across.shape, 0) == cells - 1
    back = all_velocity.index((-1, 0, 0))
    forth = all_velocity.index((1, 0, 0))
    put(0, line(0, y), total - jnp.where(last, across, -across))
    put(back, line(1, y, cells - 1), -across[: cells - 1])
    put(forth, pl.ds(ext.row(cells - 2, y), 1), across[cells - 1 :])
    put(all_velocity.index((0, 0, 1)), line(0, y), along)
    put(FLOW, line(0, y), solute)
    for side, sign_x in enumerate((1, -1)):
        x = cells - 1 if sign_x > 0 else 0
        for k, c in enumerate(ends_y):
            start = len(face_y) * cells + side * len(ends_y) + k
            put(mirrored(c, sign_x, 1), pl.ds(ext.row(x, y), 1), ref[pl.ds(start, 1), :])


def arriving(ext, ref, c, start, count):
    cx, cy, _ = all_velocity[c]
    return ref[c, pl.ds(start - (cx * ext.pitch + cy), count), :]


def advance(ext, source, first, kind):
    values = [arriving(ext, source, c, first, 8) for c in range(COUNT)]
    return collide(values[:FLOW], values[FLOW:], kind)


def second_step(ext, near, one_ref, two_ref, kinds_ref, first):
    values = advance(ext, one_ref, first, kinds_ref[pl.ds(first, 8), :])
    lane = lax.broadcasted_iota(jnp.int32, values[0].shape, 1)
    pieces = []
    for offset, count, x, y in ext.runs(first, 8):
        low, high = max(y, -near.halo), min(y + count, ext.cells_y + near.halo)
        if low < high and -near.halo <= x < ext.cells_x + near.halo:
            pieces.append((offset + low - y, high - low, near.row(x, low)))

    def store(c, value):
        for offset, count, row in pieces:
            two_ref[c, pl.ds(row, count), :] = value[offset : offset + count]

    store_shifted(values, lane, store)


def third_step(near, two_ref, three_ref, kind, first):
    for c, value in enumerate(advance(near, two_ref, first, kind)):
        three_ref[c, pl.ds(first, 8), :] = value


def finish(ext, source, x, density_ref, momentum_ref, concentration_ref):
    values = [arriving(ext, source, c, ext.row(x, 0), ext.cells_y) for c in range(COUNT)]
    lane = lax.broadcasted_iota(jnp.int32, values[0].shape, 1)

    def summed(weights):
        total = None
        for along_z in (0, 1, -1):
            part = None
            for c, weight in weights.items():
                if weight == 0 or all_velocity[c][2] != along_z:
                    continue
                if part is None:
                    part = values[c] if weight > 0 else -values[c]
                else:
                    part = part + values[c] if weight > 0 else part - values[c]
            if part is not None:
                part = depth_shift(part, along_z, lane)
                total = part if total is None else total + part
        return total

    density_ref[x] = summed({c: 1 for c in range(FLOW)})
    for axis in range(3):
        momentum_ref[axis, x] = summed({c: flow_velocity[c][axis] for c in range(FLOW)})
    concentration_ref[x] = summed({c: 1 for c in range(FLOW, COUNT)})


def interior_kernel(ext, near, odd_ref, post_ref, kinds_ref, two_ref, three_ref, ya_ref, sums_ref):
    for odd_y in (0, 1):

        @pl.when(odd_ref[0] == odd_y)
        def _():
            pack_face_y(ext, 1 - 2 * odd_y, post_ref, kinds_ref, sums_ref, ya_ref)

    for x in range(1, ext.cells_x - 1):
        second_step(ext, near, post_ref, two_ref, kinds_ref, ext.row(x, 0))
    for x in range(2, ext.cells_x - 2):
        kind = kinds_ref[pl.ds(ext.row(x, 0), ext.cells_y), :]
        third_step(near, two_ref, three_ref, kind, near.row(x, 0))


def middle_kernel(ext, near, odd_ref, _, __, ___, ____, up_ref, down_ref, cup_ref, cdown_ref,
                  yb_ref, ya_ref, one_ref, kinds_ref, two_ref, three_ref,
                  density_ref, momentum_ref, concentration_ref, near_kinds_ref):
    put = putter(one_ref, kinds_ref)
    cells_x, cells_y, depth = ext.cells_x, ext.cells_y, one_ref.shape[-1]
    zero = jnp.zeros((8, depth), jnp.float32)
    zeros = jnp.zeros((cells_x, depth), jnp.float32)
    for sign in (1, -1):
        for c in moving(0, 0):
            first = ext.row(beyond(cells_x, sign, HALO - 1), -HALO)
            for start in [*range(0, ext.pitch - 8, 8), ext.pitch - 8]:
                put(c, pl.ds(first + start, 8), zero)
        for c in moving(1, 0):
            put(c, line_y(ext, beyond(cells_y, sign, HALO - 1))(0), zeros)
    put_inner(ext, put, up_ref, -1)
    put_inner(ext, put, down_ref, 1)
    for odd_y in (0, 1):

        @pl.when(odd_ref[0] == odd_y)
        def _():
            pair = 1 - 2 * odd_y
            partner = ya_ref.at[1 - odd_y]
            put_face_y(ext, put, yb_ref, -pair)
            put_face_y(ext, put, partner, pair)
            for side, (ref, sign_x) in enumerate(((cup_ref, -1), (cdown_ref, 1))):
                put_corner(ext, put, ref, 0, sign_x, pair, 0)
                put_corner(ext, put, ref, CORNER_ROWS, sign_x, -pair, 0)
                first = partner.shape[0] - (2 - side) * CORNER_ROWS
                put_corner(ext, put, partner, first, sign_x, -pair, pair * ext.cells_y)

    last_x, last_y = ext.cells_x - 1, ext.cells_y - 1
    for space, depth in ((ext, 1), (near, 2)):
        halo = 3 - depth
        runs = [
            (space.row(-halo, -halo), space.row(depth, depth - 1)),
            (space.row(last_x - depth, last_y - depth + 1), space.row(last_x + halo, last_y + halo)),
        ] + [
            (space.row(x, last_y - depth + 1), space.row(x + 1, depth - 1))
            for x in range(depth, last_x - depth)
        ]
        if space is near:
            for x in range(-halo, ext.cells_x + halo):
                for y in (-halo, last_y + halo - 7):
                    near_kinds_ref[pl.ds(near.row(x, y), 8), :] = kinds_ref[pl.ds(ext.row(x, y), 8), :]
        for start, end in runs:
            for first in range(start, end + 1, 8):
                if space is ext:
                    second_step(ext, near, one_ref, two_ref, kinds_ref, first)
                else:
                    kind = near_kinds_ref[pl.ds(first, 8), :]
                    third_step(near, two_ref, three_ref, kind, first)
    for x in range(HALO, ext.cells_x - HALO):
        finish(near, three_ref, x, density_ref, momentum_ref, concentration_ref)


def last_kernel(ext, near, odd_ref, _, __, ___, ____, far_ref, early_density_ref, early_momentum_ref,
                early_concentration_ref, density_hbm, momentum_hbm, concentration_hbm,
                one_ref, kinds_ref, two_ref, three_ref,
                density_ref, momentum_ref, concentration_ref, sems):
    cells_x, cells_y = ext.cells_x, ext.cells_y
    put = putter(one_ref, kinds_ref)
    copies = []

    def send(planes, density, momentum, concentration):
        for source, target in (
            (density.at[planes], density_hbm.at[planes]),
            (momentum.at[:, planes], momentum_hbm.at[:, planes]),
            (concentration.at[planes], concentration_hbm.at[planes]),
        ):
            copies.append(pltpu.make_async_copy(source, target, sems.at[len(copies)]))
            copies[-1].start()

    send(
        pl.ds(HALO, cells_x - 2 * HALO),
        early_density_ref, early_momentum_ref, early_concentration_ref,
    )
    for odd_y in (0, 1):

        @pl.when(odd_ref[0] == odd_y)
        def _():
            far = 2 * odd_y - 1
            for side, sign_x in enumerate((-1, 1)):
                put_corner(
                    ext, put, far_ref, side * CORNER_ROWS, sign_x, -far, far * cells_y
                )
            for width in (2, 1):
                y = cells_y + width - 8 if far > 0 else -width
                for k in range(HALO):
                    for x in (k - width, cells_x - 1 + width - k):
                        if width == 2:
                            second_step(ext, near, one_ref, two_ref, kinds_ref, ext.row(x, y))
                        else:
                            kind = kinds_ref[pl.ds(ext.row(x, y), 8), :]
                            third_step(near, two_ref, three_ref, kind, near.row(x, y))

    for first in (0, cells_x - HALO):
        for x in range(first, first + HALO):
            finish(near, three_ref, x, density_ref, momentum_ref, concentration_ref)
        send(pl.ds(first, HALO), density_ref, momentum_ref, concentration_ref)
    for copy in copies:
        copy.wait()


def higher(i, count):
    return (i + 1) % count


def lower(i, count):
    return (i - 1) % count


def across(i, count):
    return (i + 1) % count if i % 2 else (i - 1) % count


def swapped(block, count_x, count_y, move_x, move_y):
    pairs = []
    for i in range(count_x):
        for j in range(count_y):
            to_x = move_x(i, count_x) if move_x else i
            to_y = move_y(j, count_y) if move_y else j
            pairs.append((i * count_y + j, to_x * count_y + to_y))
    return lax.ppermute(block, ("gx", "gy"), pairs)


def solution(mesh):
    count_x, count_y = mesh.shape["gx"], mesh.shape["gy"]
    assert count_y % 2 == 0

    def local(flow, solute, kind):
        _, cells_x, cells_y, depth = flow.shape
        f32 = jnp.float32
        shape = lambda *dims: jax.ShapeDtypeStruct(dims, f32)
        smem = pl.BlockSpec(memory_space=pltpu.SMEM)
        vmem = pl.BlockSpec(memory_space=pltpu.VMEM)
        hbm = pl.BlockSpec(memory_space=pltpu.HBM)
        params = pltpu.CompilerParams(vmem_limit_bytes=16 * 1024 * 1024)
        odd = jnp.reshape(lax.axis_index("gy") % 2, (1,)).astype(jnp.int32)
        ext = Extended(cells_x, cells_y)
        split = cells_x * 5 // 8
        groups = [(0, split), (split, cells_x - split)]
        flow, solute, kind = (
            pltpu.with_memory_space_constraint(a, pltpu.HBM) for a in (flow, solute, kind)
        )
        post, kinds, up, down, yb, cup, cdown = pl.pallas_call(
            functools.partial(first_kernel, ext, groups),
            out_shape=[
                shape(COUNT, ext.rows, depth),
                shape(ext.rows, depth),
                shape(len(face_x) * ext.inner_rows, depth),
                shape(len(face_x) * ext.inner_rows, depth),
                shape(ext.face_y_rows, depth),
                shape(2 * CORNER_ROWS, depth),
                shape(2 * CORNER_ROWS, depth),
            ],
            in_specs=[smem, hbm, hbm, hbm],
            out_specs=[vmem] * 7,
            scratch_shapes=[
                pltpu.VMEM(flow.shape, f32),
                pltpu.VMEM(solute.shape, f32),
                pltpu.VMEM(kind.shape, kind.dtype),
                pltpu.VMEM((8, ext.rows, depth), f32),
                pltpu.SemaphoreType.DMA((len(groups), 3)),
            ],
            compiler_params=params,
        )(odd, flow, solute, kind)
        move = functools.partial(swapped, count_x=count_x, count_y=count_y)
        cup = move(cup, move_x=higher, move_y=None)
        cdown = move(cdown, move_x=lower, move_y=None)
        yb = move(yb, move_x=None, move_y=across)
        up = move(up, move_x=higher, move_y=None)
        down = move(down, move_x=lower, move_y=None)
        near = Extended(cells_x, cells_y, HALO - 1)
        one = shape(COUNT, ext.rows, depth)
        two_shape = shape(COUNT, near.rows, depth)
        two, three, ya = pl.pallas_call(
            functools.partial(interior_kernel, ext, near),
            out_shape=[two_shape, two_shape, shape(ext.face_y_rows + 2 * CORNER_ROWS, depth)],
            in_specs=[smem] + [vmem] * 2,
            out_specs=[vmem] * 3,
            scratch_shapes=[pltpu.VMEM((8, ext.rows, depth), f32)],
            compiler_params=params,
        )(odd, post, kinds)
        ya, far = pl.pallas_call(
            forward_kernel,
            out_shape=[shape(*ya.shape), shape(2 * CORNER_ROWS, depth)],
            in_specs=[vmem] * 3,
            out_specs=[vmem] * 2,
            input_output_aliases={2: 0},
            compiler_params=params,
        )(cup, cdown, ya)
        far = move(far, move_x=None, move_y=across)
        ya = lax.all_gather(ya, "gy", axis_index_groups=[[j, j + 1] for j in range(0, count_y, 2)])
        moments = [
            shape(cells_x, cells_y, depth),
            shape(3, cells_x, cells_y, depth),
            shape(cells_x, cells_y, depth),
        ]
        post, kinds, two, three, *early = pl.pallas_call(
            functools.partial(middle_kernel, ext, near),
            out_shape=[one, shape(ext.rows, depth), two_shape, two_shape] + moments,
            in_specs=[smem] + [vmem] * 10,
            out_specs=[vmem] * 7,
            scratch_shapes=[pltpu.VMEM((near.rows, depth), f32)],
            input_output_aliases={1: 0, 2: 1, 3: 2, 4: 3},
            compiler_params=params,
        )(odd, post, kinds, two, three, up, down, cup, cdown, yb, ya)
        density, momentum, concentration, *_ = pl.pallas_call(
            functools.partial(last_kernel, ext, near),
            out_shape=moments + [one, shape(ext.rows, depth), two_shape, two_shape],
            in_specs=[smem] + [vmem] * 8,
            out_specs=[hbm] * 3 + [vmem] * 4,
            scratch_shapes=[pltpu.VMEM(m.shape, f32) for m in moments]
            + [pltpu.SemaphoreType.DMA((9,))],
            input_output_aliases={1: 3, 2: 4, 3: 5, 4: 6},
            compiler_params=params,
        )(odd, post, kinds, two, three, far, *early)
        return density, momentum, concentration

    placed = (P(None, "gx", "gy", None), P(None, "gx", "gy", None), P("gx", "gy", None))
    return jax.shard_map(
        local,
        mesh=mesh,
        in_specs=placed,
        out_specs=(P("gx", "gy", None), P(None, "gx", "gy", None), P("gx", "gy", None)),
        check_vma=False,
    )
```
